32 devices in a mesh: dp: 8 (over z, y), shard: 4 (over x, core).
Axes of the slice: x: 2, y: 2, z: 4, core: 2. Of those that a mesh axis runs over, the one named last changes fastest.
Arguments:
- tokens: bfloat16 [51200, 512], P(('dp', 'shard')), may hold values from -40 to 40
- cotangent: bfloat16 [51200, 512], P(('dp', 'shard')), may hold values from -5 to 5
- regions: int32 [51200], P(('dp', 'shard')), may hold values from 0 to 3
- validity: int32 [51200], P(('dp', 'shard')), may hold values from 0 to 1
- qkv_weight: bfloat16 [786432], P(('dp', 'shard')), may hold values from -0.25 to 0.25
- proj_weight: bfloat16 [262144], P(('dp', 'shard')), may hold values from -1 to 1
- fc1_weight: bfloat16 [1048576], P(('dp', 'shard')), may hold values from -0.25 to 0.25
- fc2_weight: bfloat16 [1048576], P(('dp', 'shard')), may hold values from -0.125 to 0.125
- vectors: bfloat16 [6144], P(('dp', 'shard')), may hold values from -1.5 to 1.65
- rel_table: float32 [361, 16], replicated, may hold values from -4 to 4
Outputs:
- result: bfloat16 [51200, 512], P(('dp', 'shard'))
- tokens_grad: float32 [51200, 512], P(('dp', 'shard'))
- qkv_grad: float32 [786432], P(('dp', 'shard'))
- proj_grad: float32 [262144], P(('dp', 'shard'))
- fc1_grad: float32 [1048576], P(('dp', 'shard'))
- fc2_grad: float32 [1048576], P(('dp', 'shard'))
- vectors_grad: float32 [6144], P(('dp', 'shard'))
- table_grad: float32 [361, 16], replicated
- stats: float32 [5], replicated
The draws below stay inside these ranges and needn't reach their ends.
All inputs are finite; a program needn't handle non-finite values.
Results may differ from the reference program's by a relative error of at most 0.011.
Values may be sent and summed in bfloat16 or wider, within the bound.
No kernel may reach another device: no remote copies, remote signals or barrier semaphores. Data moves between devices by JAX's collectives and lax.ppermute only.
A program may use at most 192 MiB of HBM per device.

```python
import jax
import jax.numpy as jnp
from jax import lax

D = 512
FF = 2048
HEADS = 16
HD = 32
WSIDE = 10
RELN = 361
TOK_DEV = 1600
TOKENS = 51200


def draw_tokens(key, part):
    key = jax.random.fold_in(key, 11)
    row_key, col_key, value_key = jax.random.split(key, 3)
    place = jnp.arange(TOKENS, dtype=jnp.float32) / TOKENS
    row_spread = jnp.exp(jax.random.uniform(row_key, (TOKENS, 1), jnp.float32, -1.15, 1.15))
    col_spread = jnp.exp(jax.random.uniform(col_key, (1, D), jnp.float32, -0.8, 0.8))
    rise = 0.4 + 0.8 * place
    base = jnp.clip(jax.random.normal(value_key, (TOKENS, D), jnp.float32), -4.0, 4.0)
    return (base * rise[:, None] * row_spread * col_spread).astype(jnp.bfloat16)


def window_layout():
    cells = jnp.arange(WSIDE * WSIDE, dtype=jnp.int32)
    return (cells // WSIDE, cells % WSIDE)


def draw_regions(key, part):
    key = jax.random.fold_in(key, 23)
    windows = TOKENS // (WSIDE * WSIDE)
    row_key, col_key = jax.random.split(key)
    first = (jnp.arange(windows, dtype=jnp.int32) == 0)[:, None]
    cut_rows = jnp.where(first, 5, jax.random.randint(row_key, (windows, 1), 1, 16))
    cut_cols = jnp.where(first, 5, jax.random.randint(col_key, (windows, 1), 1, 16))
    rows_at, cols_at = window_layout()
    region = 2 * (rows_at[None, :] >= cut_rows).astype(jnp.int32) + (cols_at[None, :] >= cut_cols).astype(jnp.int32)
    return region.reshape(-1).astype(jnp.int32)


def draw_validity(key, part):
    key = jax.random.fold_in(key, 37)
    windows = TOKENS // (WSIDE * WSIDE)
    row_key, col_key = jax.random.split(key)
    first = (jnp.arange(windows, dtype=jnp.int32) == 0)[:, None]
    valid_rows = jnp.where(first, 4, jnp.minimum(jax.random.randint(row_key, (windows, 1), 4, 17), WSIDE))
    valid_cols = jnp.minimum(jax.random.randint(col_key, (windows, 1), 4, 17), WSIDE)
    rows_at, cols_at = window_layout()
    mask = (rows_at[None, :] < valid_rows) & (cols_at[None, :] < valid_cols)
    return mask.astype(jnp.int32).reshape(-1)


def draw_vectors(key, part):
    key = jax.random.fold_in(key, 51)
    gain_key, shift_key = jax.random.split(key)
    length = 8 * D + FF
    place = jnp.arange(length, dtype=jnp.int32)
    is_gain = (place < D) | (place >= 5 * D) & (place < 6 * D)
    gains = jnp.exp(jax.random.uniform(gain_key, (length,), jnp.float32, -0.5, 0.5))
    shifts = 0.5 * jnp.clip(jax.random.normal(shift_key, (length,), jnp.float32), -3.0, 3.0)
    return jnp.where(is_gain, gains, shifts).astype(jnp.bfloat16)


def levels(rng, shape, cuts, low, top_value):
    def one(dim, blocks):
        heights = jax.random.uniform(jax.random.fold_in(jax.random.fold_in(rng, 6), dim), (blocks,), jnp.float32, low / len(cuts), top_value / len(cuts))
        return jnp.repeat(jnp.exp(heights), shape[dim] // blocks).reshape((-1,) + (1,) * (len(shape) - dim - 1))

    level = one(*cuts[0])
    for cut in cuts[1:]:
        level = level * one(*cut)
    return level


def bell_draw(own_key, dims, scale, most, cuts=(), held_as=jnp.bfloat16):
    array = scale * jax.random.normal(own_key, dims, jnp.float32)
    if cuts:
        array = array * levels(own_key, dims, cuts, -0.22, 0.18)
    return jnp.clip(array, -most, most).astype(held_as)


def setup_inputs(seed: int = 0) -> dict:
    seeds = jax.random.split(jax.random.key(seed), 11)
    tokens = draw_tokens(jax.random.fold_in(seeds[10], 71), 0)
    cotangent = bell_draw(seeds[1], (TOKENS, D), 1.0, 5.0, ((0, 32),))
    regions = draw_regions(jax.random.fold_in(seeds[10], 71), 0)
    validity = draw_validity(jax.random.fold_in(seeds[10], 71), 0)
    qkv_weight = bell_draw(seeds[4], (3 * D * D,), D ** -0.5, 0.25, ((0, 32),))
    proj_weight = bell_draw(seeds[5], (D * D,), (D // 16) ** -0.5, 1.0, ((0, 32),))
    fc1_weight = bell_draw(seeds[6], (D * FF,), D ** -0.5, 0.25, ((0, 32),))
    fc2_weight = bell_draw(seeds[7], (FF * D,), FF ** -0.5, 0.125, ((0, 32),))
    vectors = draw_vectors(jax.random.fold_in(seeds[10], 71), 0)
    rel_table = bell_draw(seeds[9], (RELN, HEADS), 0.8, 4.0, (), jnp.float32)
    return dict(tokens=tokens, cotangent=cotangent, regions=regions, validity=validity, qkv_weight=qkv_weight, proj_weight=proj_weight, fc1_weight=fc1_weight, fc2_weight=fc2_weight, vectors=vectors, rel_table=rel_table)


@jax.custom_vjp
def low(v):
    return lax.optimization_barrier(v.astype(jnp.bfloat16)).astype(jnp.float32)

@jax.custom_vjp
def low_back(v):
    return v

def low_keep(v):
    return (low(v), None)

def low_pass(kept, grad):
    return (grad,)

def back_keep(v):
    return (v, None)

def back_low(kept, grad):
    return (low(grad),)
low.defvjp(low_keep, low_pass)
low_back.defvjp(back_keep, back_low)
HIGHEST_PRECISION = lax.Precision.HIGHEST

def layer_norm(values, gain, shift):
    center = values - lax.optimization_barrier(jnp.mean(values, axis=-1, keepdims=True))
    spread = lax.optimization_barrier(jnp.mean(center * center, axis=-1, keepdims=True))
    return center * lax.rsqrt(spread + 1e-05) * gain + shift

def relative_index(side):
    cells = jnp.arange(side * side, dtype=jnp.int32)
    rows_at = cells // side
    cols_at = cells % side
    offset = (rows_at[:, None] - rows_at[None, :] + side - 1) * (2 * side - 1)
    return (offset + cols_at[:, None] - cols_at[None, :] + side - 1).reshape(-1)

def block_forward(weights, tokens, regions, validity):
    qkv_full, proj_full, up_full, down_full, vectors, table = weights
    cells = WSIDE * WSIDE
    windows = tokens.shape[0] // cells
    gain_one = vectors[0:D]
    shift_one = vectors[D:2 * D]
    query_bias = vectors[2 * D:3 * D]
    value_bias = vectors[3 * D:4 * D]
    proj_bias = vectors[4 * D:5 * D]
    gain_two = vectors[5 * D:6 * D]
    shift_two = vectors[6 * D:7 * D]
    down_bias = vectors[7 * D:8 * D]
    up_bias = vectors[8 * D:8 * D + FF]
    normed = low(layer_norm(tokens, gain_one, shift_one))
    mixed = jnp.dot(normed, qkv_full, precision=HIGHEST_PRECISION)
    queries = low(low_back(mixed[:, 0:D] + query_bias)).reshape(windows, cells, HEADS, HD)
    keys = low(low_back(mixed[:, D:2 * D])).reshape(windows, cells, HEADS, HD)
    values = low(low_back(mixed[:, 2 * D:3 * D] + value_bias)).reshape(windows, cells, HEADS, HD)
    position = table[relative_index(WSIDE)].reshape(cells, cells, HEADS).transpose(2, 0, 1)
    scores = jnp.einsum('wnhd,wmhd->whnm', queries, keys, precision=HIGHEST_PRECISION) * HD ** (-0.5)
    scores = low_back(scores + position[None])
    region_win = regions.reshape(windows, cells)
    valid_win = validity.reshape(windows, cells)
    allowed = (region_win[:, :, None] == region_win[:, None, :]) & (valid_win[:, None, :] == 1)
    allowed = allowed | jnp.eye(cells, dtype=jnp.bool_)[None]
    scores = jnp.where(allowed[:, None], scores, -1000000000.0)
    probs = low(jax.nn.softmax(scores, axis=-1))
    attended = jnp.einsum('whnm,wmhd->wnhd', probs, values, precision=HIGHEST_PRECISION)
    attended = low(low_back(attended.reshape(windows * cells, D)))
    branch = low_back(jnp.dot(attended, proj_full, precision=HIGHEST_PRECISION) + proj_bias)
    middle = tokens + branch
    normed_two = low(layer_norm(middle, gain_two, shift_two))
    pre_act = low_back(jnp.dot(normed_two, up_full, precision=HIGHEST_PRECISION) + up_bias)
    activ = low(jax.nn.gelu(pre_act, approximate=False))
    second = low_back(jnp.dot(activ, down_full, precision=HIGHEST_PRECISION) + down_bias)
    result = middle + second
    weight = validity.astype(jnp.float32)

    def masked_square(field):
        return jnp.sum(weight * lax.optimization_barrier(jnp.sum(field * field, axis=-1)))
    sums = jnp.stack([masked_square(tokens), masked_square(branch), masked_square(middle), masked_square(second), masked_square(result), jnp.sum(weight)])
    return (result, sums)

def reference(tokens, cotangent, regions, validity, qkv_weight, proj_weight, fc1_weight, fc2_weight, vectors, rel_table):
    groups = TOKENS // TOK_DEV
    step_fn = jax.checkpoint(block_forward)

    def forward(tokens_f, qkv_f, proj_f, up_f, down_f, vectors_f, table_f):
        weights = (qkv_f.reshape(D, 3 * D), proj_f.reshape(D, D), up_f.reshape(D, FF), down_f.reshape(FF, D), vectors_f, table_f)

        def visit(totals, group):
            result, sums = step_fn(weights, group[0], group[1], group[2])
            return (totals + sums, result)
        inputs = (tokens_f.reshape(groups, TOK_DEV, D), regions.reshape(groups, TOK_DEV), validity.reshape(groups, TOK_DEV))
        totals, results = lax.scan(visit, jnp.zeros((6,), jnp.float32), inputs)
        return (results.reshape(TOKENS, D), totals)
    primals = (tokens.astype(jnp.float32), qkv_weight.astype(jnp.float32), proj_weight.astype(jnp.float32), fc1_weight.astype(jnp.float32), fc2_weight.astype(jnp.float32), vectors.astype(jnp.float32), rel_table.astype(jnp.float32))
    result, pullback, totals = jax.vjp(forward, *primals, has_aux=True)
    grads = pullback(cotangent.astype(jnp.float32))
    stats = jnp.sqrt(totals[0:5] / (totals[5] * D) + 1e-06)
    return (result.astype(jnp.bfloat16), grads[0], grads[1], grads[2], grads[3], grads[4], grads[5], grads[6], stats)
```

```python
import functools

import jax
import jax.numpy as jnp
from jax import lax
from jax.experimental import pallas as pl
from jax.experimental.pallas import tpu as pltpu
from jax.sharding import PartitionSpec as P

D = 512
FF = 2048
HEADS = 16
HD = 32
WSIDE = 10
RELN = 361
CELLS = WSIDE * WSIDE
GW = 4
GR = GW * CELLS
KP = 112
LANES = 128
GL = GW * LANES
RP = 384
AXES = ("dp", "shard")
LOG2E = 1.4426950408889634
NEG = -1e9
RT2 = 0.7071067811865476
PHI = 0.3989422804014327
f32 = jnp.float32
bf16 = jnp.bfloat16
sds = jax.ShapeDtypeStruct


def nn(a, b):
    return lax.dot_general(a, b, (((1,), (0,)), ((), ())), preferred_element_type=f32)


def nt(a, b):
    return lax.dot_general(a, b, (((1,), (1,)), ((), ())), preferred_element_type=f32)


def whole(shape):
    return pl.BlockSpec(shape, lambda i: (0,) * len(shape))


def params(mib):
    return pltpu.CompilerParams(vmem_limit_bytes=mib * 2**20)


def bit_groups(count):
    bits = count.bit_length() - 1
    groups = [(0,)]
    at = 1
    while at < bits:
        groups.append(tuple(range(at, min(at + 2, bits))))
        at += 2
    return groups


def masks_of(group):
    return [sum(((v >> k) & 1) << b for k, b in enumerate(group)) for v in range(1, 1 << len(group))]


def swap(x, mask, count):
    return lax.ppermute(x, AXES, [(i, i ^ mask) for i in range(count)])


def place_of(rel, groups):
    pos = 0
    for g in groups:
        pos = pos * (1 << len(g)) + ((rel >> g[0]) & ((1 << len(g)) - 1))
    return pos


def gather_pieces(x, groups, count):
    cur = x[None]
    rels = [0]
    for g in groups[:1:-1]:
        ms = masks_of(g)
        cur = jnp.concatenate([cur] + [swap(cur, m, count) for m in ms], axis=0)
        rels = [r ^ m for m in [0] + ms for r in rels]
    pieces = [(rels, cur)]
    if len(groups) > 1:
        for m in masks_of(groups[1]):
            pieces.append(([r ^ m for r in rels], swap(cur, m, count)))
    for rs, arr in list(pieces):
        pieces.append(([r ^ 1 for r in rs], swap(arr, 1, count)))
    return pieces


def natural_order(pieces, me, count):
    rels = [r for rs, _ in pieces for r in rs]
    where = [0] * count
    for k, r in enumerate(rels):
        where[r] = k
    both = jnp.concatenate([a for _, a in pieces], axis=0)
    return jnp.take(both, jnp.asarray(where, jnp.int32)[jnp.arange(count) ^ me], axis=0)


def scatter_sum(pk, groups, count):
    half = count // 2
    cur = pk[:half].astype(f32) + swap(pk[half:], 1, count).astype(f32)
    for g in groups[1:]:
        ms = masks_of(g)
        n = cur.shape[0] // (len(ms) + 1)
        parts = [swap(cur[(k + 1) * n : (k + 2) * n].astype(bf16), m, count).astype(f32) for k, m in enumerate(ms)]
        cur = cur[:n]
        for part in parts:
            cur = cur + part
    return cur[0]


def total(x, groups, count):
    for g in groups:
        got = [x] + [swap(x, m, count) for m in masks_of(g)]
        while len(got) > 1:
            got = [got[k] + got[k + 1] for k in range(0, len(got), 2)]
        x = got[0]
    return x


def attn_fwd_body(me_ref, x_ref, rowv_ref, colv_ref, mask_ref, bias_ref, *refs, plan, rpd):
    pieces = refs[: len(plan)]
    (oT_ref, o_ref, qT_ref, kT_ref, v_ref, pT_ref, h1T_ref, w_ref) = refs[len(plan) : len(plan) + 8]
    wT, xs, h1p, kn, vT, osc, sem = refs[len(plan) + 8 :]

    @pl.when(pl.program_id(0) == 0)
    def _():
        copies = []
        for ref, rels in zip(pieces, plan):
            if rels is None:
                copies.append(pltpu.make_async_copy(ref, w_ref, sem.at[len(copies)]))
                continue
            for t, r in enumerate(rels):
                at = pl.multiple_of((r ^ me_ref[0]) * rpd, rpd)
                copies.append(
                    pltpu.make_async_copy(
                        ref.at[t, :, pl.ds(0, 3 * D)], w_ref.at[pl.ds(at, rpd), :], sem.at[len(copies)]
                    )
                )
        for c in copies:
            c.start()
        for c in copies:
            c.wait()
        for a in range(3 * D // LANES):
            wT[LANES * a : LANES * (a + 1), :] = w_ref[:, LANES * a : LANES * (a + 1)].T

    xs[0:GR, :] = x_ref[...].astype(f32)
    gain = rowv_ref[0:1, :]
    shift = rowv_ref[1:2, :]
    value_bias = rowv_ref[3:4, :]
    rows = lax.broadcasted_iota(jnp.int32, (104, 1), 0)
    for w in range(GW):
        xw = xs[CELLS * w : CELLS * w + 104, :]
        c = xw - jnp.mean(xw, axis=-1, keepdims=True)
        var = jnp.mean(c * c, axis=-1, keepdims=True)
        h = jnp.where(rows < CELLS, c * lax.rsqrt(var + 1e-5) * gain + shift, 0.0)
        h = jnp.concatenate([h, jnp.zeros((LANES - 104, D), f32)], axis=0).astype(bf16)
        h1p[LANES * w : LANES * w + LANES, :] = h
        for a in range(D // LANES):
            h1T_ref[LANES * a : LANES * a + LANES, LANES * w : LANES * w + LANES] = h[:, LANES * a : LANES * a + LANES].T
    h1T_ref[D : D + 16, :] = jnp.ones((16, GL), bf16)
    hp = h1p[...]
    qT_ref[...] = (nt(wT[0:D, :], hp) + colv_ref[:, 0:1]).astype(bf16)
    kT_ref[...] = nt(wT[D : 2 * D, :], hp).astype(bf16)
    vT[...] = (nt(wT[2 * D : 3 * D, :], hp) + colv_ref[:, 1:2]).astype(bf16)
    kn[...] = nn(hp, w_ref[:, D : 2 * D]).astype(bf16)
    v_ref[...] = (nn(hp, w_ref[:, 2 * D : 3 * D]) + value_bias).astype(bf16)
    lane = lax.broadcasted_iota(jnp.int32, (1, LANES), 1) // HD
    factor = HD**-0.5 * LOG2E

    def window(w, carry):
        at = pl.multiple_of(w * LANES, LANES)
        allowed = mask_ref[w]
        for g in range(4):
            kb = kn[pl.ds(at, KP), LANES * g : LANES * g + LANES]
            ks = jnp.concatenate([jnp.where(lane == q, kb, jnp.zeros_like(kb)) for q in range(4)], axis=0)
            s = nn(ks, qT_ref[LANES * g : LANES * g + LANES, pl.ds(at, LANES)])
            for q in range(4):
                h = 4 * g + q
                t = s[KP * q : KP * q + KP] * factor + bias_ref[h] + allowed
                e = jnp.exp2(t - jnp.max(t, axis=0, keepdims=True))
                p = (e * (1.0 / jnp.sum(e, axis=0, keepdims=True))).astype(bf16)
                pT_ref[w, h] = p
                oT_ref[HD * h : HD * h + HD, pl.ds(at, LANES)] = nn(
                    vT[HD * h : HD * h + HD, pl.ds(at, LANES)][:, 0:KP], p
                ).astype(bf16)
        return carry

    lax.fori_loop(0, GW, window, 0)
    for w in range(GW):
        for a in range(D // LANES):
            osc[CELLS * w : CELLS * w + 104, LANES * a : LANES * a + LANES] = (
                oT_ref[LANES * a : LANES * a + LANES, LANES * w : LANES * w + LANES].astype(f32).T[0:104]
            )
    o_ref[...] = osc[0:GR, :].astype(bf16)


def any_specs(n):
    return [pl.BlockSpec(memory_space=pl.ANY)] * n


SMEM = pl.BlockSpec(memory_space=pltpu.SMEM)


def attn_fwd(me, x, rowv, colv, allowed, bias, plan, pieces, rpd):
    n = x.shape[0] // GR
    copies = sum(1 if r is None else len(r) for r in plan)
    rb = pl.BlockSpec((GR, D), lambda i: (i, 0))
    tb = pl.BlockSpec((D, GL), lambda i: (0, i))
    return pl.pallas_call(
        functools.partial(attn_fwd_body, plan=plan, rpd=rpd),
        grid=(n,),
        in_specs=[SMEM, rb, whole((8, D)), whole((D, 2)), pl.BlockSpec((GW, KP, LANES), lambda i: (i, 0, 0)), whole((HEADS, KP, LANES))]
        + any_specs(len(pieces)),
        out_specs=[
            tb,
            rb,
            tb,
            tb,
            pl.BlockSpec((GL, D), lambda i: (i, 0)),
            pl.BlockSpec((GW, HEADS, KP, LANES), lambda i: (i, 0, 0, 0)),
            pl.BlockSpec((D + 16, GL), lambda i: (0, i)),
            whole((D, 3 * D)),
        ],
        out_shape=[
            sds((D, n * GL), bf16),
            sds((n * GR, D), bf16),
            sds((D, n * GL), bf16),
            sds((D, n * GL), bf16),
            sds((n * GL, D), bf16),
            sds((n * GW, HEADS, KP, LANES), bf16),
            sds((D + 16, n * GL), bf16),
            sds((D, 3 * D), bf16),
        ],
        scratch_shapes=[
            pltpu.VMEM((3 * D, D), bf16),
            pltpu.VMEM((GR + 8, D), f32),
            pltpu.VMEM((GL, D), bf16),
            pltpu.VMEM((GL, D), bf16),
            pltpu.VMEM((D, GL), bf16),
            pltpu.VMEM((GR + 8, D), f32),
            pltpu.SemaphoreType.DMA((copies,)),
        ],
        compiler_params=params(56),
        cost_estimate=pl.CostEstimate(flops=8 * 10**9, bytes_accessed=20 * 10**6, transcendentals=4 * 10**6),
        name="attn_fwd",
    )(me, x, rowv, colv, allowed, bias, *pieces)


def mlp_body(me_ref, x_ref, o_ref, g_ref, vld_ref, bf1_ref, rowv_ref, *refs, plan, rows, owners, rpd, groups):
    pieces = refs[: len(plan)]
    (mid_ref, dmid_ref, e_ref, vec_ref, dbf1_ref, sa_ref, p_ref, v_ref) = refs[len(plan) : len(plan) + 8]
    rest = refs[len(plan) + 8 :]
    if owners:
        pk_ref = rest[0]
        rest = rest[1:]
    else:
        dU_ref, dV_ref = rest[:2]
        rest = rest[2:]
    u4, h2, h2T, gp, gT, dh2, es, dus, sem = rest
    j = pl.program_id(0)
    padded = h2.shape[0]
    part = padded // 4
    proj_bias = rowv_ref[4:5, :]
    gain = rowv_ref[5:6, :]
    shift = rowv_ref[6:7, :]

    def copies():
        first, later = [], []
        count = 0
        for ref, rels in zip(pieces, plan):
            if rels is None:
                dst = (p_ref, u4, v_ref)[count]
                (first if count == 0 else later).append(pltpu.make_async_copy(ref, dst, sem.at[count]))
                count += 1
                continue
            for t, r in enumerate(rels):
                owner = r ^ me_ref[0]
                at = pl.ds(pl.multiple_of(owner * rpd, rpd), rpd)
                first.append(pltpu.make_async_copy(ref.at[t, 0], p_ref.at[at, :], sem.at[count]))
                later.append(pltpu.make_async_copy(ref.at[t, pl.ds(1, 4)], u4.at[:, at, :], sem.at[count + 1]))
                later.append(
                    pltpu.make_async_copy(
                        ref.at[t, pl.ds(5, 4)], v_ref.at[pl.ds(pl.multiple_of(owner * 4, 4), 4)], sem.at[count + 2]
                    )
                )
                count += 3
        return first, later

    @pl.when(j == 0)
    def _():
        first, later = copies()
        for c in first + later:
            c.start()
        h2[rows:padded, :] = jnp.zeros((padded - rows, D), bf16)
        gp[rows:padded, :] = jnp.zeros((padded - rows, D), bf16)
        gp[0:rows, :] = g_ref[...]
        for c in first:
            c.wait()

        def block(k, acc):
            at = pl.ds(pl.multiple_of(k * GR, 16), GR)
            a = nn(o_ref[at, :], p_ref[...]) + proj_bias
            acc = acc + jnp.sum(a * a * vld_ref[at, :], axis=0, keepdims=True)
            mid = x_ref[at, :].astype(f32) + a
            mid_ref[at, :] = mid
            c = mid - jnp.mean(mid, axis=-1, keepdims=True)
            var = jnp.mean(c * c, axis=-1, keepdims=True)
            h2[at, :] = (c * lax.rsqrt(var + 1e-5) * gain + shift).astype(bf16)
            return acc

        sa_ref[...] = jnp.broadcast_to(lax.fori_loop(0, rows // GR, block, jnp.zeros((1, D), f32)), (8, D))

        def turn(k, carry):
            at = pl.ds(pl.multiple_of(k * LANES, LANES), LANES)
            for a in range(D // LANES):
                cols = slice(LANES * a, LANES * a + LANES)
                h2T[cols, at] = h2[at, cols].T
                gT[cols, at] = gp[at, cols].T
            return carry

        lax.fori_loop(0, padded // LANES, turn, 0)
        for c in later:
            c.wait()

    up_bias = bf1_ref[...]

    def chunk(k, acc):
        at = pl.ds(pl.multiple_of(k * part, 16), part)
        u = nn(h2[at, :], u4[j]) + up_bias
        de = nt(gp[at, :], v_ref[pl.ds(pl.multiple_of(32 * j, 32), 32)].reshape(512, D))
        cdf = 0.5 * lax.erf(u * RT2) + 0.5
        es[at, :] = (u * cdf).astype(bf16)
        du = (de * (cdf + u * (PHI * jnp.exp2(u * u * (-0.5 * LOG2E))))).astype(bf16)
        dus[at, :] = du
        d = nt(du, u4[j])

        @pl.when(j == 0)
        def _():
            dh2[at, :] = d

        @pl.when(j > 0)
        def _():
            dh2[at, :] += d

        return acc + jnp.sum(du.astype(f32), axis=0, keepdims=True)

    dbf1_ref[...] = lax.fori_loop(0, 4, chunk, jnp.zeros((1, 512), f32))
    e_ref[...] = es[0:rows, :]
    dU = nn(h2T[...], dus[...]).astype(bf16)
    dV = nn(gT[...], es[...]).astype(bf16).T
    if owners:
        me = me_ref[0]
        at = pl.ds(pl.multiple_of(j * rpd, rpd), rpd)
        for k in range(owners):
            pk_ref[place_of(k ^ me, groups), at, :] = dU[rpd * k : rpd * k + rpd]
        per = 512 // (4 * rpd)
        for k in range(per):
            pk_ref[place_of((j * per + k) ^ me, groups), 4 * rpd : 8 * rpd, :] = dV[4 * rpd * k : 4 * rpd * k + 4 * rpd]
    else:
        dU_ref[...] = dU
        dV_ref[...] = dV

    @pl.when(j == pl.num_programs(0) - 1)
    def _():
        def block(k, acc):
            at = pl.ds(pl.multiple_of(k * GR, 16), GR)
            mid = mid_ref[at, :]
            c = mid - jnp.mean(mid, axis=-1, keepdims=True)
            rs = lax.rsqrt(jnp.mean(c * c, axis=-1, keepdims=True) + 1e-5)
            xh = c * rs
            d = dh2[at, :]
            dx = d * gain
            dxx = d * xh
            m1 = jnp.mean(dx, axis=-1, keepdims=True)
            m2 = jnp.mean(dxx * gain, axis=-1, keepdims=True)
            grad = g_ref[at, :].astype(f32)
            dm = grad + (dx - m1 - xh * m2) * rs
            dmid_ref[at, :] = dm
            terms = (dm.astype(bf16).astype(f32), dxx, d, grad)
            return tuple(a + jnp.sum(t, axis=0, keepdims=True) for a, t in zip(acc, terms))

        sums = lax.fori_loop(0, rows // GR, block, (jnp.zeros((1, D), f32),) * 4)
        for q in range(4):
            vec_ref[q : q + 1, :] = sums[q]
        vec_ref[4:8, :] = jnp.zeros((4, D), f32)


def mlp(me, x, o, g, vld, bf1, rowv, plan, pieces, rpd, owners, count, groups):
    rows = x.shape[0]
    padded = -(-rows // LANES) * LANES
    copies = sum(1 if r is None else 3 * len(r) for r in plan)
    rb = whole((rows, D))
    if owners:
        grad_specs = [whole((count, 8 * rpd, 512))]
        grad_shapes = [sds((count, 8 * rpd, 512), bf16)]
    else:
        grad_specs = [pl.BlockSpec((D, 512), lambda j: (0, j)), pl.BlockSpec((512, D), lambda j: (j, 0))]
        grad_shapes = [sds((D, FF), bf16), sds((FF, D), bf16)]
    return pl.pallas_call(
        functools.partial(mlp_body, plan=plan, rows=rows, owners=count if owners else 0, rpd=rpd, groups=groups),
        grid=(FF // 512,),
        in_specs=[SMEM, rb, rb, rb, whole((rows, 1)), pl.BlockSpec((1, 512), lambda j: (0, j)), whole((8, D))]
        + any_specs(len(pieces)),
        out_specs=[rb, rb, pl.BlockSpec((rows, 512), lambda j: (0, j)), whole((8, D)), pl.BlockSpec((1, 512), lambda j: (0, j)), whole((8, D)), whole((D, D)), whole((128, 16, D))]
        + grad_specs,
        out_shape=[sds((rows, D), f32), sds((rows, D), f32), sds((rows, FF), bf16), sds((8, D), f32), sds((1, FF), f32), sds((8, D), f32), sds((D, D), bf16), sds((128, 16, D), bf16)]
        + grad_shapes,
        scratch_shapes=[
            pltpu.VMEM((4, D, 512), bf16),
            pltpu.VMEM((padded, D), bf16),
            pltpu.VMEM((D, padded), bf16),
            pltpu.VMEM((padded, D), bf16),
            pltpu.VMEM((D, padded), bf16),
            pltpu.VMEM((padded, D), f32),
            pltpu.VMEM((padded, 512), bf16),
            pltpu.VMEM((padded, 512), bf16),
            pltpu.SemaphoreType.DMA((copies,)),
        ],
        compiler_params=params(60),
        cost_estimate=pl.CostEstimate(flops=18 * 10**9, bytes_accessed=30 * 10**6, transcendentals=7 * 10**6),
        name="mlp",
    )(me, x, o, g, vld, bf1, rowv, *pieces)


def attn_bwd_body(me_ref, dmid_ref, p_ref, oT_ref, qT_ref, kT_ref, v_ref, pT_ref, h1T_ref, *refs, owners, rpd, groups):
    dmT_ref, acc_ref, vec_ref = refs[:3]
    grads = refs[3:-5]
    xs, dap, doT, dw, dproj = refs[-5:]
    i = pl.program_id(0)

    @pl.when(i == 0)
    def _():
        acc_ref[...] = jnp.zeros_like(acc_ref)
        dw[...] = jnp.zeros_like(dw)
        dproj[...] = jnp.zeros_like(dproj)

    xs[0:GR, :] = dmid_ref[...]
    rows = lax.broadcasted_iota(jnp.int32, (104, 1), 0)
    for w in range(GW):
        d = jnp.where(rows < CELLS, xs[CELLS * w : CELLS * w + 104, :], 0.0)
        dap[LANES * w : LANES * w + LANES, :] = jnp.concatenate([d, jnp.zeros((LANES - 104, D), f32)], axis=0).astype(bf16)
    da = dap[...]
    doT[...] = nt(p_ref[...], da).astype(bf16)
    dproj[...] += nn(oT_ref[...], da)
    lane = lax.broadcasted_iota(jnp.int32, (1, LANES), 1) // HD
    factor = HD**-0.5
    tail = jnp.zeros((HD, LANES - KP), bf16)

    def window(w, carry):
        at = pl.ds(pl.multiple_of(w * LANES, LANES), LANES)
        for g in range(4):
            vb = v_ref[pl.ds(pl.multiple_of(w * LANES, LANES), KP), LANES * g : LANES * g + LANES]
            vs = jnp.concatenate([jnp.where(lane == q, vb, jnp.zeros_like(vb)) for q in range(4)], axis=0)
            dp = nn(vs, doT[LANES * g : LANES * g + LANES, at])
            for q in range(4):
                h = 4 * g + q
                head = slice(HD * h, HD * h + HD)
                p = pT_ref[w, h]
                do = doT[head, at]
                delta = jnp.sum(do.astype(f32) * oT_ref[head, at].astype(f32), axis=0, keepdims=True)
                ds = p.astype(f32) * (dp[KP * q : KP * q + KP] - delta)
                acc_ref[h] += ds
                ds = ds.astype(bf16)
                dmT_ref[head, at] = (nn(kT_ref[head, at][:, 0:KP], ds) * factor).astype(bf16)
                dk = (nt(qT_ref[head, at], ds) * factor).astype(bf16)
                dmT_ref[D + HD * h : D + HD * h + HD, at] = jnp.concatenate([dk, tail], axis=1)
                dv = nt(do, p).astype(bf16)
                dmT_ref[2 * D + HD * h : 2 * D + HD * h + HD, at] = jnp.concatenate([dv, tail], axis=1)
        return carry

    lax.fori_loop(0, GW, window, 0)
    dw[...] += nt(h1T_ref[...], dmT_ref[...])

    @pl.when(i == pl.num_programs(0) - 1)
    def _():
        if owners:
            me = me_ref[0]
            for k in range(owners):
                pos = place_of(k ^ me, groups)
                for q in range(3):
                    grads[0][pos, rpd * q : rpd * q + rpd, :] = dw[rpd * k : rpd * k + rpd, D * q : D * q + D].astype(bf16)
                grads[0][pos, 3 * rpd : 4 * rpd, :] = dproj[rpd * k : rpd * k + rpd, :].astype(bf16)
        else:
            grads[0][...] = dw[0:D, :].astype(bf16)
            grads[1][...] = dproj[...].astype(bf16)
        vec_ref[...] = dw[D : D + 8, :]


def attn_bwd(me, dmid, p, oT, qT, kT, v, pT, h1T, rpd, owners, count, groups):
    n = dmid.shape[0] // GR

    def tb(r):
        return pl.BlockSpec((r, GL), lambda i: (0, i))

    if owners:
        grad_shapes = [sds((count, 4 * rpd, D), bf16)]
    else:
        grad_shapes = [sds((D, 3 * D), bf16), sds((D, D), bf16)]
    return pl.pallas_call(
        functools.partial(attn_bwd_body, owners=count if owners else 0, rpd=rpd, groups=groups),
        grid=(n,),
        in_specs=[SMEM, pl.BlockSpec((GR, D), lambda i: (i, 0)), whole((D, D)), tb(D), tb(D), tb(D), pl.BlockSpec((GL, D), lambda i: (i, 0)), pl.BlockSpec((GW, HEADS, KP, LANES), lambda i: (i, 0, 0, 0)), tb(D + 16)],
        out_specs=[tb(3 * D), whole((HEADS, KP, LANES)), whole((8, 3 * D))] + [whole(s.shape) for s in grad_shapes],
        out_shape=[sds((3 * D, n * GL), bf16), sds((HEADS, KP, LANES), f32), sds((8, 3 * D), f32)] + grad_shapes,
        scratch_shapes=[
            pltpu.VMEM((GR + 8, D), f32),
            pltpu.VMEM((GL, D), bf16),
            pltpu.VMEM((D, GL), bf16),
            pltpu.VMEM((D + 16, 3 * D), f32),
            pltpu.VMEM((D, D), f32),
        ],
        compiler_params=params(60),
        cost_estimate=pl.CostEstimate(flops=15 * 10**9, bytes_accessed=25 * 10**6, transcendentals=0),
        name="attn_bwd",
    )(me, dmid, p, oT, qT, kT, v, pT, h1T)


def grad_in_body(dmT_ref, w_ref, x_ref, dmid_ref, rowv_ref, tg_ref, vec_ref, dsc):
    dT = nn(w_ref[...], dmT_ref[...])
    for w in range(GW):
        for a in range(D // LANES):
            cols = slice(LANES * a, LANES * a + LANES)
            dsc[CELLS * w : CELLS * w + 104, cols] = dT[cols, LANES * w : LANES * w + LANES].T[0:104]
    d = dsc[0:GR, :]
    x = x_ref[...].astype(f32)
    c = x - jnp.mean(x, axis=-1, keepdims=True)
    rs = lax.rsqrt(jnp.mean(c * c, axis=-1, keepdims=True) + 1e-5)
    xh = c * rs
    gain = rowv_ref[0:1, :]
    dx = d * gain
    dxx = d * xh
    m1 = jnp.mean(dx, axis=-1, keepdims=True)
    m2 = jnp.mean(dxx * gain, axis=-1, keepdims=True)
    tg_ref[...] = dmid_ref[...] + (dx - m1 - xh * m2) * rs

    @pl.when(pl.program_id(0) == 0)
    def _():
        vec_ref[...] = jnp.zeros_like(vec_ref)

    vec_ref[0:1, :] += jnp.sum(dxx, axis=0, keepdims=True)
    vec_ref[1:2, :] += jnp.sum(d, axis=0, keepdims=True)


def grad_in(dmT, w, x, dmid, rowv):
    n = x.shape[0] // GR
    rb = pl.BlockSpec((GR, D), lambda i: (i, 0))
    return pl.pallas_call(
        grad_in_body,
        grid=(n,),
        in_specs=[pl.BlockSpec((3 * D, GL), lambda i: (0, i)), whole((D, 3 * D)), rb, rb, whole((8, D))],
        out_specs=[rb, whole((8, D))],
        out_shape=[sds((n * GR, D), f32), sds((8, D), f32)],
        scratch_shapes=[pltpu.VMEM((GR + 8, D), f32)],
        compiler_params=params(40),
        cost_estimate=pl.CostEstimate(flops=4 * 10**9, bytes_accessed=16 * 10**6, transcendentals=0),
        name="grad_in",
    )(dmT, w, x, dmid, rowv)


def finish_body(e_ref, v_ref, mid_ref, x_ref, vld_ref, rowv_ref, sa_ref, res_ref, st_ref):
    f = nn(e_ref[...], v_ref[...].reshape(FF, D)) + rowv_ref[7:8, :]
    mid = mid_ref[...]
    out = mid + f
    res_ref[...] = out.astype(bf16)
    vl = vld_ref[...]
    x = x_ref[...].astype(f32)

    @pl.when(pl.program_id(0) == 0)
    def _():
        st_ref[...] = jnp.zeros_like(st_ref)
        st_ref[1:2, :] = sa_ref[0:1, :]

    for k, t in ((0, x), (2, mid), (3, f), (4, out)):
        st_ref[k : k + 1, :] += jnp.sum(t * t * vl, axis=0, keepdims=True)
    st_ref[5:6, :] += jnp.sum(jnp.broadcast_to(vl, (GR, D)), axis=0, keepdims=True)


def finish(e, v, mid, x, vld, rowv, sa):
    n = x.shape[0] // GR
    rb = pl.BlockSpec((GR, D), lambda i: (i, 0))
    return pl.pallas_call(
        finish_body,
        grid=(n,),
        in_specs=[pl.BlockSpec((GR, FF), lambda i: (i, 0)), whole((128, 16, D)), rb, rb, pl.BlockSpec((GR, 1), lambda i: (i, 0)), whole((8, D)), whole((8, D))],
        out_specs=[rb, whole((8, D))],
        out_shape=[sds((n * GR, D), bf16), sds((8, D), f32)],
        compiler_params=params(40),
        cost_estimate=pl.CostEstimate(flops=3 * 10**9, bytes_accessed=16 * 10**6, transcendentals=0),
        name="finish",
    )(e, v, mid, x, vld, rowv, sa)


def place_code(shape, axis):
    c = lax.broadcasted_iota(jnp.int32, shape, axis)
    return jnp.where(c < CELLS, (2 * WSIDE - 1) * (c // WSIDE) + c % WSIDE, -1000)


def rel_bias_body(t_ref, o_ref):
    t = t_ref[...]
    hi = t.astype(bf16)
    r = t - hi.astype(f32)
    md = r.astype(bf16)
    lo = (r - md.astype(f32)).astype(bf16)
    three = jnp.concatenate([hi, md, lo], axis=0)
    code = place_code((RP, LANES), 1) - lax.broadcasted_iota(jnp.int32, (RP, LANES), 0) + 180

    def step(j, carry):
        hit = jnp.where(code == (2 * WSIDE - 1) * (j // WSIDE) + j % WSIDE, 1.0, 0.0).astype(bf16)
        b = nn(three, hit)
        o_ref[:, pl.ds(j, 1), :] = (b[0:16] + b[16:32] + b[32:48]).reshape(HEADS, 1, LANES)
        return carry

    o_ref[:, CELLS:KP, :] = jnp.zeros((HEADS, KP - CELLS, LANES), f32)
    lax.fori_loop(0, CELLS, step, 0)


def rel_bias(table):
    return pl.pallas_call(
        rel_bias_body,
        out_shape=sds((HEADS, KP, LANES), f32),
        cost_estimate=pl.CostEstimate(flops=6 * 10**9, bytes_accessed=10**6, transcendentals=0),
        name="rel_bias",
    )(table)


def rel_grad_body(a_ref, o_ref):
    code = place_code((LANES, RP), 0) - lax.broadcasted_iota(jnp.int32, (LANES, RP), 1) + 180

    def step(j, acc):
        hit = jnp.where(code == (2 * WSIDE - 1) * (j // WSIDE) + j % WSIDE, 1.0, 0.0).astype(bf16)
        t = a_ref[:, pl.ds(j, 1), :].reshape(HEADS, LANES)
        hi = t.astype(bf16)
        lo = (t - hi.astype(f32)).astype(bf16)
        b = nn(jnp.concatenate([hi, lo], axis=0), hit)
        return acc + b[0:16] + b[16:32]

    o_ref[...] = lax.fori_loop(0, CELLS, step, jnp.zeros((HEADS, RP), f32))


def rel_grad(acc):
    return pl.pallas_call(
        rel_grad_body,
        out_shape=sds((HEADS, RP), f32),
        cost_estimate=pl.CostEstimate(flops=6 * 10**9, bytes_accessed=10**6, transcendentals=0),
        name="rel_grad",
    )(acc)


def shards(tokens, cotangent, regions, validity, qkv_weight, proj_weight, fc1_weight, fc2_weight, vectors, rel_table, *, count, inner):
    rows = tokens.shape[0]
    windows = rows // CELLS
    groups = bit_groups(count)
    rpd = D // count
    direct = rpd % 16 == 0
    me = lax.axis_index("dp") * inner + lax.axis_index("shard")
    me_s = me.astype(jnp.int32).reshape(1)

    vec_pieces = gather_pieces(vectors.reshape(1, -1), groups, count)
    attn_pieces = gather_pieces(qkv_weight.reshape(rpd, 3 * D), groups, count)
    packed = jnp.concatenate(
        [
            proj_weight.reshape(1, rpd, D),
            fc1_weight.reshape(rpd, 4, 512).transpose(1, 0, 2),
            fc2_weight.reshape(4, rpd, D),
        ],
        axis=0,
    )
    mlp_pieces = gather_pieces(packed.reshape(9 * rpd, D), groups, count)
    vec = natural_order(vec_pieces, me, count).reshape(-1).astype(f32)
    rowv = vec[: 8 * D].reshape(8, D)
    colv = rowv[2:4].T
    bf1 = vec[8 * D :].reshape(1, FF)
    if direct:
        attn_plan = [r for r, _ in attn_pieces]
        attn_w = [a for _, a in attn_pieces]
        mlp_plan = [r for r, _ in mlp_pieces]
        mlp_w = [a.reshape(-1, 9, rpd, D) for _, a in mlp_pieces]
    else:
        attn_plan = [None]
        attn_w = [natural_order(attn_pieces, me, count).reshape(D, 3 * D)]
        both = natural_order(mlp_pieces, me, count).reshape(count, 9, rpd, D)
        mlp_plan = [None] * 3
        mlp_w = [both[:, 0].reshape(D, D), both[:, 1:5].transpose(1, 0, 2, 3).reshape(4, D, 512), both[:, 5:].reshape(128, 16, D)]

    bias = rel_bias(jnp.pad(rel_table.T * LOG2E, ((0, 0), (0, RP - RELN))))
    reg = regions.reshape(windows, CELLS)
    val = validity.reshape(windows, CELLS)
    allowed = (reg[:, :, None] == reg[:, None, :]) & (val[:, :, None] == 1)
    allowed = jnp.where(allowed | jnp.eye(CELLS, dtype=jnp.bool_)[None], 0.0, NEG).astype(f32)
    allowed = jnp.pad(allowed, ((0, 0), (0, KP - CELLS), (0, LANES - CELLS)), constant_values=NEG)
    vld = validity.astype(f32).reshape(rows, 1)

    oT, o, qT, kT, v, pT, h1T, w_full = attn_fwd(me_s, tokens, rowv, colv, allowed, bias, attn_plan, attn_w, rpd)
    got = mlp(me_s, tokens, o, cotangent, vld, bf1, rowv, mlp_plan, mlp_w, rpd, direct, count, groups)
    mid, dmid, e, vec_two, dbf1, branch_sq, p_full, v_full = got[:8]
    order = None
    if direct:
        mlp_pk = got[8]
    else:
        blocks = jnp.arange(count)
        where = place_of(blocks, groups)
        order = jnp.zeros((count,), jnp.int32).at[where].set(blocks.astype(jnp.int32)) ^ me
        dU = got[8].reshape(count, rpd, 4, 512).transpose(0, 2, 1, 3).reshape(count, 4 * rpd, 512)
        mlp_pk = jnp.take(jnp.concatenate([dU, got[9].reshape(count, 4 * rpd, D)], axis=1), order, axis=0)
    mlp_sum = scatter_sum(mlp_pk, groups, count)

    got = attn_bwd(me_s, dmid, p_full, oT, qT, kT, v, pT, h1T, rpd, direct, count, groups)
    dmT, score_sums, vec_one = got[:3]
    if direct:
        attn_pk = got[3]
    else:
        dW = got[3].reshape(count, rpd, 3, D).transpose(0, 2, 1, 3).reshape(count, 3 * rpd, D)
        attn_pk = jnp.take(jnp.concatenate([dW, got[4].reshape(count, rpd, D)], axis=1), order, axis=0)
    attn_sum = scatter_sum(attn_pk, groups, count)
    grad_tokens, vec_in = grad_in(dmT, w_full, tokens, dmid, rowv)
    table = rel_grad(score_sums)
    result, squares = finish(e, v_full, mid, tokens, vld, rowv, branch_sq)
    small = jnp.concatenate(
        [
            vec_in[0:2],
            vec_one[0:1, 0:D],
            vec_one[0:1, 2 * D : 3 * D],
            vec_two[0:4],
            dbf1.reshape(4, D),
            table.reshape(-1, D),
            squares,
        ],
        axis=0,
    )
    small = total(small, groups, count)
    length = vectors.shape[0]
    grad_vectors = lax.dynamic_slice(small[:12].reshape(-1), (me * length,), (length,))
    grad_table = small[12:24].reshape(HEADS, RP)[:, :RELN].T
    sums = jnp.sum(small[24:32], axis=1)
    stats = jnp.sqrt(sums[0:5] / sums[5] + 1e-06)
    return (
        result,
        grad_tokens,
        attn_sum[: 3 * rpd].reshape(3, rpd, D).transpose(1, 0, 2).reshape(-1),
        attn_sum[3 * rpd :].reshape(-1),
        mlp_sum[: 4 * rpd].reshape(4, rpd, 512).transpose(1, 0, 2).reshape(-1),
        mlp_sum[4 * rpd :].reshape(-1),
        grad_vectors,
        grad_table,
        stats,
    )


def solution(mesh):
    flat = P(AXES)
    tall = P(AXES, None)
    in_specs = (tall, tall, flat, flat, flat, flat, flat, flat, flat, P())
    out_specs = (tall, tall, flat, flat, flat, flat, flat, P(), P())
    inner = mesh.shape["shard"]
    body = functools.partial(shards, count=mesh.shape["dp"] * inner, inner=inner)
    return jax.shard_map(body, mesh=mesh, in_specs=in_specs, out_specs=out_specs, check_vma=False)
```

```python
import functools

import jax
import jax.numpy as jnp
from jax import lax
from jax.experimental import pallas as pl
from jax.experimental.pallas import tpu as pltpu
from jax.sharding import PartitionSpec as P

D = 512
FF = 2048
HEADS = 16
HD = 32
WSIDE = 10
RELN = 361
CELLS = WSIDE * WSIDE
GW = 4
GR = GW * CELLS
KP = 112
LANES = 128
GL = GW * LANES
RP = 384
AXES = ("dp", "shard")
LOG2E = 1.4426950408889634
NEG = -1e9
RT2 = 0.7071067811865476
PHI = 0.3989422804014327
f32 = jnp.float32
bf16 = jnp.bfloat16
sds = jax.ShapeDtypeStruct


def nn(a, b):
    return lax.dot_general(a, b, (((1,), (0,)), ((), ())), preferred_element_type=f32)


def nt(a, b):
    return lax.dot_general(a, b, (((1,), (1,)), ((), ())), preferred_element_type=f32)


def whole(shape):
    return pl.BlockSpec(shape, lambda i: (0,) * len(shape))


def params(mib):
    return pltpu.CompilerParams(vmem_limit_bytes=mib * 2**20)


def bit_groups(count):
    bits = count.bit_length() - 1
    groups = [(0,)]
    at = 1
    while at < bits:
        groups.append(tuple(range(at, min(at + 2, bits))))
        at += 2
    return groups


def masks_of(group):
    return [sum(((v >> k) & 1) << b for k, b in enumerate(group)) for v in range(1, 1 << len(group))]


def swap(x, mask, count):
    return lax.ppermute(x, AXES, [(i, i ^ mask) for i in range(count)])


def place_of(rel, groups):
    pos = 0
    for g in groups:
        pos = pos * (1 << len(g)) + ((rel >> g[0]) & ((1 << len(g)) - 1))
    return pos


def after(values, *others):
    return lax.optimization_barrier((values, others))[0]


def gather_upper(x, groups, count):
    cur = x[None]
    rels = [0]
    for g in groups[:1:-1]:
        ms = masks_of(g)
        cur = jnp.concatenate([cur] + [swap(cur, m, count) for m in ms], axis=0)
        rels = [r ^ m for m in [0] + ms for r in rels]
    return rels, cur


def gather_plane(rels, cur, groups, count):
    return [(rels, cur)] + [([r ^ m for r in rels], swap(cur, m, count)) for m in masks_of(groups[1])]


def gather_core(pieces, count):
    return pieces + [([r ^ 1 for r in rels], swap(arr, 1, count)) for rels, arr in pieces]


def natural_order(pieces, me, count):
    rels = [r for rs, _ in pieces for r in rs]
    where = [0] * count
    for k, r in enumerate(rels):
        where[r] = k
    both = jnp.concatenate([a for _, a in pieces], axis=0)
    return jnp.take(both, jnp.asarray(where, jnp.int32)[jnp.arange(count) ^ me], axis=0)


def split_sum(terms, group):
    n = terms[0].shape[0] >> len(group)
    parts = [sum(t[k * n : (k + 1) * n].astype(f32) for t in terms) for k in range(1 << len(group))]
    return parts[0], [p.astype(bf16) for p in parts[1:]]


def send_parts(parts, group, count):
    return [swap(p, m, count) for p, m in zip(parts, masks_of(group))]


def total(x, groups, count):
    for g in groups:
        got = [x] + [swap(x, m, count) for m in masks_of(g)]
        while len(got) > 1:
            got = [got[k] + got[k + 1] for k in range(0, len(got), 2)]
        x = got[0]
    return x


def lay_vectors(raw, per, rowv_ref):
    unit = LANES // 2
    each = per // unit
    low = lax.broadcasted_iota(jnp.int32, (1, LANES), 1) < unit

    def half(c, high):
        owner, part = divmod(c, each)
        got = raw[owner, part // 2 : part // 2 + 1, :].astype(f32)
        return got if part % 2 == high else pltpu.roll(got, unit, 1)

    for m in range((8 * D + FF) // LANES):
        row, col = divmod(m * LANES, D)
        rowv_ref[row : row + 1, col : col + LANES] = jnp.where(low, half(2 * m, 0), half(2 * m + 1, 1))


def attn_fwd_body(me_ref, x_ref, mask_ref, bias_ref, *refs, plan, rpd, per):
    pieces = refs[: len(plan)]
    (oT_ref, o_ref, qT_ref, kT_ref, v_ref, pT_ref, h1T_ref, w_ref, rowv_ref) = refs[len(plan) : len(plan) + 9]
    wT, xs, h1p, kn, vT, osc, colv_ref, raw, sem = refs[len(plan) + 9 :]

    @pl.when(pl.program_id(0) == 0)
    def _():
        copies = []
        for ref, rels in zip(pieces, plan):
            if rels is None:
                copies.append(pltpu.make_async_copy(ref, (w_ref, rowv_ref)[len(copies)], sem.at[len(copies)]))
                continue
            for t, r in enumerate(rels):
                at = pl.multiple_of((r ^ me_ref[0]) * rpd, rpd)
                copies.append(
                    pltpu.make_async_copy(
                        ref.at[t, :, pl.ds(0, 3 * D)], w_ref.at[pl.ds(at, rpd), :], sem.at[len(copies)]
                    )
                )
                copies.append(
                    pltpu.make_async_copy(ref.at[t, :, pl.ds(3 * D, LANES)], raw.at[r ^ me_ref[0]], sem.at[len(copies)])
                )
        for c in copies:
            c.start()
        for c in copies:
            c.wait()
        for a in range(3 * D // LANES):
            wT[LANES * a : LANES * (a + 1), :] = w_ref[:, LANES * a : LANES * (a + 1)].T
        if plan[0] is not None:
            rowv_ref[12:16, :] = jnp.zeros((4, D), f32)
            lay_vectors(raw, per, rowv_ref)
        for a in range(D // LANES):
            colv_ref[LANES * a : LANES * (a + 1), :] = rowv_ref[0:8, LANES * a : LANES * (a + 1)].T

    xs[0:GR, :] = x_ref[...].astype(f32)
    gain = rowv_ref[0:1, :]
    shift = rowv_ref[1:2, :]
    value_bias = rowv_ref[3:4, :]
    rows = lax.broadcasted_iota(jnp.int32, (104, 1), 0)
    for w in range(GW):
        xw = xs[CELLS * w : CELLS * w + 104, :]
        c = xw - jnp.mean(xw, axis=-1, keepdims=True)
        var = jnp.mean(c * c, axis=-1, keepdims=True)
        h = jnp.where(rows < CELLS, c * lax.rsqrt(var + 1e-5) * gain + shift, 0.0)
        h = jnp.concatenate([h, jnp.zeros((LANES - 104, D), f32)], axis=0).astype(bf16)
        h1p[LANES * w : LANES * w + LANES, :] = h
        for a in range(D // LANES):
            h1T_ref[LANES * a : LANES * a + LANES, LANES * w : LANES * w + LANES] = h[:, LANES * a : LANES * a + LANES].T
    h1T_ref[D : D + 16, :] = jnp.ones((16, GL), bf16)
    hp = h1p[...]
    qT_ref[...] = (nt(wT[0:D, :], hp) + colv_ref[:, 2:3]).astype(bf16)
    kT_ref[...] = nt(wT[D : 2 * D, :], hp).astype(bf16)
    vT[...] = (nt(wT[2 * D : 3 * D, :], hp) + colv_ref[:, 3:4]).astype(bf16)
    kn[...] = nn(hp, w_ref[:, D : 2 * D]).astype(bf16)
    v_ref[...] = (nn(hp, w_ref[:, 2 * D : 3 * D]) + value_bias).astype(bf16)
    lane = lax.broadcasted_iota(jnp.int32, (1, LANES), 1) // HD
    factor = HD**-0.5 * LOG2E

    def window(w, carry):
        at = pl.multiple_of(w * LANES, LANES)
        allowed = mask_ref[w]
        for g in range(4):
            kb = kn[pl.ds(at, KP), LANES * g : LANES * g + LANES]
            ks = jnp.concatenate([jnp.where(lane == q, kb, jnp.zeros_like(kb)) for q in range(4)], axis=0)
            s = nn(ks, qT_ref[LANES * g : LANES * g + LANES, pl.ds(at, LANES)])
            for q in range(4):
                h = 4 * g + q
                t = s[KP * q : KP * q + KP] * factor + bias_ref[h] + allowed
                e = jnp.exp2(t - jnp.max(t, axis=0, keepdims=True))
                p = (e * (1.0 / jnp.sum(e, axis=0, keepdims=True))).astype(bf16)
                pT_ref[w, h] = p
                oT_ref[HD * h : HD * h + HD, pl.ds(at, LANES)] = nn(
                    vT[HD * h : HD * h + HD, pl.ds(at, LANES)][:, 0:KP], p
                ).astype(bf16)
        return carry

    lax.fori_loop(0, GW, window, 0)
    for w in range(GW):
        for a in range(D // LANES):
            osc[CELLS * w : CELLS * w + 104, LANES * a : LANES * a + LANES] = (
                oT_ref[LANES * a : LANES * a + LANES, LANES * w : LANES * w + LANES].astype(f32).T[0:104]
            )
    o_ref[...] = osc[0:GR, :].astype(bf16)


def any_specs(n):
    return [pl.BlockSpec(memory_space=pl.ANY)] * n


SMEM = pl.BlockSpec(memory_space=pltpu.SMEM)


def attn_fwd(me, x, allowed, bias, plan, pieces, rpd, per, count):
    n = x.shape[0] // GR
    copies = sum(1 if r is None else 2 * len(r) for r in plan)
    rb = pl.BlockSpec((GR, D), lambda i: (i, 0))
    tb = pl.BlockSpec((D, GL), lambda i: (0, i))
    return pl.pallas_call(
        functools.partial(attn_fwd_body, plan=plan, rpd=rpd, per=per),
        grid=(n,),
        in_specs=[SMEM, rb, pl.BlockSpec((GW, KP, LANES), lambda i: (i, 0, 0)), whole((HEADS, KP, LANES))]
        + any_specs(len(pieces)),
        out_specs=[
            tb,
            rb,
            tb,
            tb,
            pl.BlockSpec((GL, D), lambda i: (i, 0)),
            pl.BlockSpec((GW, HEADS, KP, LANES), lambda i: (i, 0, 0, 0)),
            pl.BlockSpec((D + 16, GL), lambda i: (0, i)),
            whole((D, 3 * D)),
            whole((16, D)),
        ],
        out_shape=[
            sds((D, n * GL), bf16),
            sds((n * GR, D), bf16),
            sds((D, n * GL), bf16),
            sds((D, n * GL), bf16),
            sds((n * GL, D), bf16),
            sds((n * GW, HEADS, KP, LANES), bf16),
            sds((D + 16, n * GL), bf16),
            sds((D, 3 * D), bf16),
            sds((16, D), f32),
        ],
        scratch_shapes=[
            pltpu.VMEM((3 * D, D), bf16),
            pltpu.VMEM((GR + 8, D), f32),
            pltpu.VMEM((GL, D), bf16),
            pltpu.VMEM((GL, D), bf16),
            pltpu.VMEM((D, GL), bf16),
            pltpu.VMEM((GR + 8, D), f32),
            pltpu.VMEM((D, 8), f32),
            pltpu.VMEM((count, max(rpd, 16), LANES), bf16),
            pltpu.SemaphoreType.DMA((copies,)),
        ],
        compiler_params=params(60),
        cost_estimate=pl.CostEstimate(flops=10**7, bytes_accessed=10**5, transcendentals=0),
        name="attn_fwd",
    )(me, x, allowed, bias, *pieces)


def mlp_body(me_ref, x_ref, o_ref, g_ref, vld_ref, rowv_ref, *refs, plan, rows, owners, rpd, groups):
    pieces = refs[: len(plan)]
    (mid_ref, dmid_ref, e_ref, vec_ref, dbf1_ref, sa_ref, p_ref, v_ref) = refs[len(plan) : len(plan) + 8]
    rest = refs[len(plan) + 8 :]
    if owners:
        keep_ref, send_ref = rest[:2]
    else:
        dU_ref, dV_ref = rest[:2]
    rest = rest[2:]
    u4, h2, h2T, gp, gT, dh2, es, dus, sem = rest
    j = pl.program_id(0)
    padded = h2.shape[0]
    part = padded // 4
    proj_bias = rowv_ref[4:5, :]
    gain = rowv_ref[5:6, :]
    shift = rowv_ref[6:7, :]

    def copies():
        first, later = [], []
        count = 0
        for ref, rels in zip(pieces, plan):
            if rels is None:
                dst = (p_ref, u4, v_ref)[count]
                (first if count == 0 else later).append(pltpu.make_async_copy(ref, dst, sem.at[count]))
                count += 1
                continue
            for t, r in enumerate(rels):
                owner = r ^ me_ref[0]
                at = pl.ds(pl.multiple_of(owner * rpd, rpd), rpd)
                first.append(pltpu.make_async_copy(ref.at[t, 0], p_ref.at[at, :], sem.at[count]))
                later.append(pltpu.make_async_copy(ref.at[t, pl.ds(1, 4)], u4.at[:, at, :], sem.at[count + 1]))
                later.append(
                    pltpu.make_async_copy(
                        ref.at[t, pl.ds(5, 4)], v_ref.at[pl.ds(pl.multiple_of(owner * 4, 4), 4)], sem.at[count + 2]
                    )
                )
                count += 3
        return first, later

    @pl.when(j == 0)
    def _():
        first, later = copies()
        for c in first + later:
            c.start()
        h2[rows:padded, :] = jnp.zeros((padded - rows, D), bf16)
        gp[rows:padded, :] = jnp.zeros((padded - rows, D), bf16)
        gp[0:rows, :] = g_ref[...]
        for c in first:
            c.wait()

        def block(k, acc):
            at = pl.ds(pl.multiple_of(k * GR, 16), GR)
            a = nn(o_ref[at, :], p_ref[...]) + proj_bias
            acc = acc + jnp.sum(a * a * vld_ref[at, :], axis=0, keepdims=True)
            mid = x_ref[at, :].astype(f32) + a
            mid_ref[at, :] = mid
            c = mid - jnp.mean(mid, axis=-1, keepdims=True)
            var = jnp.mean(c * c, axis=-1, keepdims=True)
            h2[at, :] = (c * lax.rsqrt(var + 1e-5) * gain + shift).astype(bf16)
            return acc

        sa_ref[...] = jnp.broadcast_to(lax.fori_loop(0, rows // GR, block, jnp.zeros((1, D), f32)), (8, D))

        def turn(k, carry):
            at = pl.ds(pl.multiple_of(k * LANES, LANES), LANES)
            for a in range(D // LANES):
                cols = slice(LANES * a, LANES * a + LANES)
                h2T[cols, at] = h2[at, cols].T
                gT[cols, at] = gp[at, cols].T
            return carry

        lax.fori_loop(0, padded // LANES, turn, 0)
        for c in later:
            c.wait()

    up_bias = rowv_ref[pl.ds(8 + j, 1), :]

    def chunk(k, acc):
        at = pl.ds(pl.multiple_of(k * part, 16), part)
        u = nn(h2[at, :], u4[j]) + up_bias
        de = nt(gp[at, :], v_ref[pl.ds(pl.multiple_of(32 * j, 32), 32)].reshape(512, D))
        cdf = 0.5 * lax.erf(u * RT2) + 0.5
        es[at, :] = (u * cdf).astype(bf16)
        du = (de * (cdf + u * (PHI * jnp.exp2(u * u * (-0.5 * LOG2E))))).astype(bf16)
        dus[at, :] = du
        d = nt(du, u4[j])

        @pl.when(j == 0)
        def _():
            dh2[at, :] = d

        @pl.when(j > 0)
        def _():
            dh2[at, :] += d

        return acc + jnp.sum(du.astype(f32), axis=0, keepdims=True)

    dbf1_ref[...] = lax.fori_loop(0, 4, chunk, jnp.zeros((1, 512), f32))
    e_ref[...] = es[0:rows, :]
    dU = nn(h2T[...], dus[...]).astype(bf16)
    dV = nn(gT[...], es[...]).astype(bf16).T
    if owners:
        me = me_ref[0]
        at = pl.ds(pl.multiple_of(j * rpd, rpd), rpd)
        per = 512 // (4 * rpd)

        def store(flip):
            for k in range(owners):
                to = (keep_ref, send_ref)[(k ^ flip) & 1]
                to[place_of(k ^ me, groups[1:]), at, :] = dU[rpd * k : rpd * k + rpd]
            for k in range(per):
                to = (keep_ref, send_ref)[(k ^ flip) & 1]
                to[place_of((j * per + k) ^ me, groups[1:]), 4 * rpd : 8 * rpd, :] = dV[4 * rpd * k : 4 * rpd * k + 4 * rpd]

        pl.when(me & 1 == 0)(lambda: store(0))
        pl.when(me & 1 == 1)(lambda: store(1))
    else:
        dU_ref[...] = dU
        dV_ref[...] = dV

    @pl.when(j == pl.num_programs(0) - 1)
    def _():
        def block(k, acc):
            at = pl.ds(pl.multiple_of(k * GR, 16), GR)
            mid = mid_ref[at, :]
            c = mid - jnp.mean(mid, axis=-1, keepdims=True)
            rs = lax.rsqrt(jnp.mean(c * c, axis=-1, keepdims=True) + 1e-5)
            xh = c * rs
            d = dh2[at, :]
            dx = d * gain
            dxx = d * xh
            m1 = jnp.mean(dx, axis=-1, keepdims=True)
            m2 = jnp.mean(dxx * gain, axis=-1, keepdims=True)
            grad = g_ref[at, :].astype(f32)
            dm = grad + (dx - m1 - xh * m2) * rs
            dmid_ref[at, :] = dm
            terms = (dm.astype(bf16).astype(f32), dxx, d, grad)
            return tuple(a + jnp.sum(t, axis=0, keepdims=True) for a, t in zip(acc, terms))

        sums = lax.fori_loop(0, rows // GR, block, (jnp.zeros((1, D), f32),) * 4)
        for q in range(4):
            vec_ref[q : q + 1, :] = sums[q]
        vec_ref[4:8, :] = jnp.zeros((4, D), f32)


def mlp(me, x, o, g, vld, rowv, plan, pieces, rpd, owners, count, groups):
    rows = x.shape[0]
    padded = -(-rows // LANES) * LANES
    copies = sum(1 if r is None else 3 * len(r) for r in plan)
    rb = whole((rows, D))
    if owners:
        grad_specs = [whole((count // 2, 8 * rpd, 512))] * 2
        grad_shapes = [sds((count // 2, 8 * rpd, 512), bf16)] * 2
    else:
        grad_specs = [pl.BlockSpec((D, 512), lambda j: (0, j)), pl.BlockSpec((512, D), lambda j: (j, 0))]
        grad_shapes = [sds((D, FF), bf16), sds((FF, D), bf16)]
    return pl.pallas_call(
        functools.partial(mlp_body, plan=plan, rows=rows, owners=count if owners else 0, rpd=rpd, groups=groups),
        grid=(FF // 512,),
        in_specs=[SMEM, rb, rb, rb, whole((rows, 1)), whole((16, D))]
        + any_specs(len(pieces)),
        out_specs=[rb, rb, pl.BlockSpec((rows, 512), lambda j: (0, j)), whole((8, D)), pl.BlockSpec((1, 512), lambda j: (0, j)), whole((8, D)), whole((D, D)), whole((128, 16, D))]
        + grad_specs,
        out_shape=[sds((rows, D), f32), sds((rows, D), f32), sds((rows, FF), bf16), sds((8, D), f32), sds((1, FF), f32), sds((8, D), f32), sds((D, D), bf16), sds((128, 16, D), bf16)]
        + grad_shapes,
        scratch_shapes=[
            pltpu.VMEM((4, D, 512), bf16),
            pltpu.VMEM((padded, D), bf16),
            pltpu.VMEM((D, padded), bf16),
            pltpu.VMEM((padded, D), bf16),
            pltpu.VMEM((D, padded), bf16),
            pltpu.VMEM((padded, D), f32),
            pltpu.VMEM((padded, 512), bf16),
            pltpu.VMEM((padded, 512), bf16),
            pltpu.SemaphoreType.DMA((copies,)),
        ],
        compiler_params=params(60),
        cost_estimate=pl.CostEstimate(flops=10**7, bytes_accessed=10**5, transcendentals=0),
        name="mlp",
    )(me, x, o, g, vld, rowv, *pieces)


def attn_bwd_body(me_ref, dmid_ref, p_ref, oT_ref, qT_ref, kT_ref, v_ref, pT_ref, h1T_ref, *refs, owners, rpd, groups):
    dmT_ref, acc_ref, vec_ref = refs[:3]
    grads = refs[3:-5]
    xs, dap, doT, dw, dproj = refs[-5:]
    i = pl.program_id(0)

    @pl.when(i == 0)
    def _():
        acc_ref[...] = jnp.zeros_like(acc_ref)
        dw[...] = jnp.zeros_like(dw)
        dproj[...] = jnp.zeros_like(dproj)

    xs[0:GR, :] = dmid_ref[...]
    rows = lax.broadcasted_iota(jnp.int32, (104, 1), 0)
    for w in range(GW):
        d = jnp.where(rows < CELLS, xs[CELLS * w : CELLS * w + 104, :], 0.0)
        dap[LANES * w : LANES * w + LANES, :] = jnp.concatenate([d, jnp.zeros((LANES - 104, D), f32)], axis=0).astype(bf16)
    da = dap[...]
    doT[...] = nt(p_ref[...], da).astype(bf16)
    dproj[...] += nn(oT_ref[...], da)
    lane = lax.broadcasted_iota(jnp.int32, (1, LANES), 1) // HD
    factor = HD**-0.5
    tail = jnp.zeros((HD, LANES - KP), bf16)

    def window(w, carry):
        at = pl.ds(pl.multiple_of(w * LANES, LANES), LANES)
        for g in range(4):
            vb = v_ref[pl.ds(pl.multiple_of(w * LANES, LANES), KP), LANES * g : LANES * g + LANES]
            vs = jnp.concatenate([jnp.where(lane == q, vb, jnp.zeros_like(vb)) for q in range(4)], axis=0)
            dp = nn(vs, doT[LANES * g : LANES * g + LANES, at])
            for q in range(4):
                h = 4 * g + q
                head = slice(HD * h, HD * h + HD)
                p = pT_ref[w, h]
                do = doT[head, at]
                delta = jnp.sum(do.astype(f32) * oT_ref[head, at].astype(f32), axis=0, keepdims=True)
                ds = p.astype(f32) * (dp[KP * q : KP * q + KP] - delta)
                acc_ref[h] += ds
                ds = ds.astype(bf16)
                dmT_ref[head, at] = (nn(kT_ref[head, at][:, 0:KP], ds) * factor).astype(bf16)
                dk = (nt(qT_ref[head, at], ds) * factor).astype(bf16)
                dmT_ref[D + HD * h : D + HD * h + HD, at] = jnp.concatenate([dk, tail], axis=1)
                dv = nt(do, p).astype(bf16)
                dmT_ref[2 * D + HD * h : 2 * D + HD * h + HD, at] = jnp.concatenate([dv, tail], axis=1)
        return carry

    lax.fori_loop(0, GW, window, 0)
    dw[...] += nt(h1T_ref[...], dmT_ref[...])

    @pl.when(i == pl.num_programs(0) - 1)
    def _():
        if owners:
            me = me_ref[0]

            def store(flip):
                for k in range(owners):
                    to = grads[(k ^ flip) & 1]
                    pos = place_of(k ^ me, groups[1:])
                    for q in range(3):
                        to[pos, rpd * q : rpd * q + rpd, :] = dw[rpd * k : rpd * k + rpd, D * q : D * q + D].astype(bf16)
                    to[pos, 3 * rpd : 4 * rpd, :] = dproj[rpd * k : rpd * k + rpd, :].astype(bf16)

            pl.when(me & 1 == 0)(lambda: store(0))
            pl.when(me & 1 == 1)(lambda: store(1))
        else:
            grads[0][...] = dw[0:D, :].astype(bf16)
            grads[1][...] = dproj[...].astype(bf16)
        vec_ref[...] = dw[D : D + 8, :]


def attn_bwd(me, dmid, p, oT, qT, kT, v, pT, h1T, rpd, owners, count, groups):
    n = dmid.shape[0] // GR

    def tb(r):
        return pl.BlockSpec((r, GL), lambda i: (0, i))

    if owners:
        grad_shapes = [sds((count // 2, 4 * rpd, D), bf16)] * 2
    else:
        grad_shapes = [sds((D, 3 * D), bf16), sds((D, D), bf16)]
    return pl.pallas_call(
        functools.partial(attn_bwd_body, owners=count if owners else 0, rpd=rpd, groups=groups),
        grid=(n,),
        in_specs=[SMEM, pl.BlockSpec((GR, D), lambda i: (i, 0)), whole((D, D)), tb(D), tb(D), tb(D), pl.BlockSpec((GL, D), lambda i: (i, 0)), pl.BlockSpec((GW, HEADS, KP, LANES), lambda i: (i, 0, 0, 0)), tb(D + 16)],
        out_specs=[tb(3 * D), whole((HEADS, KP, LANES)), whole((8, 3 * D))] + [whole(s.shape) for s in grad_shapes],
        out_shape=[sds((3 * D, n * GL), bf16), sds((HEADS, KP, LANES), f32), sds((8, 3 * D), f32)] + grad_shapes,
        scratch_shapes=[
            pltpu.VMEM((GR + 8, D), f32),
            pltpu.VMEM((GL, D), bf16),
            pltpu.VMEM((D, GL), bf16),
            pltpu.VMEM((D + 16, 3 * D), f32),
            pltpu.VMEM((D, D), f32),
        ],
        compiler_params=params(60),
        cost_estimate=pl.CostEstimate(flops=10**7, bytes_accessed=10**5, transcendentals=0),
        name="attn_bwd",
    )(me, dmid, p, oT, qT, kT, v, pT, h1T)


def grad_in_body(dmT_ref, w_ref, x_ref, dmid_ref, rowv_ref, tg_ref, vec_ref, dsc):
    dT = nn(w_ref[...], dmT_ref[...])
    for w in range(GW):
        for a in range(D // LANES):
            cols = slice(LANES * a, LANES * a + LANES)
            dsc[CELLS * w : CELLS * w + 104, cols] = dT[cols, LANES * w : LANES * w + LANES].T[0:104]
    d = dsc[0:GR, :]
    x = x_ref[...].astype(f32)
    c = x - jnp.mean(x, axis=-1, keepdims=True)
    rs = lax.rsqrt(jnp.mean(c * c, axis=-1, keepdims=True) + 1e-5)
    xh = c * rs
    gain = rowv_ref[0:1, :]
    dx = d * gain
    dxx = d * xh
    m1 = jnp.mean(dx, axis=-1, keepdims=True)
    m2 = jnp.mean(dxx * gain, axis=-1, keepdims=True)
    tg_ref[...] = dmid_ref[...] + (dx - m1 - xh * m2) * rs

    @pl.when(pl.program_id(0) == 0)
    def _():
        vec_ref[...] = jnp.zeros_like(vec_ref)

    vec_ref[0:1, :] += jnp.sum(dxx, axis=0, keepdims=True)
    vec_ref[1:2, :] += jnp.sum(d, axis=0, keepdims=True)


def grad_in(dmT, w, x, dmid, rowv):
    n = x.shape[0] // GR
    rb = pl.BlockSpec((GR, D), lambda i: (i, 0))
    return pl.pallas_call(
        grad_in_body,
        grid=(n,),
        in_specs=[pl.BlockSpec((3 * D, GL), lambda i: (0, i)), whole((D, 3 * D)), rb, rb, whole((16, D))],
        out_specs=[rb, whole((8, D))],
        out_shape=[sds((n * GR, D), f32), sds((8, D), f32)],
        scratch_shapes=[pltpu.VMEM((GR + 8, D), f32)],
        compiler_params=params(60),
        cost_estimate=pl.CostEstimate(flops=10**7, bytes_accessed=10**5, transcendentals=0),
        name="grad_in",
    )(dmT, w, x, dmid, rowv)


def finish_body(e_ref, v_ref, mid_ref, x_ref, vld_ref, rowv_ref, sa_ref, res_ref, st_ref):
    f = nn(e_ref[...], v_ref[...].reshape(FF, D)) + rowv_ref[7:8, :]
    mid = mid_ref[...]
    out = mid + f
    res_ref[...] = out.astype(bf16)
    vl = vld_ref[...]
    x = x_ref[...].astype(f32)

    @pl.when(pl.program_id(0) == 0)
    def _():
        st_ref[...] = jnp.zeros_like(st_ref)
        st_ref[1:2, :] = sa_ref[0:1, :]

    for k, t in ((0, x), (2, mid), (3, f), (4, out)):
        st_ref[k : k + 1, :] += jnp.sum(t * t * vl, axis=0, keepdims=True)
    st_ref[5:6, :] += jnp.sum(jnp.broadcast_to(vl, (GR, D)), axis=0, keepdims=True)


def finish(e, v, mid, x, vld, rowv, sa):
    n = x.shape[0] // GR
    rb = pl.BlockSpec((GR, D), lambda i: (i, 0))
    return pl.pallas_call(
        finish_body,
        grid=(n,),
        in_specs=[pl.BlockSpec((GR, FF), lambda i: (i, 0)), whole((128, 16, D)), rb, rb, pl.BlockSpec((GR, 1), lambda i: (i, 0)), whole((16, D)), whole((8, D))],
        out_specs=[rb, whole((8, D))],
        out_shape=[sds((n * GR, D), bf16), sds((8, D), f32)],
        compiler_params=params(60),
        cost_estimate=pl.CostEstimate(flops=10**7, bytes_accessed=10**5, transcendentals=0),
        name="finish",
    )(e, v, mid, x, vld, rowv, sa)


def place_hits(shape, axis, rev=0):
    c = lax.broadcasted_iota(jnp.int32, shape, 1 - axis)
    code = jnp.where(c < CELLS, (2 * WSIDE - 1) * (c // WSIDE) + c % WSIDE, -1000)
    if rev:
        code = rev - code
    return jnp.where(code == lax.broadcasted_iota(jnp.int32, shape, axis), 1.0, 0.0).astype(bf16)


def rel_bias_body(t_ref, o_ref):
    keys = place_hits((KP, 192), 1)
    queries = place_hits((256, LANES), 0)

    def head(h, carry):
        row = pltpu.roll(jnp.broadcast_to(t_ref[pl.ds(h, 1), :], (8, RP)), 0, 1, stride=1, stride_axis=0)
        t = jnp.concatenate([pltpu.roll(row, (8 * k - 180) % RP, 1)[:, 0:256] for k in range(24)], axis=0)
        hi = t.astype(bf16)
        r = t - hi.astype(f32)
        md = r.astype(bf16)
        lo = (r - md.astype(f32)).astype(bf16)
        o_ref[h] = sum(nn(nn(keys, part).astype(bf16), queries) for part in (lo, md, hi))
        return carry

    lax.fori_loop(0, HEADS, head, 0, unroll=8)


def rel_bias(table):
    return pl.pallas_call(
        rel_bias_body,
        out_shape=sds((HEADS, KP, LANES), f32),
        compiler_params=params(60),
        cost_estimate=pl.CostEstimate(flops=10**7, bytes_accessed=10**5, transcendentals=0),
        name="rel_bias",
    )(table)


def rel_grad_body(a_ref, o_ref):
    keys = place_hits((192, KP), 0, 191)
    queries = place_hits((LANES, 256), 1)
    zero = jnp.zeros((8, RP - 256), f32)

    def head(h, carry):
        a = a_ref[h]
        hi = a.astype(bf16)
        lo = (a - hi.astype(f32)).astype(bf16)
        b = nn(nn(keys, hi).astype(bf16), queries) + nn(nn(keys, lo).astype(bf16), queries)
        t = jnp.zeros((8, RP), f32)
        for k in range(24):
            t = t + pltpu.roll(jnp.concatenate([b[8 * k : 8 * k + 8], zero], axis=1), (8 * k - 11) % RP, 1)
        t = pltpu.roll(t, 0, 1, stride=1, stride_axis=0)
        o_ref[pl.ds(h, 1), :] = jnp.sum(t, axis=0, keepdims=True)
        return carry

    lax.fori_loop(0, HEADS, head, 0, unroll=8)


def rel_grad(acc):
    return pl.pallas_call(
        rel_grad_body,
        out_shape=sds((HEADS, RP), f32),
        compiler_params=params(60),
        cost_estimate=pl.CostEstimate(flops=10**7, bytes_accessed=10**5, transcendentals=0),
        name="rel_grad",
    )(acc)


def shards(tokens, cotangent, regions, validity, qkv_weight, proj_weight, fc1_weight, fc2_weight, vectors, rel_table, *, count, inner):
    rows = tokens.shape[0]
    windows = rows // CELLS
    groups = bit_groups(count)
    rpd = D // count
    direct = rpd % 16 == 0
    me = lax.axis_index("dp") * inner + lax.axis_index("shard")
    me_s = me.astype(jnp.int32).reshape(1)

    per = vectors.shape[0]
    if direct:
        own = jnp.pad(vectors, (0, rpd * LANES - per)).reshape(rpd, LANES)
        own = jnp.concatenate([qkv_weight.reshape(rpd, 3 * D), own], axis=1)
    else:
        own = jnp.concatenate([qkv_weight, vectors]).reshape(1, -1)
    rels, attn_up = gather_upper(own, groups, count)
    packed = jnp.concatenate(
        [
            proj_weight.reshape(1, rpd, D),
            fc1_weight.reshape(rpd, 4, 512).transpose(1, 0, 2),
            fc2_weight.reshape(4, rpd, D),
        ],
        axis=0,
    )
    packed = after(packed.reshape(9 * rpd, D), attn_up)
    _, mlp_up = gather_upper(packed, groups, count)
    attn_pieces = gather_core(gather_plane(rels, attn_up, groups, count), count)
    mlp_pieces = gather_plane(rels, mlp_up, groups, count)
    if direct:
        attn_plan = [r for r, _ in attn_pieces]
        attn_w = [a for _, a in attn_pieces]
    else:
        attn_plan = [None] * 2
        both = natural_order(attn_pieces, me, count).reshape(count, -1)
        attn_w = [both[:, : 3 * D * rpd].reshape(D, 3 * D), jnp.pad(both[:, 3 * D * rpd :].astype(f32).reshape(12, D), ((0, 4), (0, 0)))]

    bias = rel_bias(jnp.pad(rel_table.T * LOG2E, ((0, 0), (0, RP - RELN))))
    reg = regions.reshape(windows, CELLS)
    val = validity.reshape(windows, CELLS)
    allowed = (reg[:, :, None] == reg[:, None, :]) & (val[:, :, None] == 1)
    allowed = jnp.where(allowed | jnp.eye(CELLS, dtype=jnp.bool_)[None], 0.0, NEG).astype(f32)
    allowed = jnp.pad(allowed, ((0, 0), (0, KP - CELLS), (0, LANES - CELLS)), constant_values=NEG)
    vld = validity.astype(f32).reshape(rows, 1)

    x = after(tokens, mlp_up)
    oT, o, qT, kT, v, pT, h1T, w_full, rowv = attn_fwd(me_s, x, allowed, bias, attn_plan, attn_w, rpd, per, count)

    held = after([a for _, a in mlp_pieces], o)
    mlp_pieces = gather_core([(r, a) for (r, _), a in zip(mlp_pieces, held)], count)
    if direct:
        mlp_plan = [r for r, _ in mlp_pieces]
        mlp_w = [a.reshape(-1, 9, rpd, D) for _, a in mlp_pieces]
    else:
        both = natural_order(mlp_pieces, me, count).reshape(count, 9, rpd, D)
        mlp_plan = [None] * 3
        mlp_w = [both[:, 0].reshape(D, D), both[:, 1:5].transpose(1, 0, 2, 3).reshape(4, D, 512), both[:, 5:].reshape(128, 16, D)]
    got = mlp(me_s, tokens, o, cotangent, vld, rowv, mlp_plan, mlp_w, rpd, direct, count, groups)
    mid, dmid, e, vec_two, dbf1, branch_sq, p_full, v_full = got[:8]
    order = None
    if direct:
        mlp_keep, mlp_send = got[8:]
    else:
        blocks = jnp.arange(count)
        where = place_of(blocks, groups)
        order = jnp.zeros((count,), jnp.int32).at[where].set(blocks.astype(jnp.int32)) ^ me
        dU = got[8].reshape(count, rpd, 4, 512).transpose(0, 2, 1, 3).reshape(count, 4 * rpd, 512)
        pk = jnp.take(jnp.concatenate([dU, got[9].reshape(count, 4 * rpd, D)], axis=1), order, axis=0)
        mlp_keep, mlp_send = pk[: count // 2], pk[count // 2 :]

    other = swap(mlp_send, 1, count)
    result, squares = finish(e, v_full, mid, tokens, vld, rowv, branch_sq)
    other = after(other, result)
    mlp_own, parts = split_sum([mlp_keep, other], groups[1])
    mlp_got = send_parts(parts, groups[1], count)
    dmid = after(dmid, parts)
    got = attn_bwd(me_s, dmid, p_full, oT, qT, kT, v, pT, h1T, rpd, direct, count, groups)
    dmT, score_sums, vec_one = got[:3]
    if direct:
        attn_keep, attn_send = got[3:]
    else:
        dW = got[3].reshape(count, rpd, 3, D).transpose(0, 2, 1, 3).reshape(count, 3 * rpd, D)
        pk = jnp.take(jnp.concatenate([dW, got[4].reshape(count, rpd, D)], axis=1), order, axis=0)
        attn_keep, attn_send = pk[: count // 2], pk[count // 2 :]
    mlp_got, attn_send, score_sums, dmT = lax.optimization_barrier((mlp_got, attn_send, score_sums, dmT))
    other = swap(attn_send, 1, count)
    attn_own, parts = split_sum([attn_keep, other], groups[1])
    attn_got = send_parts(parts, groups[1], count)
    mlp_terms = [mlp_own] + mlp_got
    dmT = after(dmT, parts)
    grad_tokens, vec_in = grad_in(dmT, w_full, tokens, dmid, rowv)
    table = rel_grad(after(score_sums, parts))
    attn_terms = [attn_own] + after(attn_got, grad_tokens)
    for g in groups[2:]:
        mlp_own, parts = split_sum(mlp_terms, g)
        mlp_terms = [mlp_own] + send_parts(parts, g, count)
        attn_own, parts = split_sum(attn_terms, g)
        attn_terms = [attn_own] + send_parts(parts, g, count)
    mlp_sum = sum(t[0].astype(f32) for t in mlp_terms)
    attn_sum = sum(t[0].astype(f32) for t in attn_terms)
    small = jnp.concatenate(
        [
            vec_in[0:2],
            vec_one[0:1, 0:D],
            vec_one[0:1, 2 * D : 3 * D],
            vec_two[0:4],
            dbf1.reshape(4, D),
            table.reshape(-1, D),
            squares,
        ],
        axis=0,
    )
    small = total(small, groups, count)
    length = vectors.shape[0]
    grad_vectors = lax.dynamic_slice(small[:12].reshape(-1), (me * length,), (length,))
    grad_table = small[12:24].reshape(HEADS, RP)[:, :RELN].T
    sums = jnp.sum(small[24:32], axis=1)
    stats = jnp.sqrt(sums[0:5] / sums[5] + 1e-06)
    return (
        result,
        grad_tokens,
        attn_sum[: 3 * rpd].reshape(3, rpd, D).transpose(1, 0, 2).reshape(-1),
        attn_sum[3 * rpd :].reshape(-1),
        mlp_sum[: 4 * rpd].reshape(4, rpd, 512).transpose(1, 0, 2).reshape(-1),
        mlp_sum[4 * rpd :].reshape(-1),
        grad_vectors,
        grad_table,
        stats,
    )


def solution(mesh):
    flat = P(AXES)
    tall = P(AXES, None)
    in_specs = (tall, tall, flat, flat, flat, flat, flat, flat, flat, P())
    out_specs = (tall, tall, flat, flat, flat, flat, flat, P(), P())
    inner = mesh.shape["shard"]
    body = functools.partial(shards, count=mesh.shape["dp"] * inner, inner=inner)
    return jax.shard_map(body, mesh=mesh, in_specs=in_specs, out_specs=out_specs, check_vma=False)
```

```python
import functools

import jax
import jax.numpy as jnp
from jax import lax
from jax.experimental import pallas as pl
from jax.experimental.pallas import tpu as pltpu
from jax.sharding import PartitionSpec as P

D = 512
FF = 2048
HEADS = 16
HD = 32
WSIDE = 10
RELN = 361
CELLS = WSIDE * WSIDE
GW = 4
GR = GW * CELLS
KP = 112
LANES = 128
GL = GW * LANES
RP = 384
AXES = ("dp", "shard")
LOG2E = 1.4426950408889634
NEG = -1e9
RT2 = 0.7071067811865476
PHI = 0.3989422804014327
f32 = jnp.float32
bf16 = jnp.bfloat16
sds = jax.ShapeDtypeStruct


def nn(a, b):
    return lax.dot_general(a, b, (((1,), (0,)), ((), ())), preferred_element_type=f32)


def nt(a, b):
    return lax.dot_general(a, b, (((1,), (1,)), ((), ())), preferred_element_type=f32)


def whole(shape):
    return pl.BlockSpec(shape, lambda i: (0,) * len(shape))


def params(mib):
    return pltpu.CompilerParams(vmem_limit_bytes=mib * 2**20)


def bit_groups(count):
    bits = count.bit_length() - 1
    groups = [(0,)]
    at = 1
    while at < bits:
        groups.append(tuple(range(at, min(at + 2, bits))))
        at += 2
    return groups


def masks_of(group):
    return [sum(((v >> k) & 1) << b for k, b in enumerate(group)) for v in range(1, 1 << len(group))]


def swap(x, mask, count):
    return lax.ppermute(x, AXES, [(i, i ^ mask) for i in range(count)])


def place_of(rel, groups):
    pos = 0
    for g in groups:
        pos = pos * (1 << len(g)) + ((rel >> g[0]) & ((1 << len(g)) - 1))
    return pos


def after(values, *others):
    return lax.optimization_barrier((values, others))[0]


def gather_upper(x, groups, count):
    cur = x[None]
    rels = [0]
    for g in groups[:1:-1]:
        ms = masks_of(g)
        cur = jnp.concatenate([cur] + [swap(cur, m, count) for m in ms], axis=0)
        rels = [r ^ m for m in [0] + ms for r in rels]
    return rels, cur


def gather_plane(rels, cur, groups, count):
    return [(rels, cur)] + [([r ^ m for r in rels], swap(cur, m, count)) for m in masks_of(groups[1])]


def gather_core(pieces, count):
    return pieces + [([r ^ 1 for r in rels], swap(arr, 1, count)) for rels, arr in pieces]


def natural_order(pieces, me, count):
    rels = [r for rs, _ in pieces for r in rs]
    where = [0] * count
    for k, r in enumerate(rels):
        where[r] = k
    both = jnp.concatenate([a for _, a in pieces], axis=0)
    return jnp.take(both, jnp.asarray(where, jnp.int32)[jnp.arange(count) ^ me], axis=0)


def split_sum(terms, group):
    n = terms[0].shape[0] >> len(group)
    parts = [sum(t[k * n : (k + 1) * n].astype(f32) for t in terms) for k in range(1 << len(group))]
    return parts[0], [p.astype(bf16) for p in parts[1:]]


def send_parts(parts, group, count):
    return [swap(p, m, count) for p, m in zip(parts, masks_of(group))]


def total(x, groups, count):
    for g in groups:
        got = [x] + [swap(x, m, count) for m in masks_of(g)]
        while len(got) > 1:
            got = [got[k] + got[k + 1] for k in range(0, len(got), 2)]
        x = got[0]
    return x


def lay_vectors(raw, per, rowv_ref):
    unit = LANES // 2
    each = per // unit
    low = lax.broadcasted_iota(jnp.int32, (1, LANES), 1) < unit

    def half(c, high):
        owner, part = divmod(c, each)
        got = raw[owner, part // 2 : part // 2 + 1, :].astype(f32)
        return got if part % 2 == high else pltpu.roll(got, unit, 1)

    for m in range((8 * D + FF) // LANES):
        row, col = divmod(m * LANES, D)
        rowv_ref[row : row + 1, col : col + LANES] = jnp.where(low, half(2 * m, 0), half(2 * m + 1, 1))


def pad_window(rows):
    at = lax.broadcasted_iota(jnp.int32, (104, 1), 0)
    rows = jnp.where(at < CELLS, rows, 0.0)
    return jnp.concatenate([rows, jnp.zeros((LANES - 104, rows.shape[1]), f32)], axis=0).astype(bf16)


def head_lanes():
    return lax.broadcasted_iota(jnp.int32, (1, LANES), 1) // HD


def by_head(block):
    lane = head_lanes()
    return jnp.concatenate([jnp.where(lane == q, block, jnp.zeros_like(block)) for q in range(4)], axis=0)


def attn_fwd_body(me_ref, x_ref, mask_ref, bias_ref, *refs, plan, rpd, per):
    pieces = refs[: len(plan)]
    (oT_ref, o_ref, q_ref, kT_ref, v_ref, pT_ref, h1T_ref, w_ref, rowv_ref) = refs[len(plan) : len(plan) + 9]
    xs, h1p, qT, kn, vT, osc, raw, sem = refs[len(plan) + 9 :]

    @pl.when(pl.program_id(0) == 0)
    def _():
        copies = []
        for ref, rels in zip(pieces, plan):
            if rels is None:
                copies.append(pltpu.make_async_copy(ref, (w_ref, rowv_ref)[len(copies)], sem.at[len(copies)]))
                continue
            for t, r in enumerate(rels):
                at = pl.multiple_of((r ^ me_ref[0]) * rpd, rpd)
                copies.append(
                    pltpu.make_async_copy(
                        ref.at[t, :, pl.ds(0, 3 * D)], w_ref.at[pl.ds(at, rpd), :], sem.at[len(copies)]
                    )
                )
                copies.append(
                    pltpu.make_async_copy(ref.at[t, :, pl.ds(3 * D, LANES)], raw.at[r ^ me_ref[0]], sem.at[len(copies)])
                )
        for c in copies:
            c.start()
        for c in copies:
            c.wait()
        if plan[0] is not None:
            rowv_ref[12:16, :] = jnp.zeros((4, D), f32)
            lay_vectors(raw, per, rowv_ref)

    xs[0:GR, :] = x_ref[...].astype(f32)
    gain = rowv_ref[0:1, :]
    shift = rowv_ref[1:2, :]
    for w in range(GW):
        xw = xs[CELLS * w : CELLS * w + 104, :]
        c = xw - jnp.mean(xw, axis=-1, keepdims=True)
        var = jnp.mean(c * c, axis=-1, keepdims=True)
        h = pad_window(c * lax.rsqrt(var + 1e-5) * gain + shift)
        h1p[LANES * w : LANES * w + LANES, :] = h
        for a in range(D // LANES):
            h1T_ref[LANES * a : LANES * a + LANES, LANES * w : LANES * w + LANES] = h[:, LANES * a : LANES * a + LANES].T
    h1T_ref[D : D + 16, :] = jnp.ones((16, GL), bf16)
    hp = h1p[...]
    q_ref[...] = (nn(hp, w_ref[:, 0:D]) + rowv_ref[2:3, :]).astype(bf16)
    kn[...] = nn(hp, w_ref[:, D : 2 * D]).astype(bf16)
    v_ref[...] = (nn(hp, w_ref[:, 2 * D : 3 * D]) + rowv_ref[3:4, :]).astype(bf16)
    for src, dst in ((q_ref, qT), (kn, kT_ref), (v_ref, vT)):
        for w in range(GW):
            for a in range(D // LANES):
                rows, cols = slice(LANES * w, LANES * w + LANES), slice(LANES * a, LANES * a + LANES)
                dst[cols, rows] = src[rows, cols].T
    factor = HD**-0.5 * LOG2E

    def window(w, carry):
        start = pl.multiple_of(w * LANES, LANES)
        at = pl.ds(start, LANES)
        allowed = mask_ref[w]
        for g in range(4):
            cols = slice(LANES * g, LANES * g + LANES)
            s = nn(by_head(kn[pl.ds(start, KP), cols]), qT[cols, at])
            ps = []
            for q in range(4):
                h = 4 * g + q
                t = s[KP * q : KP * q + KP] * factor + bias_ref[h] + allowed
                e = jnp.exp2(t - jnp.max(t, axis=0, keepdims=True))
                p = (e * (1.0 / jnp.sum(e, axis=0, keepdims=True))).astype(bf16)
                pT_ref[w, h] = p
                ps.append(p)
            o = [nn(vT[LANES * g + HD * q : LANES * g + HD * q + HD, at][:, 0:KP], ps[q]) for q in range(4)]
            oT_ref[cols, at] = jnp.concatenate(o, axis=0).astype(bf16)
        return carry

    lax.fori_loop(0, GW, window, 0, unroll=4)
    for w in range(GW):
        for a in range(D // LANES):
            osc[CELLS * w : CELLS * w + 104, LANES * a : LANES * a + LANES] = (
                oT_ref[LANES * a : LANES * a + LANES, LANES * w : LANES * w + LANES].T[0:112].astype(f32)[0:104]
            )
    o_ref[...] = osc[0:GR, :].astype(bf16)


def any_specs(n):
    return [pl.BlockSpec(memory_space=pl.ANY)] * n


SMEM = pl.BlockSpec(memory_space=pltpu.SMEM)


def attn_fwd(me, x, allowed, bias, plan, pieces, rpd, per, count):
    n = x.shape[0] // GR
    copies = sum(1 if r is None else 2 * len(r) for r in plan)
    rb = pl.BlockSpec((GR, D), lambda i: (i, 0))
    tb = pl.BlockSpec((D, GL), lambda i: (0, i))
    pb = pl.BlockSpec((GL, D), lambda i: (i, 0))
    return pl.pallas_call(
        functools.partial(attn_fwd_body, plan=plan, rpd=rpd, per=per),
        grid=(n,),
        in_specs=[SMEM, rb, pl.BlockSpec((GW, KP, LANES), lambda i: (i, 0, 0)), whole((HEADS, KP, LANES))]
        + any_specs(len(pieces)),
        out_specs=[
            tb,
            rb,
            pb,
            tb,
            pb,
            pl.BlockSpec((GW, HEADS, KP, LANES), lambda i: (i, 0, 0, 0)),
            pl.BlockSpec((D + 16, GL), lambda i: (0, i)),
            whole((D, 3 * D)),
            whole((16, D)),
        ],
        out_shape=[
            sds((D, n * GL), bf16),
            sds((n * GR, D), bf16),
            sds((n * GL, D), bf16),
            sds((D, n * GL), bf16),
            sds((n * GL, D), bf16),
            sds((n * GW, HEADS, KP, LANES), bf16),
            sds((D + 16, n * GL), bf16),
            sds((D, 3 * D), bf16),
            sds((16, D), f32),
        ],
        scratch_shapes=[
            pltpu.VMEM((GR + 8, D), f32),
            pltpu.VMEM((GL, D), bf16),
            pltpu.VMEM((D, GL), bf16),
            pltpu.VMEM((GL, D), bf16),
            pltpu.VMEM((D, GL), bf16),
            pltpu.VMEM((GR + 8, D), f32),
            pltpu.VMEM((count, max(rpd, 16), LANES), bf16),
            pltpu.SemaphoreType.DMA((copies,)),
        ],
        compiler_params=params(60),
        cost_estimate=pl.CostEstimate(flops=10**7, bytes_accessed=10**5, transcendentals=0),
        name="attn_fwd",
    )(me, x, allowed, bias, *pieces)


def mlp_body(me_ref, vld_ref, rowv_ref, x_any, o_any, g_any, *refs, plan, rows, owners, rpd, groups):
    pieces = refs[: len(plan)]
    refs = refs[len(plan) :]
    res_any, dmid_any, p_any, first_any, second_any, vec_ref, dbf1_ref, st_ref = refs[:8]
    xb, ob, gp, gT, h2, h2T, mid, dh2, es, dus, u4, vv, pp, res, pk, sem, sem_x, sem_o, sem_p, sem_g, sem_du, sem_dv, sem_r, sem_m = refs[8:]
    j = pl.program_id(0)
    last = FF // 512 - 1
    padded = h2.shape[0]
    blocks = rows // GR
    me = me_ref[0]
    proj_bias = rowv_ref[4:5, :]
    gain = rowv_ref[5:6, :]
    shift = rowv_ref[6:7, :]

    def weights():
        first, later = [], []
        count = 0
        for ref, rels in zip(pieces, plan):
            if rels is None:
                dst = (pp, u4, vv)[count]
                (first if count == 0 else later).append(pltpu.make_async_copy(ref, dst, sem.at[count]))
                count += 1
                continue
            for t, r in enumerate(rels):
                at = pl.ds(pl.multiple_of((r ^ me) * rpd, rpd), rpd)
                first.append(pltpu.make_async_copy(ref.at[t, 0], pp.at[at, :], sem.at[count]))
                later.append(pltpu.make_async_copy(ref.at[t, pl.ds(1, 4)], u4.at[:, at, :], sem.at[count + 1]))
                to = vv.at[pl.ds(pl.multiple_of((r ^ me) * 4, 4), 4)]
                later.append(pltpu.make_async_copy(ref.at[t, pl.ds(5, 4)], to, sem.at[count + 2]))
                count += 3
        return first, later

    def rows_of(k):
        return pl.ds(k * GR, GR)

    def grads_out(j):
        if not owners:
            cols = pl.ds(pl.multiple_of(j * 512, 512), 512)
            return [
                pltpu.make_async_copy(pk.at[0], first_any.at[:, cols], sem_du.at[j, 0]),
                pltpu.make_async_copy(pk.at[1], second_any.at[cols, :], sem_du.at[j, 1]),
            ]
        at = pl.ds(pl.multiple_of(j * rpd, rpd), rpd)
        low = pl.ds(4 * rpd, 4 * rpd)
        out = []
        for c, to in enumerate((first_any, second_any)):
            out.append(pltpu.make_async_copy(pk.at[c, :, at, :], to.at[:, at, :], sem_du.at[j, c]))
            for m in range(256 // (4 * rpd)):
                pos = place_of((j * (256 // (4 * rpd)) + m) ^ (me >> 1), [tuple(b - 1 for b in g) for g in groups[1:]])
                n = 2 * m + c
                out.append(pltpu.make_async_copy(pk.at[c, pos, low, :], to.at[pos, low, :], sem_dv.at[j, n]))
        return out

    @pl.when(j == 0)
    def _():
        first, later = weights()
        ins = []
        for c in first:
            c.start()
        for k in range(blocks):
            ins.append(pltpu.make_async_copy(x_any.at[rows_of(k)], xb.at[rows_of(k)], sem_x.at[k]))
            ins.append(pltpu.make_async_copy(o_any.at[rows_of(k)], ob.at[rows_of(k)], sem_o.at[k]))
        load_g = pltpu.make_async_copy(g_any, gp.at[pl.ds(0, rows)], sem_g.at[0])
        for c in ins + [load_g] + later:
            c.start()
        h2[rows:padded, :] = jnp.zeros((padded - rows, D), bf16)
        gp[rows:padded, :] = jnp.zeros((padded - rows, D), bf16)
        dh2[...] = jnp.zeros_like(dh2)
        for c in first:
            c.wait()
        store_p = pltpu.make_async_copy(pp, p_any, sem_p.at[0])
        store_p.start()
        squares = jnp.zeros((1, D), f32)
        for k in range(blocks):
            at = slice(k * GR, k * GR + GR)
            ins[2 * k].wait()
            ins[2 * k + 1].wait()
            a = nn(ob[at, :], pp[...]) + proj_bias
            squares = squares + jnp.sum(a * a * vld_ref[at, :], axis=0, keepdims=True)
            m = xb[at, :].astype(f32) + a
            mid[at, :] = m
            c = m - jnp.mean(m, axis=-1, keepdims=True)
            var = jnp.mean(c * c, axis=-1, keepdims=True)
            h2[at, :] = (c * lax.rsqrt(var + 1e-5) * gain + shift).astype(bf16)
        st_ref[...] = jnp.zeros_like(st_ref)
        st_ref[1:2, :] = squares
        load_g.wait()

        def turn(k, carry):
            at = pl.ds(pl.multiple_of(k * LANES, LANES), LANES)
            for a in range(D // LANES):
                cols = slice(LANES * a, LANES * a + LANES)
                h2T[cols, at] = h2[at, cols].T
                gT[cols, at] = gp[at, cols].T
            return carry

        lax.fori_loop(0, padded // LANES, turn, 0)
        for c in later:
            c.wait()
        store_p.wait()

    u = nn(h2[...], u4[j]) + rowv_ref[pl.ds(8 + j, 1), :]
    de = nt(gp[...], vv[pl.ds(pl.multiple_of(32 * j, 32), 32)].reshape(512, D))
    cdf = 0.5 * lax.erf(u * RT2) + 0.5
    es[j] = (u * cdf).astype(bf16)
    du = de * (cdf + u * (PHI * jnp.exp2(u * u * (-0.5 * LOG2E))))
    dus[...] = du.astype(bf16)
    dbf1_ref[pl.ds(j, 1), :] = jnp.sum(du, axis=0, keepdims=True)
    dh2[...] += nt(dus[...], u4[j])
    dU = nn(h2T[...], dus[...]).astype(bf16)
    dV = nn(gT[...], es[j]).astype(bf16).T
    if owners:
        at = pl.ds(pl.multiple_of(j * rpd, rpd), rpd)
        for k in range(owners):
            pk[(k ^ me) & 1, place_of(k ^ me, groups[1:]), at, :] = dU[rpd * k : rpd * k + rpd]
        per = 512 // (4 * rpd)
        for k in range(per):
            rel = (j * per + k) ^ me
            pk[rel & 1, place_of(rel, groups[1:]), 4 * rpd : 8 * rpd, :] = dV[4 * rpd * k : 4 * rpd * k + 4 * rpd]
        for c in grads_out(j):
            c.start()
    else:
        pk[0] = dU
        pk[1] = dV
        for c in grads_out(j):
            c.start()
        for c in grads_out(j):
            c.wait()

    @pl.when(j == last)
    def _():
        zero = jnp.zeros((1, D), f32)
        sums = [zero] * 4
        stats = [zero] * 5
        outs = []
        for k in range(blocks):
            at = slice(k * GR, k * GR + GR)
            m = mid[at, :]
            c = m - jnp.mean(m, axis=-1, keepdims=True)
            rs = lax.rsqrt(jnp.mean(c * c, axis=-1, keepdims=True) + 1e-5)
            xh = c * rs
            d = dh2[at, :]
            dx = d * gain
            dxx = d * xh
            m1 = jnp.mean(dx, axis=-1, keepdims=True)
            m2 = jnp.mean(dxx * gain, axis=-1, keepdims=True)
            grad = gp[at, :].astype(f32)
            dm = grad + (dx - m1 - xh * m2) * rs
            dh2[at, :] = dm
            outs.append(pltpu.make_async_copy(dh2.at[rows_of(k)], dmid_any.at[rows_of(k)], sem_m.at[k]))
            outs[-1].start()
            terms = (dm.astype(bf16).astype(f32), dxx, d, grad)
            sums = [a + jnp.sum(t, axis=0, keepdims=True) for a, t in zip(sums, terms)]
            f = rowv_ref[7:8, :]
            for b in range(4):
                f = f + nn(es[b, at, :], vv[32 * b : 32 * b + 32].reshape(512, D))
            out = m + f
            res[at, :] = out.astype(bf16)
            outs.append(pltpu.make_async_copy(res.at[rows_of(k)], res_any.at[rows_of(k)], sem_r.at[k]))
            outs[-1].start()
            vl = vld_ref[at, :]
            x = xb[at, :].astype(f32)
            terms = (x * x * vl, m * m * vl, f * f * vl, out * out * vl, jnp.broadcast_to(vl, (GR, D)))
            stats = [a + jnp.sum(t, axis=0, keepdims=True) for a, t in zip(stats, terms)]
        for q in range(4):
            vec_ref[q : q + 1, :] = sums[q]
        vec_ref[4:8, :] = jnp.zeros((4, D), f32)
        dbf1_ref[4:8, :] = jnp.zeros((4, D), f32)
        for q, t in zip((0, 2, 3, 4, 5), stats):
            st_ref[q : q + 1, :] = t
        if owners:
            for step in range(last + 1):
                outs += grads_out(step)
        for c in outs:
            c.wait()


def mlp(me, x, o, g, vld, rowv, plan, pieces, rpd, owners, count, groups):
    rows = x.shape[0]
    blocks = rows // GR
    steps = FF // 512
    padded = -(-rows // LANES) * LANES
    copies = sum(1 if r is None else 3 * len(r) for r in plan)
    if owners:
        grad_shapes = [sds((count // 2, 8 * rpd, 512), bf16)] * 2
        pk = (2, count // 2, 8 * rpd, 512)
    else:
        grad_shapes = [sds((D, FF), bf16), sds((FF, D), bf16)]
        pk = (2, 512, 512)
    dma = pltpu.SemaphoreType.DMA
    return pl.pallas_call(
        functools.partial(mlp_body, plan=plan, rows=rows, owners=count if owners else 0, rpd=rpd, groups=groups),
        grid=(steps,),
        in_specs=[SMEM, whole((rows, 1)), whole((16, D))] + any_specs(3 + len(pieces)),
        out_specs=any_specs(5) + [whole((8, D))] * 3,
        out_shape=[sds((rows, D), bf16), sds((rows, D), f32), sds((D, D), bf16)] + grad_shapes + [sds((8, D), f32)] * 3,
        scratch_shapes=[
            pltpu.VMEM((rows, D), bf16),
            pltpu.VMEM((rows, D), bf16),
            pltpu.VMEM((padded, D), bf16),
            pltpu.VMEM((D, padded), bf16),
            pltpu.VMEM((padded, D), bf16),
            pltpu.VMEM((D, padded), bf16),
            pltpu.VMEM((rows, D), f32),
            pltpu.VMEM((padded, D), f32),
            pltpu.VMEM((steps, padded, 512), bf16),
            pltpu.VMEM((padded, 512), bf16),
            pltpu.VMEM((steps, D, 512), bf16),
            pltpu.VMEM((FF // 16, 16, D), bf16),
            pltpu.VMEM((D, D), bf16),
            pltpu.VMEM((rows, D), bf16),
            pltpu.VMEM(pk, bf16),
            dma((copies,)),
            dma((blocks,)),
            dma((blocks,)),
            dma((1,)),
            dma((1,)),
            dma((steps, 2)),
            dma((steps, max(1, 512 // (4 * rpd)))),
            dma((blocks,)),
            dma((blocks,)),
        ],
        compiler_params=params(62),
        cost_estimate=pl.CostEstimate(flops=10**7, bytes_accessed=10**5, transcendentals=0),
        name="mlp",
    )(me, vld, rowv, x, o, g, *pieces)


def attn_bwd_body(me_ref, dmid_ref, p_ref, oT_ref, q_ref, kT_ref, v_ref, pT_ref, h1T_ref, *refs, owners, rpd, groups):
    dm_ref, acc_ref, vec_ref = refs[:3]
    grads = refs[3:-6]
    xs, dap, don, doT, dw, dproj = refs[-6:]
    i = pl.program_id(0)

    @pl.when(i == 0)
    def _():
        acc_ref[...] = jnp.zeros_like(acc_ref)
        dw[...] = jnp.zeros_like(dw)
        dproj[...] = jnp.zeros_like(dproj)

    xs[0:GR, :] = dmid_ref[...]
    for w in range(GW):
        dap[LANES * w : LANES * w + LANES, :] = pad_window(xs[CELLS * w : CELLS * w + 104, :])
        dm_ref[LANES * w + KP : LANES * w + LANES, :] = jnp.zeros((LANES - KP, 3 * D), bf16)
    da = dap[...]
    don[...] = nt(da, p_ref[...]).astype(bf16)
    dproj[...] += nn(oT_ref[...], da)
    for w in range(GW):
        for a in range(D // LANES):
            rows, cols = slice(LANES * w, LANES * w + LANES), slice(LANES * a, LANES * a + LANES)
            doT[cols, rows] = don[rows, cols].T
    factor = HD**-0.5

    def window(w, carry):
        start = pl.multiple_of(w * LANES, LANES)
        at = pl.ds(start, LANES)
        keys = pl.ds(start, KP)
        for g in range(4):
            c0 = LANES * g
            cols = slice(c0, c0 + LANES)
            dp = nn(by_head(v_ref[keys, cols]), doT[cols, at])
            dss = []
            for q in range(4):
                h = 4 * g + q
                head = slice(HD * h, HD * h + HD)
                delta = jnp.sum(doT[head, at].astype(f32) * oT_ref[head, at].astype(f32), axis=0, keepdims=True)
                ds = pT_ref[w, h].astype(f32) * (dp[KP * q : KP * q + KP] - delta)
                acc_ref[h] += ds
                dss.append(ds.astype(bf16))
            dq = [nn(kT_ref[c0 + HD * q : c0 + HD * q + HD, at][:, 0:KP], dss[q]) for q in range(4)]
            dm_ref[at, cols] = (jnp.concatenate(dq, axis=0) * factor).astype(bf16).T
            dk = nn(jnp.concatenate(dss, axis=1), by_head(q_ref[at, cols])) * factor
            dm_ref[keys, D + c0 : D + c0 + LANES] = dk.astype(bf16)
            dv = nn(jnp.concatenate([pT_ref[w, 4 * g + q] for q in range(4)], axis=1), by_head(don[at, cols]))
            dm_ref[keys, 2 * D + c0 : 2 * D + c0 + LANES] = dv.astype(bf16)
        return carry

    lax.fori_loop(0, GW, window, 0, unroll=4)
    dw[...] += nn(h1T_ref[...], dm_ref[...])

    @pl.when(i == pl.num_programs(0) - 1)
    def _():
        if owners:
            me = me_ref[0]

            def store(flip):
                for k in range(owners):
                    to = grads[(k ^ flip) & 1]
                    pos = place_of(k ^ me, groups[1:])
                    for q in range(3):
                        to[pos, rpd * q : rpd * q + rpd, :] = dw[rpd * k : rpd * k + rpd, D * q : D * q + D].astype(bf16)
                    to[pos, 3 * rpd : 4 * rpd, :] = dproj[rpd * k : rpd * k + rpd, :].astype(bf16)

            pl.when(me & 1 == 0)(lambda: store(0))
            pl.when(me & 1 == 1)(lambda: store(1))
        else:
            grads[0][...] = dw[0:D, :].astype(bf16)
            grads[1][...] = dproj[...].astype(bf16)
        vec_ref[...] = dw[D : D + 8, :]


def attn_bwd(me, dmid, p, oT, q, kT, v, pT, h1T, rpd, owners, count, groups):
    n = dmid.shape[0] // GR

    def tb(r):
        return pl.BlockSpec((r, GL), lambda i: (0, i))

    pb = pl.BlockSpec((GL, D), lambda i: (i, 0))
    if owners:
        grad_shapes = [sds((count // 2, 4 * rpd, D), bf16)] * 2
    else:
        grad_shapes = [sds((D, 3 * D), bf16), sds((D, D), bf16)]
    return pl.pallas_call(
        functools.partial(attn_bwd_body, owners=count if owners else 0, rpd=rpd, groups=groups),
        grid=(n,),
        in_specs=[SMEM, pl.BlockSpec((GR, D), lambda i: (i, 0)), whole((D, D)), tb(D), pb, tb(D), pb, pl.BlockSpec((GW, HEADS, KP, LANES), lambda i: (i, 0, 0, 0)), tb(D + 16)],
        out_specs=[pl.BlockSpec((GL, 3 * D), lambda i: (i, 0)), whole((HEADS, KP, LANES)), whole((8, 3 * D))] + [whole(s.shape) for s in grad_shapes],
        out_shape=[sds((n * GL, 3 * D), bf16), sds((HEADS, KP, LANES), f32), sds((8, 3 * D), f32)] + grad_shapes,
        scratch_shapes=[
            pltpu.VMEM((GR + 8, D), f32),
            pltpu.VMEM((GL, D), bf16),
            pltpu.VMEM((GL, D), bf16),
            pltpu.VMEM((D, GL), bf16),
            pltpu.VMEM((D + 16, 3 * D), f32),
            pltpu.VMEM((D, D), f32),
        ],
        compiler_params=params(60),
        cost_estimate=pl.CostEstimate(flops=10**7, bytes_accessed=10**5, transcendentals=0),
        name="attn_bwd",
    )(me, dmid, p, oT, q, kT, v, pT, h1T)


def grad_in_body(dm_ref, w_ref, x_ref, dmid_ref, rowv_ref, tg_ref, vec_ref, dsc):
    dh = nt(dm_ref[...], w_ref[...])
    for w in range(GW):
        dsc[CELLS * w : CELLS * w + 104, :] = dh[LANES * w : LANES * w + 104]
    d = dsc[0:GR, :]
    x = x_ref[...].astype(f32)
    c = x - jnp.mean(x, axis=-1, keepdims=True)
    rs = lax.rsqrt(jnp.mean(c * c, axis=-1, keepdims=True) + 1e-5)
    xh = c * rs
    gain = rowv_ref[0:1, :]
    dx = d * gain
    dxx = d * xh
    m1 = jnp.mean(dx, axis=-1, keepdims=True)
    m2 = jnp.mean(dxx * gain, axis=-1, keepdims=True)
    tg_ref[...] = dmid_ref[...] + (dx - m1 - xh * m2) * rs

    @pl.when(pl.program_id(0) == 0)
    def _():
        vec_ref[...] = jnp.zeros_like(vec_ref)

    vec_ref[0:1, :] += jnp.sum(dxx, axis=0, keepdims=True)
    vec_ref[1:2, :] += jnp.sum(d, axis=0, keepdims=True)


def grad_in(dm, w, x, dmid, rowv):
    n = x.shape[0] // GR
    rb = pl.BlockSpec((GR, D), lambda i: (i, 0))
    return pl.pallas_call(
        grad_in_body,
        grid=(n,),
        in_specs=[pl.BlockSpec((GL, 3 * D), lambda i: (i, 0)), whole((D, 3 * D)), rb, rb, whole((16, D))],
        out_specs=[rb, whole((8, D))],
        out_shape=[sds((n * GR, D), f32), sds((8, D), f32)],
        scratch_shapes=[pltpu.VMEM((GR + 8, D), f32)],
        compiler_params=params(60),
        cost_estimate=pl.CostEstimate(flops=10**7, bytes_accessed=10**5, transcendentals=0),
        name="grad_in",
    )(dm, w, x, dmid, rowv)


def place_hits(shape, axis, rev=0):
    c = lax.broadcasted_iota(jnp.int32, shape, 1 - axis)
    code = jnp.where(c < CELLS, (2 * WSIDE - 1) * (c // WSIDE) + c % WSIDE, -1000)
    if rev:
        code = rev - code
    return jnp.where(code == lax.broadcasted_iota(jnp.int32, shape, axis), 1.0, 0.0).astype(bf16)


def rel_bias_body(t_ref, o_ref):
    keys = place_hits((KP, 192), 1)
    queries = place_hits((256, LANES), 0)

    def head(h, carry):
        row = pltpu.roll(jnp.broadcast_to(t_ref[pl.ds(h, 1), :], (8, RP)), 0, 1, stride=1, stride_axis=0)
        t = jnp.concatenate([pltpu.roll(row, (8 * k - 180) % RP, 1)[:, 0:256] for k in range(24)], axis=0)
        hi = t.astype(bf16)
        r = t - hi.astype(f32)
        md = r.astype(bf16)
        lo = (r - md.astype(f32)).astype(bf16)
        o_ref[h] = sum(nn(nn(keys, part).astype(bf16), queries) for part in (lo, md, hi))
        return carry

    lax.fori_loop(0, HEADS, head, 0, unroll=8)


def rel_bias(table):
    return pl.pallas_call(
        rel_bias_body,
        out_shape=sds((HEADS, KP, LANES), f32),
        compiler_params=params(60),
        cost_estimate=pl.CostEstimate(flops=10**7, bytes_accessed=10**5, transcendentals=0),
        name="rel_bias",
    )(table)


def rel_grad_body(a_ref, o_ref):
    keys = place_hits((192, KP), 0, 191)
    queries = place_hits((LANES, 256), 1)
    zero = jnp.zeros((8, RP - 256), f32)

    def head(h, carry):
        a = a_ref[h]
        hi = a.astype(bf16)
        lo = (a - hi.astype(f32)).astype(bf16)
        b = nn(nn(keys, hi).astype(bf16), queries) + nn(nn(keys, lo).astype(bf16), queries)
        t = jnp.zeros((8, RP), f32)
        for k in range(24):
            t = t + pltpu.roll(jnp.concatenate([b[8 * k : 8 * k + 8], zero], axis=1), (8 * k - 11) % RP, 1)
        t = pltpu.roll(t, 0, 1, stride=1, stride_axis=0)
        o_ref[pl.ds(h, 1), :] = jnp.sum(t, axis=0, keepdims=True)
        return carry

    lax.fori_loop(0, HEADS, head, 0, unroll=8)


def rel_grad(acc):
    return pl.pallas_call(
        rel_grad_body,
        out_shape=sds((HEADS, RP), f32),
        compiler_params=params(60),
        cost_estimate=pl.CostEstimate(flops=10**7, bytes_accessed=10**5, transcendentals=0),
        name="rel_grad",
    )(acc)


def shards(tokens, cotangent, regions, validity, qkv_weight, proj_weight, fc1_weight, fc2_weight, vectors, rel_table, *, count, inner):
    rows = tokens.shape[0]
    windows = rows // CELLS
    groups = bit_groups(count)
    rpd = D // count
    direct = rpd % 16 == 0
    me = lax.axis_index("dp") * inner + lax.axis_index("shard")
    me_s = me.astype(jnp.int32).reshape(1)

    per = vectors.shape[0]
    if direct:
        own = jnp.pad(vectors, (0, rpd * LANES - per)).reshape(rpd, LANES)
        own = jnp.concatenate([qkv_weight.reshape(rpd, 3 * D), own], axis=1)
    else:
        own = jnp.concatenate([qkv_weight, vectors]).reshape(1, -1)
    rels, attn_up = gather_upper(own, groups, count)
    packed = jnp.concatenate(
        [
            proj_weight.reshape(1, rpd, D),
            fc1_weight.reshape(rpd, 4, 512).transpose(1, 0, 2),
            fc2_weight.reshape(4, rpd, D),
        ],
        axis=0,
    )
    packed, table_in, valid_in = after((packed.reshape(9 * rpd, D), rel_table, validity), attn_up)
    attn_pieces = gather_plane(rels, attn_up, groups, count)
    _, mlp_up = gather_upper(packed, groups, count)

    bias = rel_bias(jnp.pad(table_in.T * LOG2E, ((0, 0), (0, RP - RELN))))
    reg = regions.reshape(windows, CELLS)
    val = valid_in.reshape(windows, CELLS)
    allowed = (reg[:, :, None] == reg[:, None, :]) & (val[:, :, None] == 1)
    allowed = jnp.where(allowed | jnp.eye(CELLS, dtype=jnp.bool_)[None], 0.0, NEG).astype(f32)
    allowed = jnp.pad(allowed, ((0, 0), (0, KP - CELLS), (0, LANES - CELLS)), constant_values=NEG)
    vld = valid_in.astype(f32).reshape(rows, 1)

    held, mlp_up = after(([a for _, a in attn_pieces], mlp_up), bias, allowed, vld)
    mlp_up = after(mlp_up, held)
    attn_pieces = gather_core([(r, a) for (r, _), a in zip(attn_pieces, held)], count)
    mlp_pieces = gather_plane(rels, mlp_up, groups, count)
    if direct:
        attn_plan = [r for r, _ in attn_pieces]
        attn_w = [a for _, a in attn_pieces]
    else:
        attn_plan = [None] * 2
        both = natural_order(attn_pieces, me, count).reshape(count, -1)
        attn_w = [both[:, : 3 * D * rpd].reshape(D, 3 * D), jnp.pad(both[:, 3 * D * rpd :].astype(f32).reshape(12, D), ((0, 4), (0, 0)))]

    x = after(tokens, mlp_up, vld)
    oT, o, q, kT, v, pT, h1T, w_full, rowv = attn_fwd(me_s, x, allowed, bias, attn_plan, attn_w, rpd, per, count)

    held = after([a for _, a in mlp_pieces], o)
    mlp_pieces = gather_core([(r, a) for (r, _), a in zip(mlp_pieces, held)], count)
    if direct:
        mlp_plan = [r for r, _ in mlp_pieces]
        mlp_w = [a.reshape(-1, 9, rpd, D) for _, a in mlp_pieces]
    else:
        both = natural_order(mlp_pieces, me, count).reshape(count, 9, rpd, D)
        mlp_plan = [None] * 3
        mlp_w = [both[:, 0].reshape(D, D), both[:, 1:5].transpose(1, 0, 2, 3).reshape(4, D, 512), both[:, 5:].reshape(128, 16, D)]
    result, dmid, p_full, mlp_keep, mlp_send, vec_two, dbf1, squares = mlp(
        me_s, tokens, o, cotangent, vld, rowv, mlp_plan, mlp_w, rpd, direct, count, groups
    )
    order = None
    if not direct:
        blocks = jnp.arange(count)
        where = place_of(blocks, groups)
        order = jnp.zeros((count,), jnp.int32).at[where].set(blocks.astype(jnp.int32)) ^ me
        dU = mlp_keep.reshape(count, rpd, 4, 512).transpose(0, 2, 1, 3).reshape(count, 4 * rpd, 512)
        pk = jnp.take(jnp.concatenate([dU, mlp_send.reshape(count, 4 * rpd, D)], axis=1), order, axis=0)
        mlp_keep, mlp_send = pk[: count // 2], pk[count // 2 :]

    other = swap(mlp_send, 1, count)
    mlp_own, parts = split_sum([mlp_keep, other], groups[1])
    mlp_got = send_parts(parts, groups[1], count)
    dmid = after(dmid, parts)
    got = attn_bwd(me_s, dmid, p_full, oT, q, kT, v, pT, h1T, rpd, direct, count, groups)
    dm, score_sums, vec_one = got[:3]
    if direct:
        attn_keep, attn_send = got[3:]
    else:
        dW = got[3].reshape(count, rpd, 3, D).transpose(0, 2, 1, 3).reshape(count, 3 * rpd, D)
        pk = jnp.take(jnp.concatenate([dW, got[4].reshape(count, rpd, D)], axis=1), order, axis=0)
        attn_keep, attn_send = pk[: count // 2], pk[count // 2 :]
    mlp_got, attn_send, score_sums, dm = lax.optimization_barrier((mlp_got, attn_send, score_sums, dm))
    other = swap(attn_send, 1, count)
    attn_own, parts = split_sum([attn_keep, other], groups[1])
    attn_got = send_parts(parts, groups[1], count)
    mlp_terms = [mlp_own] + mlp_got
    dm = after(dm, parts)
    grad_tokens, vec_in = grad_in(dm, w_full, tokens, dmid, rowv)
    table = rel_grad(after(score_sums, parts))
    attn_terms = [attn_own] + after(attn_got, grad_tokens)
    for g in groups[2:]:
        mlp_own, parts = split_sum(mlp_terms, g)
        mlp_terms = [mlp_own] + send_parts(parts, g, count)
        attn_own, parts = split_sum(attn_terms, g)
        attn_terms = [attn_own] + send_parts(parts, g, count)
    mlp_sum = sum(t[0].astype(f32) for t in mlp_terms)
    attn_sum = sum(t[0].astype(f32) for t in attn_terms)
    small = jnp.concatenate(
        [
            vec_in[0:2],
            vec_one[0:1, 0:D],
            vec_one[0:1, 2 * D : 3 * D],
            vec_two[0:4],
            dbf1[0:4],
            table.reshape(-1, D),
            squares,
        ],
        axis=0,
    )
    small = total(small, groups, count)
    length = vectors.shape[0]
    grad_vectors = lax.dynamic_slice(small[:12].reshape(-1), (me * length,), (length,))
    grad_table = small[12:24].reshape(HEADS, RP)[:, :RELN].T
    sums = jnp.sum(small[24:32], axis=1)
    stats = jnp.sqrt(sums[0:5] / sums[5] + 1e-06)
    return (
        result,
        grad_tokens,
        attn_sum[: 3 * rpd].reshape(3, rpd, D).transpose(1, 0, 2).reshape(-1),
        attn_sum[3 * rpd :].reshape(-1),
        mlp_sum[: 4 * rpd].reshape(4, rpd, 512).transpose(1, 0, 2).reshape(-1),
        mlp_sum[4 * rpd :].reshape(-1),
        grad_vectors,
        grad_table,
        stats,
    )


def solution(mesh):
    flat = P(AXES)
    tall = P(AXES, None)
    in_specs = (tall, tall, flat, flat, flat, flat, flat, flat, flat, P())
    out_specs = (tall, tall, flat, flat, flat, flat, flat, P(), P())
    inner = mesh.shape["shard"]
    body = functools.partial(shards, count=mesh.shape["dp"] * inner, inner=inner)
    return jax.shard_map(body, mesh=mesh, in_specs=in_specs, out_specs=out_specs, check_vma=False)
```

```python
import functools

import jax
import jax.numpy as jnp
from jax import lax
from jax.experimental import pallas as pl
from jax.experimental.pallas import tpu as pltpu
from jax.sharding import PartitionSpec as P

D = 512
FF = 2048
HEADS = 16
HD = 32
WSIDE = 10
RELN = 361
CELLS = WSIDE * WSIDE
GW = 4
GR = GW * CELLS
KP = 112
LANES = 128
GL = GW * LANES
RP = 384
AXES = ("dp", "shard")
LOG2E = 1.4426950408889634
NEG = -1e9
RT2 = 0.7071067811865476
PHI = 0.3989422804014327
f32 = jnp.float32
bf16 = jnp.bfloat16
sds = jax.ShapeDtypeStruct


def nn(a, b):
    return lax.dot_general(a, b, (((1,), (0,)), ((), ())), preferred_element_type=f32)


def nt(a, b):
    return lax.dot_general(a, b, (((1,), (1,)), ((), ())), preferred_element_type=f32)


def whole(shape):
    return pl.BlockSpec(shape, lambda i: (0,) * len(shape))


def params(mib):
    return pltpu.CompilerParams(vmem_limit_bytes=mib * 2**20)


def bit_groups(count):
    bits = count.bit_length() - 1
    groups = [(0,)]
    at = 1
    while at < bits:
        groups.append(tuple(range(at, min(at + 2, bits))))
        at += 2
    return groups


def masks_of(group):
    return [sum(((v >> k) & 1) << b for k, b in enumerate(group)) for v in range(1, 1 << len(group))]


def swap(x, mask, count):
    return lax.ppermute(x, AXES, [(i, i ^ mask) for i in range(count)])


def place_of(rel, groups):
    pos = 0
    for g in groups:
        pos = pos * (1 << len(g)) + ((rel >> g[0]) & ((1 << len(g)) - 1))
    return pos


def after(values, *others):
    return lax.optimization_barrier((values, others))[0]


def gather_upper(x, groups, count, *others):
    cur = x[None]
    rels = [0]
    for k, g in enumerate(groups[:1:-1]):
        if k and others:
            cur = after(cur, *others)
        ms = masks_of(g)
        cur = jnp.concatenate([cur] + [swap(cur, m, count) for m in ms], axis=0)
        rels = [r ^ m for m in [0] + ms for r in rels]
    return rels, cur


def gather_plane(rels, cur, groups, count):
    return [(rels, cur)] + [([r ^ m for r in rels], swap(cur, m, count)) for m in masks_of(groups[1])]


def gather_core(pieces, count):
    return pieces + [([r ^ 1 for r in rels], swap(arr, 1, count)) for rels, arr in pieces]


def natural_order(pieces, me, count):
    rels = [r for rs, _ in pieces for r in rs]
    where = [0] * count
    for k, r in enumerate(rels):
        where[r] = k
    both = jnp.concatenate([a for _, a in pieces], axis=0)
    return jnp.take(both, jnp.asarray(where, jnp.int32)[jnp.arange(count) ^ me], axis=0)


def split_sum(terms, group):
    n = terms[0].shape[0] >> len(group)
    parts = [sum(t[k * n : (k + 1) * n].astype(f32) for t in terms) for k in range(1 << len(group))]
    return parts[0], [p.astype(bf16) for p in parts[1:]]


def send_parts(parts, group, count):
    return [swap(p, m, count) for p, m in zip(parts, masks_of(group))]


def lay_vectors(raw, per, rowv_ref):
    unit = LANES // 2
    each = per // unit
    low = lax.broadcasted_iota(jnp.int32, (1, LANES), 1) < unit

    def half(c, high):
        owner, part = divmod(c, each)
        got = raw[owner, part // 2 : part // 2 + 1, :].astype(f32)
        return got if part % 2 == high else pltpu.roll(got, unit, 1)

    for m in range((8 * D + FF) // LANES):
        row, col = divmod(m * LANES, D)
        rowv_ref[row : row + 1, col : col + LANES] = jnp.where(low, half(2 * m, 0), half(2 * m + 1, 1))


def pad_window(rows):
    at = lax.broadcasted_iota(jnp.int32, (104, 1), 0)
    rows = jnp.where(at < CELLS, rows, 0.0)
    return jnp.concatenate([rows, jnp.zeros((LANES - 104, rows.shape[1]), f32)], axis=0).astype(bf16)


def head_lanes():
    return lax.broadcasted_iota(jnp.int32, (1, LANES), 1) // HD


def by_head(block):
    lane = head_lanes()
    return jnp.concatenate([jnp.where(lane == q, block, jnp.zeros_like(block)) for q in range(4)], axis=0)


def attn_fwd_body(me_ref, x_ref, code_ref, bias_ref, *refs, plan, rpd, per):
    pieces = refs[: len(plan)]
    (oT_ref, o_ref, q_ref, kT_ref, v_ref, pT_ref, xT_ref, vld_ref, w_ref, rowv_ref) = refs[len(plan) : len(plan) + 10]
    xs, h1p, qT, kn, vT, osc, vsc, mask_ref, raw, sem = refs[len(plan) + 10 :]

    @pl.when(pl.program_id(0) == 0)
    def _():
        copies = []
        for ref, rels in zip(pieces, plan):
            if rels is None:
                copies.append(pltpu.make_async_copy(ref, (w_ref, rowv_ref)[len(copies)], sem.at[len(copies)]))
                continue
            for t, r in enumerate(rels):
                at = pl.multiple_of((r ^ me_ref[0]) * rpd, rpd)
                copies.append(
                    pltpu.make_async_copy(
                        ref.at[t, :, pl.ds(0, 3 * D)], w_ref.at[pl.ds(at, rpd), :], sem.at[len(copies)]
                    )
                )
                copies.append(
                    pltpu.make_async_copy(ref.at[t, :, pl.ds(3 * D, LANES)], raw.at[r ^ me_ref[0]], sem.at[len(copies)])
                )
        for c in copies:
            c.start()
        for c in copies:
            c.wait()
        if plan[0] is not None:
            rowv_ref[12:16, :] = jnp.zeros((4, D), f32)
            lay_vectors(raw, per, rowv_ref)

    xs[0:GR, :] = x_ref[...].astype(f32)
    gain = rowv_ref[0:1, :]
    shift = rowv_ref[1:2, :]
    for w in range(GW):
        xw = xs[CELLS * w : CELLS * w + 104, :]
        c = xw - jnp.mean(xw, axis=-1, keepdims=True)
        var = jnp.mean(c * c, axis=-1, keepdims=True)
        xh = c * lax.rsqrt(var + 1e-5)
        h1p[LANES * w : LANES * w + LANES, :] = pad_window(xh * gain + shift)
        xh = pad_window(xh)
        for a in range(D // LANES):
            xT_ref[LANES * a : LANES * a + LANES, LANES * w : LANES * w + LANES] = xh[:, LANES * a : LANES * a + LANES].T
    xT_ref[D : D + 16, :] = jnp.ones((16, GL), bf16)
    turned = code_ref[0].T
    keys = lax.broadcasted_iota(jnp.int32, (KP, LANES), 0)
    same = (keys == lax.broadcasted_iota(jnp.int32, (KP, LANES), 1)) & (keys < CELLS)
    for w in range(GW):
        of_key = turned[:, GW + w : GW + w + 1]
        equal = jnp.broadcast_to(of_key[0:KP], (KP, LANES)) == jnp.broadcast_to(code_ref[0, w : w + 1, :], (KP, LANES))
        mask_ref[w] = jnp.where(equal | same, 0.0, NEG)
        vsc[CELLS * w : CELLS * w + 104, :] = jnp.broadcast_to(jnp.where(of_key[0:104] >= 0.0, 1.0, 0.0), (104, LANES))
    vld_ref[...] = vsc[0:GR, :]
    hp = h1p[...]
    q_ref[...] = (nn(hp, w_ref[:, 0:D]) + rowv_ref[2:3, :]).astype(bf16)
    kn[...] = nn(hp, w_ref[:, D : 2 * D]).astype(bf16)
    v_ref[...] = (nn(hp, w_ref[:, 2 * D : 3 * D]) + rowv_ref[3:4, :]).astype(bf16)
    for src, dst in ((q_ref, qT), (kn, kT_ref), (v_ref, vT)):
        for w in range(GW):
            for a in range(D // LANES):
                rows, cols = slice(LANES * w, LANES * w + LANES), slice(LANES * a, LANES * a + LANES)
                dst[cols, rows] = src[rows, cols].T
    factor = HD**-0.5 * LOG2E

    def window(w, carry):
        start = pl.multiple_of(w * LANES, LANES)
        at = pl.ds(start, LANES)
        allowed = mask_ref[w]
        for g in range(4):
            cols = slice(LANES * g, LANES * g + LANES)
            s = nn(by_head(kn[pl.ds(start, KP), cols]), qT[cols, at])
            ps = []
            for q in range(4):
                h = 4 * g + q
                t = s[KP * q : KP * q + KP] * factor + bias_ref[h] + allowed
                e = jnp.exp2(t - jnp.max(t, axis=0, keepdims=True))
                p = (e * (1.0 / jnp.sum(e, axis=0, keepdims=True))).astype(bf16)
                pT_ref[w, h] = p
                ps.append(p)
            o = [nn(vT[LANES * g + HD * q : LANES * g + HD * q + HD, at][:, 0:KP], ps[q]) for q in range(4)]
            oT_ref[cols, at] = jnp.concatenate(o, axis=0).astype(bf16)
        return carry

    lax.fori_loop(0, GW, window, 0, unroll=4)
    for w in range(GW):
        for a in range(D // LANES):
            osc[CELLS * w : CELLS * w + 104, LANES * a : LANES * a + LANES] = (
                oT_ref[LANES * a : LANES * a + LANES, LANES * w : LANES * w + LANES].T[0:112].astype(f32)[0:104]
            )
    o_ref[...] = osc[0:GR, :].astype(bf16)


def any_specs(n):
    return [pl.BlockSpec(memory_space=pl.ANY)] * n


SMEM = pl.BlockSpec(memory_space=pltpu.SMEM)


def attn_fwd(me, x, codes, bias, plan, pieces, rpd, per, count):
    n = x.shape[0] // GR
    copies = sum(1 if r is None else 2 * len(r) for r in plan)
    rb = pl.BlockSpec((GR, D), lambda i: (i, 0))
    tb = pl.BlockSpec((D, GL), lambda i: (0, i))
    pb = pl.BlockSpec((GL, D), lambda i: (i, 0))
    return pl.pallas_call(
        functools.partial(attn_fwd_body, plan=plan, rpd=rpd, per=per),
        grid=(n,),
        in_specs=[SMEM, rb, pl.BlockSpec((1, 2 * GW, LANES), lambda i: (i, 0, 0)), whole((HEADS, KP, LANES))]
        + any_specs(len(pieces)),
        out_specs=[
            tb,
            rb,
            pb,
            tb,
            pb,
            pl.BlockSpec((GW, HEADS, KP, LANES), lambda i: (i, 0, 0, 0)),
            pl.BlockSpec((D + 16, GL), lambda i: (0, i)),
            pl.BlockSpec((GR, LANES), lambda i: (i, 0)),
            whole((D, 3 * D)),
            whole((16, D)),
        ],
        out_shape=[
            sds((D, n * GL), bf16),
            sds((n * GR, D), bf16),
            sds((n * GL, D), bf16),
            sds((D, n * GL), bf16),
            sds((n * GL, D), bf16),
            sds((n * GW, HEADS, KP, LANES), bf16),
            sds((D + 16, n * GL), bf16),
            sds((n * GR, LANES), f32),
            sds((D, 3 * D), bf16),
            sds((16, D), f32),
        ],
        scratch_shapes=[
            pltpu.VMEM((GR + 8, D), f32),
            pltpu.VMEM((GL, D), bf16),
            pltpu.VMEM((D, GL), bf16),
            pltpu.VMEM((GL, D), bf16),
            pltpu.VMEM((D, GL), bf16),
            pltpu.VMEM((GR + 8, D), f32),
            pltpu.VMEM((GR + 8, LANES), f32),
            pltpu.VMEM((GW, KP, LANES), f32),
            pltpu.VMEM((count, max(rpd, 16), LANES), bf16),
            pltpu.SemaphoreType.DMA((copies,)),
        ],
        compiler_params=params(60),
        cost_estimate=pl.CostEstimate(flops=10**7, bytes_accessed=10**5, transcendentals=0),
        name="attn_fwd",
    )(me, x, codes, bias, *pieces)


def mlp_body(me_ref, vld_ref, rowv_ref, x_any, o_any, g_any, *refs, plan, rows, owners, rpd, groups):
    pieces = refs[: len(plan)]
    refs = refs[len(plan) :]
    res_any, dmid_any, p_any, first_any, second_any, vec_ref, dbf1_ref, st_ref = refs[:8]
    xb, ob, gp, gT, h2, h2T, mid, dh2, es, dus, u4, vv, pp, res, pk, sem, sem_x, sem_o, sem_p, sem_g, sem_du, sem_dv, sem_r, sem_m = refs[8:]
    j = pl.program_id(0)
    last = FF // 512 - 1
    padded = h2.shape[0]
    blocks = rows // GR
    me = me_ref[0]
    proj_bias = rowv_ref[4:5, :]
    gain = rowv_ref[5:6, :]
    shift = rowv_ref[6:7, :]

    def weights():
        first, later = [], []
        count = 0
        for ref, rels in zip(pieces, plan):
            if rels is None:
                dst = (pp, u4, vv)[count]
                (first if count == 0 else later).append(pltpu.make_async_copy(ref, dst, sem.at[count]))
                count += 1
                continue
            for t, r in enumerate(rels):
                at = pl.ds(pl.multiple_of((r ^ me) * rpd, rpd), rpd)
                first.append(pltpu.make_async_copy(ref.at[t, 0], pp.at[at, :], sem.at[count]))
                later.append(pltpu.make_async_copy(ref.at[t, pl.ds(1, 4)], u4.at[:, at, :], sem.at[count + 1]))
                to = vv.at[pl.ds(pl.multiple_of((r ^ me) * 4, 4), 4)]
                later.append(pltpu.make_async_copy(ref.at[t, pl.ds(5, 4)], to, sem.at[count + 2]))
                count += 3
        return first, later

    def rows_of(k):
        return pl.ds(k * GR, GR)

    def grads_out(j):
        if not owners:
            cols = pl.ds(pl.multiple_of(j * 512, 512), 512)
            return [
                pltpu.make_async_copy(pk.at[0], first_any.at[:, cols], sem_du.at[j, 0]),
                pltpu.make_async_copy(pk.at[1], second_any.at[cols, :], sem_du.at[j, 1]),
            ]
        at = pl.ds(pl.multiple_of(j * rpd, rpd), rpd)
        low = pl.ds(4 * rpd, 4 * rpd)
        out = []
        for c, to in enumerate((first_any, second_any)):
            out.append(pltpu.make_async_copy(pk.at[c, :, at, :], to.at[:, at, :], sem_du.at[j, c]))
            for m in range(256 // (4 * rpd)):
                pos = place_of((j * (256 // (4 * rpd)) + m) ^ (me >> 1), [tuple(b - 1 for b in g) for g in groups[1:]])
                n = 2 * m + c
                out.append(pltpu.make_async_copy(pk.at[c, pos, low, :], to.at[pos, low, :], sem_dv.at[j, n]))
        return out

    @pl.when(j == 0)
    def _():
        first, later = weights()
        ins = []
        for c in first:
            c.start()
        for k in range(blocks):
            ins.append(pltpu.make_async_copy(x_any.at[rows_of(k)], xb.at[rows_of(k)], sem_x.at[k]))
            ins.append(pltpu.make_async_copy(o_any.at[rows_of(k)], ob.at[rows_of(k)], sem_o.at[k]))
        load_g = pltpu.make_async_copy(g_any, gp.at[pl.ds(0, rows)], sem_g.at[0])
        for c in ins + [load_g] + later:
            c.start()
        h2[rows:padded, :] = jnp.zeros((padded - rows, D), bf16)
        gp[rows:padded, :] = jnp.zeros((padded - rows, D), bf16)
        dus[rows:padded, :] = jnp.zeros((padded - rows, 512), bf16)
        for q in range(FF // 512):
            es[q, rows:padded, :] = jnp.zeros((padded - rows, 512), bf16)
        dh2[...] = jnp.zeros_like(dh2)
        for c in first:
            c.wait()
        store_p = pltpu.make_async_copy(pp, p_any, sem_p.at[0])
        store_p.start()
        squares = jnp.zeros((1, D), f32)
        for k in range(blocks):
            at = slice(k * GR, k * GR + GR)
            ins[2 * k].wait()
            ins[2 * k + 1].wait()
            a = nn(ob[at, :], pp[...]) + proj_bias
            squares = squares + jnp.sum(a * a * vld_ref[at, 0:1], axis=0, keepdims=True)
            m = xb[at, :].astype(f32) + a
            mid[at, :] = m
            c = m - jnp.mean(m, axis=-1, keepdims=True)
            var = jnp.mean(c * c, axis=-1, keepdims=True)
            h2[at, :] = (c * lax.rsqrt(var + 1e-5) * gain + shift).astype(bf16)
        st_ref[...] = jnp.zeros_like(st_ref)
        st_ref[1:2, :] = squares
        load_g.wait()

        def turn(k, carry):
            at = pl.ds(pl.multiple_of(k * LANES, LANES), LANES)
            for a in range(D // LANES):
                cols = slice(LANES * a, LANES * a + LANES)
                h2T[cols, at] = h2[at, cols].T
                gT[cols, at] = gp[at, cols].T
            return carry

        lax.fori_loop(0, padded // LANES, turn, 0)
        for c in later:
            c.wait()
        store_p.wait()

    up = u4[j]
    down = vv[pl.ds(pl.multiple_of(32 * j, 32), 32)].reshape(512, D)
    up_bias = rowv_ref[pl.ds(8 + j, 1), :]

    def products(k):
        at = slice(k * GR, k * GR + GR)
        return nn(h2[at, :], up) + up_bias, nt(gp[at, :], down)

    up_sum = jnp.zeros((1, 512), f32)
    ahead = products(0)
    for k in range(blocks):
        u, de = ahead
        if k + 1 < blocks:
            ahead = products(k + 1)
        at = slice(k * GR, k * GR + GR)
        cdf = 0.5 * lax.erf(u * RT2) + 0.5
        es[j, at, :] = (u * cdf).astype(bf16)
        du = de * (cdf + u * (PHI * jnp.exp2(u * u * (-0.5 * LOG2E))))
        dus[at, :] = du.astype(bf16)
        up_sum = up_sum + jnp.sum(du, axis=0, keepdims=True)
        dh2[at, :] += nt(dus[at, :], up)
    dbf1_ref[pl.ds(j, 1), :] = up_sum
    dU = nn(h2T[...], dus[...]).astype(bf16)
    dV = nn(gT[...], es[j]).astype(bf16).T
    if owners:
        at = pl.ds(pl.multiple_of(j * rpd, rpd), rpd)
        for k in range(owners):
            pk[(k ^ me) & 1, place_of(k ^ me, groups[1:]), at, :] = dU[rpd * k : rpd * k + rpd]
        per = 512 // (4 * rpd)
        for k in range(per):
            rel = (j * per + k) ^ me
            pk[rel & 1, place_of(rel, groups[1:]), 4 * rpd : 8 * rpd, :] = dV[4 * rpd * k : 4 * rpd * k + 4 * rpd]
        for c in grads_out(j):
            c.start()
    else:
        pk[0] = dU
        pk[1] = dV
        for c in grads_out(j):
            c.start()
        for c in grads_out(j):
            c.wait()

    @pl.when(j == last)
    def _():
        zero = jnp.zeros((1, D), f32)
        sums = [zero] * 4
        stats = [zero] * 5
        outs = []
        for k in range(blocks):
            at = slice(k * GR, k * GR + GR)
            m = mid[at, :]
            c = m - jnp.mean(m, axis=-1, keepdims=True)
            rs = lax.rsqrt(jnp.mean(c * c, axis=-1, keepdims=True) + 1e-5)
            xh = c * rs
            d = dh2[at, :]
            dx = d * gain
            dxx = d * xh
            m1 = jnp.mean(dx, axis=-1, keepdims=True)
            m2 = jnp.mean(dxx * gain, axis=-1, keepdims=True)
            grad = gp[at, :].astype(f32)
            dm = grad + (dx - m1 - xh * m2) * rs
            dh2[at, :] = dm
            outs.append(pltpu.make_async_copy(dh2.at[rows_of(k)], dmid_any.at[rows_of(k)], sem_m.at[k]))
            outs[-1].start()
            terms = (dm.astype(bf16).astype(f32), dxx, d, grad)
            sums = [a + jnp.sum(t, axis=0, keepdims=True) for a, t in zip(sums, terms)]
            f = rowv_ref[7:8, :]
            for b in range(4):
                f = f + nn(es[b, at, :], vv[32 * b : 32 * b + 32].reshape(512, D))
            out = m + f
            res[at, :] = out.astype(bf16)
            outs.append(pltpu.make_async_copy(res.at[rows_of(k)], res_any.at[rows_of(k)], sem_r.at[k]))
            outs[-1].start()
            vl = vld_ref[at, 0:1]
            x = xb[at, :].astype(f32)
            terms = (x * x * vl, m * m * vl, f * f * vl, out * out * vl, jnp.broadcast_to(vl, (GR, D)))
            stats = [a + jnp.sum(t, axis=0, keepdims=True) for a, t in zip(stats, terms)]
        for q in range(4):
            vec_ref[q : q + 1, :] = sums[q]
        vec_ref[4:8, :] = jnp.zeros((4, D), f32)
        dbf1_ref[4:8, :] = jnp.zeros((4, D), f32)
        for q, t in zip((0, 2, 3, 4, 5), stats):
            st_ref[q : q + 1, :] = t
        if owners:
            for step in range(last + 1):
                outs += grads_out(step)
        for c in outs:
            c.wait()


def mlp(me, x, o, g, vld, rowv, plan, pieces, rpd, owners, count, groups):
    rows = x.shape[0]
    blocks = rows // GR
    steps = FF // 512
    padded = -(-rows // LANES) * LANES
    copies = sum(1 if r is None else 3 * len(r) for r in plan)
    if owners:
        grad_shapes = [sds((count // 2, 8 * rpd, 512), bf16)] * 2
        pk = (2, count // 2, 8 * rpd, 512)
    else:
        grad_shapes = [sds((D, FF), bf16), sds((FF, D), bf16)]
        pk = (2, 512, 512)
    dma = pltpu.SemaphoreType.DMA
    return pl.pallas_call(
        functools.partial(mlp_body, plan=plan, rows=rows, owners=count if owners else 0, rpd=rpd, groups=groups),
        grid=(steps,),
        in_specs=[SMEM, whole((rows, LANES)), whole((16, D))] + any_specs(3 + len(pieces)),
        out_specs=any_specs(5) + [whole((8, D))] * 3,
        out_shape=[sds((rows, D), bf16), sds((rows, D), f32), sds((D, D), bf16)] + grad_shapes + [sds((8, D), f32)] * 3,
        scratch_shapes=[
            pltpu.VMEM((rows, D), bf16),
            pltpu.VMEM((rows, D), bf16),
            pltpu.VMEM((padded, D), bf16),
            pltpu.VMEM((D, padded), bf16),
            pltpu.VMEM((padded, D), bf16),
            pltpu.VMEM((D, padded), bf16),
            pltpu.VMEM((rows, D), f32),
            pltpu.VMEM((rows, D), f32),
            pltpu.VMEM((steps, padded, 512), bf16),
            pltpu.VMEM((padded, 512), bf16),
            pltpu.VMEM((steps, D, 512), bf16),
            pltpu.VMEM((FF // 16, 16, D), bf16),
            pltpu.VMEM((D, D), bf16),
            pltpu.VMEM((rows, D), bf16),
            pltpu.VMEM(pk, bf16),
            dma((copies,)),
            dma((blocks,)),
            dma((blocks,)),
            dma((1,)),
            dma((1,)),
            dma((steps, 2)),
            dma((steps, max(1, 512 // (4 * rpd)))),
            dma((blocks,)),
            dma((blocks,)),
        ],
        compiler_params=params(62),
        cost_estimate=pl.CostEstimate(flops=10**7, bytes_accessed=10**5, transcendentals=0),
        name="mlp",
    )(me, vld, rowv, x, o, g, *pieces)


def attn_bwd_body(me_ref, dmid_ref, p_ref, oT_ref, q_ref, kT_ref, v_ref, pT_ref, xT_ref, w_ref, rowv_ref, *refs, owners, rpd, groups):
    dm_ref, acc_ref, vec_ref = refs[:3]
    grads = refs[3:-6]
    xs, dap, don, doT, dw, dproj = refs[-6:]
    i = pl.program_id(0)

    @pl.when(i == 0)
    def _():
        acc_ref[...] = jnp.zeros_like(acc_ref)
        dw[...] = jnp.zeros_like(dw)
        dproj[...] = jnp.zeros_like(dproj)

    xs[0:GR, :] = dmid_ref[...]
    for w in range(GW):
        dap[LANES * w : LANES * w + LANES, :] = pad_window(xs[CELLS * w : CELLS * w + 104, :])
        dm_ref[LANES * w + KP : LANES * w + LANES, :] = jnp.zeros((LANES - KP, 3 * D), bf16)
    da = dap[...]
    don[...] = nt(da, p_ref[...]).astype(bf16)
    dproj[...] += nn(oT_ref[...], da)
    for w in range(GW):
        for a in range(D // LANES):
            rows, cols = slice(LANES * w, LANES * w + LANES), slice(LANES * a, LANES * a + LANES)
            doT[cols, rows] = don[rows, cols].T
    factor = HD**-0.5

    def window(w, carry):
        start = pl.multiple_of(w * LANES, LANES)
        at = pl.ds(start, LANES)
        keys = pl.ds(start, KP)
        for g in range(4):
            c0 = LANES * g
            cols = slice(c0, c0 + LANES)
            dp = nn(by_head(v_ref[keys, cols]), doT[cols, at])
            dss = []
            for q in range(4):
                h = 4 * g + q
                head = slice(HD * h, HD * h + HD)
                delta = jnp.sum(doT[head, at].astype(f32) * oT_ref[head, at].astype(f32), axis=0, keepdims=True)
                ds = pT_ref[w, h].astype(f32) * (dp[KP * q : KP * q + KP] - delta)
                acc_ref[h] += ds
                dss.append(ds.astype(bf16))
            dq = [nn(kT_ref[c0 + HD * q : c0 + HD * q + HD, at][:, 0:KP], dss[q]) for q in range(4)]
            dm_ref[at, cols] = (jnp.concatenate(dq, axis=0) * factor).astype(bf16).T
            dk = nn(jnp.concatenate(dss, axis=1), by_head(q_ref[at, cols])) * factor
            dm_ref[keys, D + c0 : D + c0 + LANES] = dk.astype(bf16)
            dv = nn(jnp.concatenate([pT_ref[w, 4 * g + q] for q in range(4)], axis=1), by_head(don[at, cols]))
            dm_ref[keys, 2 * D + c0 : 2 * D + c0 + LANES] = dv.astype(bf16)
        return carry

    lax.fori_loop(0, GW, window, 0, unroll=4)
    dw[...] += nn(xT_ref[...], dm_ref[...])

    @pl.when(i == pl.num_programs(0) - 1)
    def _():
        s = dw[D : D + 1, :]
        vec_ref[...] = jnp.zeros_like(vec_ref)
        vec_ref[0:1, :] = s
        for a in range(D // LANES):
            rows = slice(LANES * a, LANES * a + LANES)
            col = rowv_ref[0:8, rows].T
            x = dw[rows, :]
            wt = w_ref[rows, :].astype(f32)
            by_gain = jnp.broadcast_to(jnp.sum(wt * x, axis=1, keepdims=True), (LANES, LANES)).T
            by_shift = jnp.broadcast_to(jnp.sum(wt * s, axis=1, keepdims=True), (LANES, LANES)).T
            vec_ref[1:2, rows] = by_gain[0:1]
            vec_ref[2:3, rows] = by_shift[0:1]
            dw[rows, :] = col[:, 0:1] * x + col[:, 1:2] * s
        if owners:
            me = me_ref[0]
            for k in range(owners):
                rel = k ^ me
                pos = place_of(rel, groups[1:])
                mine = slice(rpd * k, rpd * k + rpd)

                def store(to, mine=mine, pos=pos):
                    for q in range(3):
                        to[pos, rpd * q : rpd * q + rpd, :] = dw[mine, D * q : D * q + D].astype(bf16)
                    to[pos, 3 * rpd : 4 * rpd, :] = dproj[mine, :].astype(bf16)

                pl.when(rel & 1 == 0)(functools.partial(store, grads[0]))
                pl.when(rel & 1 == 1)(functools.partial(store, grads[1]))
        else:
            grads[0][...] = dw[0:D, :].astype(bf16)
            grads[1][...] = dproj[...].astype(bf16)


def attn_bwd(me, dmid, p, oT, q, kT, v, pT, xT, w, rowv, rpd, owners, count, groups):
    n = q.shape[0] // GL

    def tb(r):
        return pl.BlockSpec((r, GL), lambda i: (0, i))

    pb = pl.BlockSpec((GL, D), lambda i: (i, 0))
    if owners:
        grad_shapes = [sds((count // 2, 4 * rpd, D), bf16)] * 2
    else:
        grad_shapes = [sds((D, 3 * D), bf16), sds((D, D), bf16)]
    return pl.pallas_call(
        functools.partial(attn_bwd_body, owners=count if owners else 0, rpd=rpd, groups=groups),
        grid=(n,),
        in_specs=[SMEM, pl.BlockSpec((GR, D), lambda i: (i, 0)), whole((D, D)), tb(D), pb, tb(D), pb, pl.BlockSpec((GW, HEADS, KP, LANES), lambda i: (i, 0, 0, 0)), tb(D + 16), whole((D, 3 * D)), whole((16, D))],
        out_specs=[pl.BlockSpec((GL, 3 * D), lambda i: (i, 0)), whole((HEADS, KP, LANES)), whole((8, 3 * D))] + [whole(s.shape) for s in grad_shapes],
        out_shape=[sds((n * GL, 3 * D), bf16), sds((HEADS, KP, LANES), f32), sds((8, 3 * D), f32)] + grad_shapes,
        scratch_shapes=[
            pltpu.VMEM((GR + 8, D), f32),
            pltpu.VMEM((GL, D), bf16),
            pltpu.VMEM((GL, D), bf16),
            pltpu.VMEM((D, GL), bf16),
            pltpu.VMEM((D + 16, 3 * D), f32),
            pltpu.VMEM((D, D), f32),
        ],
        compiler_params=params(60),
        cost_estimate=pl.CostEstimate(flops=10**7, bytes_accessed=10**5, transcendentals=0),
        name="attn_bwd",
    )(me, dmid, p, oT, q, kT, v, pT, xT, w, rowv)


def grad_in_body(dm_ref, w_ref, x_ref, dmid_ref, rowv_ref, tg_ref, dsc):
    dh = nt(dm_ref[...], w_ref[...])
    for w in range(GW):
        dsc[CELLS * w : CELLS * w + 104, :] = dh[LANES * w : LANES * w + 104]
    x = x_ref[...].astype(f32)
    c = x - jnp.mean(x, axis=-1, keepdims=True)
    rs = lax.rsqrt(jnp.mean(c * c, axis=-1, keepdims=True) + 1e-5)
    xh = c * rs
    dx = dsc[0:GR, :] * rowv_ref[0:1, :]
    m1 = jnp.mean(dx, axis=-1, keepdims=True)
    m2 = jnp.mean(dx * xh, axis=-1, keepdims=True)
    tg_ref[...] = dmid_ref[...] + (dx - m1 - xh * m2) * rs


def grad_in(dm, w, x, dmid, rowv):
    n = x.shape[0] // GR
    rb = pl.BlockSpec((GR, D), lambda i: (i, 0))
    return pl.pallas_call(
        grad_in_body,
        grid=(n,),
        in_specs=[pl.BlockSpec((GL, 3 * D), lambda i: (i, 0)), whole((D, 3 * D)), rb, rb, whole((16, D))],
        out_specs=rb,
        out_shape=sds((n * GR, D), f32),
        scratch_shapes=[pltpu.VMEM((GR + 8, D), f32)],
        compiler_params=params(60),
        cost_estimate=pl.CostEstimate(flops=10**7, bytes_accessed=10**5, transcendentals=0),
        name="grad_in",
    )(dm, w, x, dmid, rowv)


SMALL = 24


def two_terms(x):
    hi = x.astype(bf16).astype(f32)
    return jnp.concatenate([hi, x - hi], axis=0).astype(bf16)


def one_term(x):
    x = x.astype(f32)
    return x[0:SMALL] + x[SMALL : 2 * SMALL]


def fold_body(*refs, first, terms, parts):
    ins, outs = refs[: 2 * terms if first else terms + 1], refs[2 * terms if first else terms + 1 :]
    nb, rows = ins[0].shape[0], ins[0].shape[1]
    n = nb // (parts + 1)
    if first:
        small = ins[2][...] + ins[3][...]
    else:
        got = [one_term(ins[1][...])] + [one_term(r[nb * rows :, :]) for r in ins[2:]]
        while len(got) > 1:
            got = [got[k] + got[k + 1] for k in range(0, len(got), 2)]
        small = got[0]
    for p in range(parts + 1):
        at = slice(p * n, p * n + n)
        total = ins[0][at].astype(f32)
        if first:
            total = total + ins[1][at].astype(f32)
        else:
            for r in ins[2:]:
                total = total + r[p * n * rows : (p + 1) * n * rows, :].astype(f32).reshape(n, rows, D)
        if p == 0:
            outs[0][...] = total
            outs[1][...] = two_terms(small)
        else:
            outs[p + 1][0 : n * rows, :] = total.reshape(n * rows, D).astype(bf16)
            outs[p + 1][n * rows :, :] = two_terms(small)


def fold(arrays, parts, first=False):
    terms = 2 if first else len(arrays) - 1
    nb, rows = arrays[0].shape[:2]
    n = nb // (parts + 1)
    return pl.pallas_call(
        functools.partial(fold_body, first=first, terms=terms, parts=parts),
        out_shape=[sds((n, rows, D), f32), sds((2 * SMALL, D), bf16)] + [sds((n * rows + 2 * SMALL, D), bf16)] * parts,
        compiler_params=params(16),
        cost_estimate=pl.CostEstimate(flops=10**6, bytes_accessed=10**5, transcendentals=0),
        name="fold",
    )(*arrays)


def spread(o_ref, block, width, at):
    each = width // LANES
    for b in range(block.shape[1] // LANES):
        o_ref[pl.ds(at // LANES + b, block.shape[0], stride=each), :] = block[:, LANES * b : LANES * b + LANES]


def attn_last_body(me_ref, own_ref, kept_ref, *refs, rpd, per):
    got_refs, (qkv_ref, proj_ref, vec_ref, table_ref, stats_ref, lines) = refs[:-6], refs[-6:]
    rows = 4 * rpd
    total = own_ref[0]
    for r in got_refs:
        total = total + r[0:rows, :].astype(f32)
    for q in range(3):
        spread(qkv_ref, total[rpd * q : rpd * q + rpd], 3 * D, D * q)
    spread(proj_ref, total[3 * rpd : rows], D, 0)
    got = [one_term(kept_ref[...])] + [one_term(r[rows:, :]) for r in got_refs]
    while len(got) > 1:
        got = [got[k] + got[k + 1] for k in range(0, len(got), 2)]
    small = got[0]
    for k in range(8):
        for a in range(4):
            lines[4 * k + a : 4 * k + a + 1, :] = small[k : k + 1, LANES * a : LANES * a + LANES]
    lines[32:48, :] = small[8:24, RP:D]
    if per % 64:
        vec_ref[...] = lines[...]
    else:
        low = lax.broadcasted_iota(jnp.int32, (1, LANES), 1) < 64
        for p in range(0, per // 64, 2):
            halves = []
            for k in range(2):
                c = me_ref[0] * (per // 64) + min(p + k, per // 64 - 1)
                line = lines[pl.ds(c >> 1, 1), :]
                halves.append(jnp.where(c & 1 == k, line, pltpu.roll(line, 64, 1)))
            vec_ref[p // 2 : p // 2 + 1, :] = jnp.where(low, halves[0], halves[1])
    turned = small[8:24, 0:RP].T
    table_ref[...] = turned[0:RELN]
    line = turned[RELN : RELN + 1]
    stats_ref[...] = jnp.sqrt(line / line[:, 5:6] + 1e-06)


def attn_last(me, arrays, rpd, per):
    lines = -(-per // LANES) if per % 64 == 0 else 48
    return pl.pallas_call(
        functools.partial(attn_last_body, rpd=rpd, per=per),
        in_specs=[SMEM] + [pl.BlockSpec(memory_space=pltpu.VMEM)] * len(arrays),
        out_shape=[sds((12 * rpd, LANES), f32), sds((4 * rpd, LANES), f32), sds((lines, LANES), f32), sds((RELN, HEADS), f32), sds((1, HEADS), f32)],
        scratch_shapes=[pltpu.VMEM((48, LANES), f32)],
        compiler_params=params(16),
        cost_estimate=pl.CostEstimate(flops=10**6, bytes_accessed=10**5, transcendentals=0),
        name="attn_last",
    )(me, *arrays)


def mlp_last_body(own_ref, *refs, rpd):
    total = own_ref[0]
    for r in refs[:-2]:
        total = total + r[0].astype(f32)
    for q in range(4):
        spread(refs[-2], total[rpd * q : rpd * q + rpd], FF, 512 * q)
    spread(refs[-1], total[4 * rpd :], D, 0)


def mlp_last(arrays, rpd):
    return pl.pallas_call(
        functools.partial(mlp_last_body, rpd=rpd),
        out_shape=[sds((16 * rpd, LANES), f32)] * 2,
        compiler_params=params(16),
        cost_estimate=pl.CostEstimate(flops=10**6, bytes_accessed=10**5, transcendentals=0),
        name="mlp_last",
    )(*arrays)


def place_hits(shape, axis, rev=0):
    c = lax.broadcasted_iota(jnp.int32, shape, 1 - axis)
    code = jnp.where(c < CELLS, (2 * WSIDE - 1) * (c // WSIDE) + c % WSIDE, -1000)
    if rev:
        code = rev - code
    return jnp.where(code == lax.broadcasted_iota(jnp.int32, shape, axis), 1.0, 0.0).astype(bf16)


def rel_bias_body(t_ref, o_ref):
    keys = place_hits((KP, 192), 1)
    queries = place_hits((256, LANES), 0)

    def head(h, carry):
        row = pltpu.roll(jnp.broadcast_to(t_ref[pl.ds(h, 1), :], (8, RP)), 0, 1, stride=1, stride_axis=0)
        t = jnp.concatenate([pltpu.roll(row, (8 * k - 180) % RP, 1)[:, 0:256] for k in range(24)], axis=0)
        hi = t.astype(bf16)
        lo = (t - hi.astype(f32)).astype(bf16)
        b = nn(jnp.concatenate([hi, lo], axis=0), queries).astype(bf16)
        b = nn(keys, jnp.concatenate([b[0:192], b[192:384]], axis=1))
        o_ref[h] = b[:, 0:LANES] + b[:, LANES : 2 * LANES]
        return carry

    lax.fori_loop(0, HEADS, head, 0, unroll=8)


def rel_bias(table):
    return pl.pallas_call(
        rel_bias_body,
        out_shape=sds((HEADS, KP, LANES), f32),
        compiler_params=params(16),
        cost_estimate=pl.CostEstimate(flops=10**7, bytes_accessed=10**5, transcendentals=0),
        name="rel_bias",
    )(table)


def rel_grad_body(a_ref, one_ref, two_ref, up_ref, squares_ref, o_ref):
    keys = place_hits((192, KP), 0, 191)
    queries = place_hits((LANES, 256), 1)
    zero = jnp.zeros((8, RP - 256), f32)
    o_ref[0:2, :] = one_ref[1:3, 0:D]
    o_ref[2:3, :] = one_ref[0:1, 0:D]
    o_ref[3:4, :] = one_ref[0:1, 2 * D : 3 * D]
    o_ref[4:8, :] = two_ref[0:4, :]

    def head(h, carry):
        a = a_ref[h]
        hi = a.astype(bf16)
        lo = (a - hi.astype(f32)).astype(bf16)
        b = nn(keys, jnp.concatenate([hi, lo], axis=1)).astype(bf16)
        b = nn(jnp.concatenate([b[:, 0:LANES], b[:, LANES : 2 * LANES]], axis=0), queries)
        b = b[0:192] + b[192:384]
        t = jnp.zeros((8, RP), f32)
        for k in range(24):
            t = t + pltpu.roll(jnp.concatenate([b[8 * k : 8 * k + 8], zero], axis=1), (8 * k - 11) % RP, 1)
        t = pltpu.roll(t, 0, 1, stride=1, stride_axis=0)
        o_ref[pl.ds(8 + h, 1), 0:RP] = jnp.sum(t, axis=0, keepdims=True)
        return carry

    lax.fori_loop(0, HEADS, head, 0, unroll=16)
    for k in range(4):
        for a in range(4):
            o_ref[8 + 4 * k + a : 9 + 4 * k + a, RP:D] = up_ref[k : k + 1, LANES * a : LANES * a + LANES]
    for k in range(6):
        o_ref[8 + k : 9 + k, RELN : RELN + 1] = jnp.sum(squares_ref[k : k + 1, :], axis=1, keepdims=True)


def rel_grad(acc, one, two, up, squares):
    return pl.pallas_call(
        rel_grad_body,
        out_shape=sds((SMALL, D), f32),
        compiler_params=params(16),
        cost_estimate=pl.CostEstimate(flops=10**7, bytes_accessed=10**5, transcendentals=0),
        name="rel_grad",
    )(acc, one, two, up, squares)


def shards(tokens, cotangent, regions, validity, qkv_weight, proj_weight, fc1_weight, fc2_weight, vectors, rel_table, *, count, inner):
    rows = tokens.shape[0]
    groups = bit_groups(count)
    single = groups[:2] + [(b,) for g in groups[2:] for b in g]
    rpd = D // count
    direct = rpd % 16 == 0
    me = lax.axis_index("dp") * inner + lax.axis_index("shard")
    me_s = me.astype(jnp.int32).reshape(1)

    per = vectors.shape[0]
    if direct:
        own = jnp.pad(vectors, (0, rpd * LANES - per)).reshape(rpd, LANES)
        own = jnp.concatenate([qkv_weight.reshape(rpd, 3 * D), own], axis=1)
    else:
        own = jnp.concatenate([qkv_weight, vectors]).reshape(1, -1)
    rels, attn_up = gather_upper(own, groups, count)
    packed = jnp.concatenate(
        [
            proj_weight.reshape(1, rpd, D),
            fc1_weight.reshape(rpd, 4, 512).transpose(1, 0, 2),
            fc2_weight.reshape(4, rpd, D),
        ],
        axis=0,
    )
    packed = packed.reshape(9 * rpd, D)
    attn_pieces = gather_plane(rels, attn_up, groups, count)
    table_in = after(rel_table, attn_up)
    mlp_rels, mlp_up = gather_upper(packed, single, count, attn_up)

    bias = rel_bias(jnp.pad(table_in.T * LOG2E, ((0, 0), (0, RP - RELN))))
    reg = regions.reshape(-1, GW, CELLS).astype(f32)
    key_code = jnp.where(validity.reshape(-1, GW, CELLS) == 1, reg, -2.0)
    codes = jnp.pad(jnp.concatenate([reg, key_code], axis=1), ((0, 0), (0, 0), (0, LANES - CELLS)), constant_values=-3.0)

    held, mlp_up = after(([a for _, a in attn_pieces], mlp_up), bias, codes)
    mlp_up = after(mlp_up, held)
    attn_pieces = gather_core([(r, a) for (r, _), a in zip(attn_pieces, held)], count)
    mlp_pieces = gather_plane(mlp_rels, mlp_up, groups, count)
    if direct:
        attn_plan = [r for r, _ in attn_pieces]
        attn_w = [a for _, a in attn_pieces]
    else:
        attn_plan = [None] * 2
        both = natural_order(attn_pieces, me, count).reshape(count, -1)
        attn_w = [both[:, : 3 * D * rpd].reshape(D, 3 * D), jnp.pad(both[:, 3 * D * rpd :].astype(f32).reshape(12, D), ((0, 4), (0, 0)))]

    x = after(tokens, mlp_up)
    oT, o, q, kT, v, pT, xT, vld, w_full, rowv = attn_fwd(me_s, x, codes, bias, attn_plan, attn_w, rpd, per, count)

    held = after([a for _, a in mlp_pieces], o)
    mlp_pieces = gather_core([(r, a) for (r, _), a in zip(mlp_pieces, held)], count)
    if direct:
        mlp_plan = [r for r, _ in mlp_pieces]
        mlp_w = [a.reshape(-1, 9, rpd, D) for _, a in mlp_pieces]
    else:
        both = natural_order(mlp_pieces, me, count).reshape(count, 9, rpd, D)
        mlp_plan = [None] * 3
        mlp_w = [both[:, 0].reshape(D, D), both[:, 1:5].transpose(1, 0, 2, 3).reshape(4, D, 512), both[:, 5:].reshape(128, 16, D)]
    result, dmid, p_full, mlp_keep, mlp_send, vec_two, dbf1, squares = mlp(
        me_s, tokens, o, cotangent, vld, rowv, mlp_plan, mlp_w, rpd, direct, count, single
    )
    order = None
    if not direct:
        blocks = jnp.arange(count)
        order, mlp_order = (
            jnp.zeros((count,), jnp.int32).at[place_of(blocks, way)].set(blocks.astype(jnp.int32)) ^ me for way in (groups, single)
        )
        dU = mlp_keep.reshape(count, rpd, 4, 512).transpose(0, 2, 1, 3).reshape(count, 4 * rpd, 512)
        pk = jnp.take(jnp.concatenate([dU, mlp_send.reshape(count, 4 * rpd, D)], axis=1), mlp_order, axis=0)
        mlp_keep, mlp_send = pk[: count // 2], pk[count // 2 :]

    other = swap(mlp_send, 1, count)
    mlp_own, parts = split_sum([mlp_keep, other], groups[1])
    mlp_got = send_parts(parts, groups[1], count)
    dmid = after(dmid, parts)
    got = attn_bwd(me_s, dmid, p_full, oT, q, kT, v, pT, xT, w_full, rowv, rpd, direct, count, groups)
    dm, score_sums, vec_one = got[:3]
    if direct:
        attn_keep, attn_send = got[3:]
    else:
        dW = got[3].reshape(count, rpd, 3, D).transpose(0, 2, 1, 3).reshape(count, 3 * rpd, D)
        pk = jnp.take(jnp.concatenate([dW, got[4].reshape(count, rpd, D)], axis=1), order, axis=0)
        attn_keep, attn_send = pk[: count // 2], pk[count // 2 :]
    mlp_got, attn_send, score_sums, dm = lax.optimization_barrier((mlp_got, attn_send, score_sums, dm))

    other = swap(attn_send, 1, count)
    mlp_terms = [mlp_own] + mlp_got
    for g in single[2:3]:
        mlp_own, parts = split_sum(mlp_terms, g)
        mlp_terms = [mlp_own] + send_parts(parts, g, count)
        score_sums = after(score_sums, parts)
    small = rel_grad(score_sums, vec_one, vec_two, dbf1, squares)
    other = after(other, small)
    levels = [len(masks_of(g)) for g in groups[1:]]
    out = fold([attn_keep, other, small, swap(small, 1, count)], levels[0], first=True)
    for k, g in enumerate(groups[1:]):
        own, kept, parts = out[0], out[1], out[2:]
        sent = send_parts(parts, g, count)
        if k == 0:
            dm = after(dm, parts)
            grad_tokens = grad_in(dm, w_full, tokens, dmid, rowv)
            sent, mlp_terms = after((sent, mlp_terms), grad_tokens)
            for up in single[3:]:
                mlp_own, parts = split_sum(mlp_terms, up)
                mlp_terms = [mlp_own] + send_parts(parts, up, count)
        if k + 1 < len(levels):
            out = fold([own, kept] + sent, levels[k + 1])
            mlp_terms = after(mlp_terms, out)
    grad_fc1, grad_fc2 = mlp_last(mlp_terms, rpd)
    sent = after(sent, grad_fc1)
    grad_qkv, grad_proj, grad_vectors, grad_table, stats = attn_last(me_s, [own, kept] + sent, rpd, per)
    if per % 64 == 0:
        grad_vectors = grad_vectors.reshape(-1)[:per]
    else:
        grad_vectors = lax.dynamic_slice(grad_vectors.reshape(-1), (me * per,), (per,))
    return (
        result,
        grad_tokens,
        grad_qkv.reshape(-1),
        grad_proj.reshape(-1),
        grad_fc1.reshape(-1),
        grad_fc2.reshape(-1),
        grad_vectors,
        grad_table,
        stats[0, 0:5],
    )


def solution(mesh):
    flat = P(AXES)
    tall = P(AXES, None)
    in_specs = (tall, tall, flat, flat, flat, flat, flat, flat, flat, P())
    out_specs = (tall, tall, flat, flat, flat, flat, flat, P(), P())
    inner = mesh.shape["shard"]
    body = functools.partial(shards, count=mesh.shape["dp"] * inner, inner=inner)
    return jax.shard_map(body, mesh=mesh, in_specs=in_specs, out_specs=out_specs, check_vma=False)
```

```python
import functools

import jax
import jax.numpy as jnp
from jax import lax
from jax.experimental import pallas as pl
from jax.experimental.pallas import tpu as pltpu
from jax.sharding import PartitionSpec as P

D = 512
FF = 2048
HEADS = 16
HD = 32
WSIDE = 10
RELN = 361
CELLS = WSIDE * WSIDE
GW = 4
GR = GW * CELLS
KP = 112
LANES = 128
GL = GW * LANES
RP = 384
AXES = ("dp", "shard")
LOG2E = 1.4426950408889634
NEG = -1e9
RT2 = 0.7071067811865476
PHI = 0.3989422804014327
f32 = jnp.float32
bf16 = jnp.bfloat16
sds = jax.ShapeDtypeStruct


def nn(a, b):
    return lax.dot_general(a, b, (((1,), (0,)), ((), ())), preferred_element_type=f32)


def nt(a, b):
    return lax.dot_general(a, b, (((1,), (1,)), ((), ())), preferred_element_type=f32)


def whole(shape):
    return pl.BlockSpec(shape, lambda i: (0,) * len(shape))


def params(mib):
    return pltpu.CompilerParams(vmem_limit_bytes=mib * 2**20)


def bit_groups(count):
    bits = count.bit_length() - 1
    groups = [(0,)]
    at = 1
    while at < bits:
        groups.append(tuple(range(at, min(at + 2, bits))))
        at += 2
    return groups


def masks_of(group):
    return [sum(((v >> k) & 1) << b for k, b in enumerate(group)) for v in range(1, 1 << len(group))]


def swap(x, mask, count):
    return lax.ppermute(x, AXES, [(i, i ^ mask) for i in range(count)])


def place_of(rel, groups):
    pos = 0
    for g in groups:
        pos = pos * (1 << len(g)) + ((rel >> g[0]) & ((1 << len(g)) - 1))
    return pos


def after(values, *others):
    return lax.optimization_barrier((values, others))[0]


def gather_upper(x, groups, count, *others):
    cur = x[None]
    rels = [0]
    for k, g in enumerate(groups[:1:-1]):
        if k and others:
            cur = after(cur, *others)
        ms = masks_of(g)
        cur = jnp.concatenate([cur] + [swap(cur, m, count) for m in ms], axis=0)
        rels = [r ^ m for m in [0] + ms for r in rels]
    return rels, cur


def gather_plane(rels, cur, groups, count):
    return [(rels, cur)] + [([r ^ m for r in rels], swap(cur, m, count)) for m in masks_of(groups[1])]


def gather_core(pieces, count):
    return pieces + [([r ^ 1 for r in rels], swap(arr, 1, count)) for rels, arr in pieces]


def hold(pieces, *others):
    held = after([a for _, a in pieces[1:]], *others)
    return pieces[:1] + [(r, a) for (r, _), a in zip(pieces[1:], held)]


def natural_order(pieces, me, count):
    rels = [r for rs, _ in pieces for r in rs]
    where = [0] * count
    for k, r in enumerate(rels):
        where[r] = k
    both = jnp.concatenate([a for _, a in pieces], axis=0)
    return jnp.take(both, jnp.asarray(where, jnp.int32)[jnp.arange(count) ^ me], axis=0)


def send_parts(parts, group, count):
    return [swap(p, m, count) for p, m in zip(parts, masks_of(group))]


def lay_vectors(raw, per, rowv_ref):
    unit = LANES // 2
    each = per // unit
    low = lax.broadcasted_iota(jnp.int32, (1, LANES), 1) < unit

    def half(c, high):
        owner, part = divmod(c, each)
        got = raw[owner, part // 2 : part // 2 + 1, :].astype(f32)
        return got if part % 2 == high else pltpu.roll(got, unit, 1)

    for m in range((8 * D + FF) // LANES):
        row, col = divmod(m * LANES, D)
        rowv_ref[row : row + 1, col : col + LANES] = jnp.where(low, half(2 * m, 0), half(2 * m + 1, 1))


def pad_window(rows):
    at = lax.broadcasted_iota(jnp.int32, (104, 1), 0)
    rows = jnp.where(at < CELLS, rows, 0.0)
    return jnp.concatenate([rows, jnp.zeros((LANES - 104, rows.shape[1]), f32)], axis=0).astype(bf16)


def head_lanes():
    return lax.broadcasted_iota(jnp.int32, (1, LANES), 1) // HD


def by_head(block):
    lane = head_lanes()
    return jnp.concatenate([jnp.where(lane == q, block, jnp.zeros_like(block)) for q in range(4)], axis=0)


def attn_fwd_body(me_ref, x_ref, code_ref, bias_ref, *refs, plan, rpd, per):
    pieces = refs[: len(plan)]
    (oT_ref, o_ref, q_ref, kT_ref, v_ref, pT_ref, xT_ref, vld_ref, w_ref, rowv_ref) = refs[len(plan) : len(plan) + 10]
    xs, h1p, qT, kn, vT, osc, vsc, mask_ref, raw, sem = refs[len(plan) + 10 :]

    @pl.when(pl.program_id(0) == 0)
    def _():
        copies = []
        for ref, rels in zip(pieces, plan):
            if rels is None:
                copies.append(pltpu.make_async_copy(ref, (w_ref, rowv_ref)[len(copies)], sem.at[len(copies)]))
                continue
            for t, r in enumerate(rels):
                at = pl.multiple_of((r ^ me_ref[0]) * rpd, rpd)
                copies.append(
                    pltpu.make_async_copy(
                        ref.at[t, :, pl.ds(0, 3 * D)], w_ref.at[pl.ds(at, rpd), :], sem.at[len(copies)]
                    )
                )
                copies.append(
                    pltpu.make_async_copy(ref.at[t, :, pl.ds(3 * D, LANES)], raw.at[r ^ me_ref[0]], sem.at[len(copies)])
                )
        for c in copies:
            c.start()
        for c in copies:
            c.wait()
        if plan[0] is not None:
            rowv_ref[12:16, :] = jnp.zeros((4, D), f32)
            lay_vectors(raw, per, rowv_ref)

    xs[0:GR, :] = x_ref[...].astype(f32)
    gain = rowv_ref[0:1, :]
    shift = rowv_ref[1:2, :]
    for w in range(GW):
        xw = xs[CELLS * w : CELLS * w + 104, :]
        c = xw - jnp.mean(xw, axis=-1, keepdims=True)
        var = jnp.mean(c * c, axis=-1, keepdims=True)
        xh = c * lax.rsqrt(var + 1e-5)
        h1p[LANES * w : LANES * w + LANES, :] = pad_window(xh * gain + shift)
        xh = pad_window(xh)
        for a in range(D // LANES):
            xT_ref[LANES * a : LANES * a + LANES, LANES * w : LANES * w + LANES] = xh[:, LANES * a : LANES * a + LANES].T
    xT_ref[D : D + 16, :] = jnp.ones((16, GL), bf16)
    turned = code_ref[0].T
    keys = lax.broadcasted_iota(jnp.int32, (KP, LANES), 0)
    same = (keys == lax.broadcasted_iota(jnp.int32, (KP, LANES), 1)) & (keys < CELLS)
    for w in range(GW):
        of_key = turned[:, GW + w : GW + w + 1]
        equal = jnp.broadcast_to(of_key[0:KP], (KP, LANES)) == jnp.broadcast_to(code_ref[0, w : w + 1, :], (KP, LANES))
        mask_ref[w] = jnp.where(equal | same, 0.0, NEG)
        vsc[CELLS * w : CELLS * w + 104, :] = jnp.broadcast_to(jnp.where(of_key[0:104] >= 0.0, 1.0, 0.0), (104, LANES))
    vld_ref[...] = vsc[0:GR, :]
    hp = h1p[...]
    q_ref[...] = (nn(hp, w_ref[:, 0:D]) + rowv_ref[2:3, :]).astype(bf16)
    kn[...] = nn(hp, w_ref[:, D : 2 * D]).astype(bf16)
    v_ref[...] = (nn(hp, w_ref[:, 2 * D : 3 * D]) + rowv_ref[3:4, :]).astype(bf16)
    for src, dst in ((q_ref, qT), (kn, kT_ref), (v_ref, vT)):
        for w in range(GW):
            for a in range(D // LANES):
                rows, cols = slice(LANES * w, LANES * w + LANES), slice(LANES * a, LANES * a + LANES)
                dst[cols, rows] = src[rows, cols].T
    factor = HD**-0.5 * LOG2E

    def window(w, carry):
        start = pl.multiple_of(w * LANES, LANES)
        at = pl.ds(start, LANES)
        allowed = mask_ref[w]
        for g in range(4):
            cols = slice(LANES * g, LANES * g + LANES)
            s = nn(by_head(kn[pl.ds(start, KP), cols]), qT[cols, at])
            ps = []
            for q in range(4):
                h = 4 * g + q
                t = s[KP * q : KP * q + KP] * factor + bias_ref[h] + allowed
                e = jnp.exp2(t - jnp.max(t, axis=0, keepdims=True))
                p = (e * (1.0 / jnp.sum(e, axis=0, keepdims=True))).astype(bf16)
                pT_ref[w, h] = p
                ps.append(p)
            o = [nn(vT[LANES * g + HD * q : LANES * g + HD * q + HD, at][:, 0:KP], ps[q]) for q in range(4)]
            oT_ref[cols, at] = jnp.concatenate(o, axis=0).astype(bf16)
        return carry

    lax.fori_loop(0, GW, window, 0, unroll=4)
    for w in range(GW):
        for a in range(D // LANES):
            osc[CELLS * w : CELLS * w + 104, LANES * a : LANES * a + LANES] = (
                oT_ref[LANES * a : LANES * a + LANES, LANES * w : LANES * w + LANES].T[0:112].astype(f32)[0:104]
            )
    o_ref[...] = osc[0:GR, :].astype(bf16)


def any_specs(n):
    return [pl.BlockSpec(memory_space=pl.ANY)] * n


SMEM = pl.BlockSpec(memory_space=pltpu.SMEM)


def attn_fwd(me, x, codes, bias, plan, pieces, rpd, per, count):
    n = x.shape[0] // GR
    copies = sum(1 if r is None else 2 * len(r) for r in plan)
    rb = pl.BlockSpec((GR, D), lambda i: (i, 0))
    tb = pl.BlockSpec((D, GL), lambda i: (0, i))
    pb = pl.BlockSpec((GL, D), lambda i: (i, 0))
    return pl.pallas_call(
        functools.partial(attn_fwd_body, plan=plan, rpd=rpd, per=per),
        grid=(n,),
        in_specs=[SMEM, rb, pl.BlockSpec((1, 2 * GW, LANES), lambda i: (i, 0, 0)), whole((HEADS, KP, LANES))]
        + any_specs(len(pieces)),
        out_specs=[
            tb,
            rb,
            pb,
            tb,
            pb,
            pl.BlockSpec((GW, HEADS, KP, LANES), lambda i: (i, 0, 0, 0)),
            pl.BlockSpec((D + 16, GL), lambda i: (0, i)),
            pl.BlockSpec((GR, LANES), lambda i: (i, 0)),
            whole((D, 3 * D)),
            whole((16, D)),
        ],
        out_shape=[
            sds((D, n * GL), bf16),
            sds((n * GR, D), bf16),
            sds((n * GL, D), bf16),
            sds((D, n * GL), bf16),
            sds((n * GL, D), bf16),
            sds((n * GW, HEADS, KP, LANES), bf16),
            sds((D + 16, n * GL), bf16),
            sds((n * GR, LANES), f32),
            sds((D, 3 * D), bf16),
            sds((16, D), f32),
        ],
        scratch_shapes=[
            pltpu.VMEM((GR + 8, D), f32),
            pltpu.VMEM((GL, D), bf16),
            pltpu.VMEM((D, GL), bf16),
            pltpu.VMEM((GL, D), bf16),
            pltpu.VMEM((D, GL), bf16),
            pltpu.VMEM((GR + 8, D), f32),
            pltpu.VMEM((GR + 8, LANES), f32),
            pltpu.VMEM((GW, KP, LANES), f32),
            pltpu.VMEM((count, max(rpd, 16), LANES), bf16),
            pltpu.SemaphoreType.DMA((copies,)),
        ],
        compiler_params=params(60),
        cost_estimate=pl.CostEstimate(flops=10**7, bytes_accessed=10**5, transcendentals=0),
        name="attn_fwd",
    )(me, x, codes, bias, *pieces)


def mlp_body(me_ref, vld_ref, rowv_ref, x_any, o_any, g_any, *refs, plan, rows, owners, rpd, groups):
    pieces = refs[: len(plan)]
    refs = refs[len(plan) :]
    res_any, dmid_any, p_any, first_any, second_any, vec_ref, dbf1_ref, st_ref = refs[:8]
    xb, ob, gp, gT, h2, h2T, mid, dh2, es, dus, u4, vv, pp, res, pk, sem, sem_x, sem_o, sem_p, sem_g, sem_du, sem_dv, sem_r, sem_m = refs[8:]
    j = pl.program_id(0)
    last = FF // 512 - 1
    padded = h2.shape[0]
    blocks = rows // GR
    me = me_ref[0]
    proj_bias = rowv_ref[4:5, :]
    gain = rowv_ref[5:6, :]
    shift = rowv_ref[6:7, :]

    def weights():
        first, later = [], []
        count = 0
        for ref, rels in zip(pieces, plan):
            if rels is None:
                dst = (pp, u4, vv)[count]
                (first if count == 0 else later).append(pltpu.make_async_copy(ref, dst, sem.at[count]))
                count += 1
                continue
            for t, r in enumerate(rels):
                at = pl.ds(pl.multiple_of((r ^ me) * rpd, rpd), rpd)
                first.append(pltpu.make_async_copy(ref.at[t, 0], pp.at[at, :], sem.at[count]))
                later.append(pltpu.make_async_copy(ref.at[t, pl.ds(1, 4)], u4.at[:, at, :], sem.at[count + 1]))
                to = vv.at[pl.ds(pl.multiple_of((r ^ me) * 4, 4), 4)]
                later.append(pltpu.make_async_copy(ref.at[t, pl.ds(5, 4)], to, sem.at[count + 2]))
                count += 3
        return first, later

    def rows_of(k):
        return pl.ds(k * GR, GR)

    def grads_out(j):
        if not owners:
            cols = pl.ds(pl.multiple_of(j * 512, 512), 512)
            return [
                pltpu.make_async_copy(pk.at[0], first_any.at[:, cols], sem_du.at[j, 0]),
                pltpu.make_async_copy(pk.at[1], second_any.at[cols, :], sem_du.at[j, 1]),
            ]
        at = pl.ds(pl.multiple_of(j * rpd, rpd), rpd)
        low = pl.ds(4 * rpd, 4 * rpd)
        out = []
        for c, to in enumerate((first_any, second_any)):
            out.append(pltpu.make_async_copy(pk.at[c, :, at, :], to.at[:, at, :], sem_du.at[j, c]))
            for m in range(256 // (4 * rpd)):
                pos = place_of((j * (256 // (4 * rpd)) + m) ^ (me >> 1), [tuple(b - 1 for b in g) for g in groups[1:]])
                n = 2 * m + c
                out.append(pltpu.make_async_copy(pk.at[c, pos, low, :], to.at[pos, low, :], sem_dv.at[j, n]))
        return out

    @pl.when(j == 0)
    def _():
        first, later = weights()
        ins = []
        for c in first:
            c.start()
        for k in range(blocks):
            ins.append(pltpu.make_async_copy(x_any.at[rows_of(k)], xb.at[rows_of(k)], sem_x.at[k]))
            ins.append(pltpu.make_async_copy(o_any.at[rows_of(k)], ob.at[rows_of(k)], sem_o.at[k]))
        load_g = pltpu.make_async_copy(g_any, gp.at[pl.ds(0, rows)], sem_g.at[0])
        for c in ins + [load_g] + later:
            c.start()
        h2[rows:padded, :] = jnp.zeros((padded - rows, D), bf16)
        gp[rows:padded, :] = jnp.zeros((padded - rows, D), bf16)
        dus[rows:padded, :] = jnp.zeros((padded - rows, 512), bf16)
        for q in range(FF // 512):
            es[q, rows:padded, :] = jnp.zeros((padded - rows, 512), bf16)
        dh2[...] = jnp.zeros_like(dh2)
        for c in first:
            c.wait()
        store_p = pltpu.make_async_copy(pp, p_any, sem_p.at[0])
        store_p.start()
        squares = jnp.zeros((1, D), f32)
        for k in range(blocks):
            at = slice(k * GR, k * GR + GR)
            ins[2 * k].wait()
            ins[2 * k + 1].wait()
            a = nn(ob[at, :], pp[...]) + proj_bias
            squares = squares + jnp.sum(a * a * vld_ref[at, 0:1], axis=0, keepdims=True)
            m = xb[at, :].astype(f32) + a
            mid[at, :] = m
            c = m - jnp.mean(m, axis=-1, keepdims=True)
            var = jnp.mean(c * c, axis=-1, keepdims=True)
            h2[at, :] = (c * lax.rsqrt(var + 1e-5) * gain + shift).astype(bf16)
        st_ref[...] = jnp.zeros_like(st_ref)
        st_ref[1:2, :] = squares
        load_g.wait()

        def turn(k, carry):
            at = pl.ds(pl.multiple_of(k * LANES, LANES), LANES)
            for a in range(D // LANES):
                cols = slice(LANES * a, LANES * a + LANES)
                h2T[cols, at] = h2[at, cols].T
                gT[cols, at] = gp[at, cols].T
            return carry

        lax.fori_loop(0, padded // LANES, turn, 0)
        for c in later:
            c.wait()
        store_p.wait()

    up = u4[j]
    down = vv[pl.ds(pl.multiple_of(32 * j, 32), 32)].reshape(512, D)
    up_bias = rowv_ref[pl.ds(8 + j, 1), :]

    def products(k):
        at = slice(k * GR, k * GR + GR)
        return nn(h2[at, :], up) + up_bias, nt(gp[at, :], down)

    up_sum = jnp.zeros((1, 512), f32)
    ahead = products(0)
    for k in range(blocks):
        u, de = ahead
        if k + 1 < blocks:
            ahead = products(k + 1)
        at = slice(k * GR, k * GR + GR)
        cdf = 0.5 * lax.erf(u * RT2) + 0.5
        es[j, at, :] = (u * cdf).astype(bf16)
        du = de * (cdf + u * (PHI * jnp.exp2(u * u * (-0.5 * LOG2E))))
        dus[at, :] = du.astype(bf16)
        up_sum = up_sum + jnp.sum(du, axis=0, keepdims=True)
        dh2[at, :] += nt(dus[at, :], up)
    dbf1_ref[pl.ds(j, 1), :] = up_sum
    dU = nn(h2T[...], dus[...]).astype(bf16)
    dV = nn(gT[...], es[j]).astype(bf16).T
    if owners:
        at = pl.ds(pl.multiple_of(j * rpd, rpd), rpd)
        for k in range(owners):
            pk[(k ^ me) & 1, place_of(k ^ me, groups[1:]), at, :] = dU[rpd * k : rpd * k + rpd]
        per = 512 // (4 * rpd)
        for k in range(per):
            rel = (j * per + k) ^ me
            pk[rel & 1, place_of(rel, groups[1:]), 4 * rpd : 8 * rpd, :] = dV[4 * rpd * k : 4 * rpd * k + 4 * rpd]
        for c in grads_out(j):
            c.start()
    else:
        pk[0] = dU
        pk[1] = dV
        for c in grads_out(j):
            c.start()
        for c in grads_out(j):
            c.wait()

    @pl.when(j == last)
    def _():
        zero = jnp.zeros((1, D), f32)
        sums = [zero] * 4
        stats = [zero] * 5
        outs = []
        for k in range(blocks):
            at = slice(k * GR, k * GR + GR)
            m = mid[at, :]
            c = m - jnp.mean(m, axis=-1, keepdims=True)
            rs = lax.rsqrt(jnp.mean(c * c, axis=-1, keepdims=True) + 1e-5)
            xh = c * rs
            d = dh2[at, :]
            dx = d * gain
            dxx = d * xh
            m1 = jnp.mean(dx, axis=-1, keepdims=True)
            m2 = jnp.mean(dxx * gain, axis=-1, keepdims=True)
            grad = gp[at, :].astype(f32)
            dm = grad + (dx - m1 - xh * m2) * rs
            dh2[at, :] = dm
            outs.append(pltpu.make_async_copy(dh2.at[rows_of(k)], dmid_any.at[rows_of(k)], sem_m.at[k]))
            outs[-1].start()
            terms = (dm.astype(bf16).astype(f32), dxx, d, grad)
            sums = [a + jnp.sum(t, axis=0, keepdims=True) for a, t in zip(sums, terms)]
            f = rowv_ref[7:8, :]
            for b in range(4):
                f = f + nn(es[b, at, :], vv[32 * b : 32 * b + 32].reshape(512, D))
            out = m + f
            res[at, :] = out.astype(bf16)
            outs.append(pltpu.make_async_copy(res.at[rows_of(k)], res_any.at[rows_of(k)], sem_r.at[k]))
            outs[-1].start()
            vl = vld_ref[at, 0:1]
            x = xb[at, :].astype(f32)
            terms = (x * x * vl, m * m * vl, f * f * vl, out * out * vl, jnp.broadcast_to(vl, (GR, D)))
            stats = [a + jnp.sum(t, axis=0, keepdims=True) for a, t in zip(stats, terms)]
        for q in range(4):
            vec_ref[q : q + 1, :] = sums[q]
        vec_ref[4:8, :] = jnp.zeros((4, D), f32)
        dbf1_ref[4:8, :] = jnp.zeros((4, D), f32)
        for q, t in zip((0, 2, 3, 4, 5), stats):
            st_ref[q : q + 1, :] = t
        if owners:
            for step in range(last + 1):
                outs += grads_out(step)
        for c in outs:
            c.wait()


def mlp(me, x, o, g, vld, rowv, plan, pieces, rpd, owners, count, groups):
    rows = x.shape[0]
    blocks = rows // GR
    steps = FF // 512
    padded = -(-rows // LANES) * LANES
    copies = sum(1 if r is None else 3 * len(r) for r in plan)
    if owners:
        grad_shapes = [sds((count // 2, 8 * rpd, 512), bf16)] * 2
        pk = (2, count // 2, 8 * rpd, 512)
    else:
        grad_shapes = [sds((D, FF), bf16), sds((FF, D), bf16)]
        pk = (2, 512, 512)
    dma = pltpu.SemaphoreType.DMA
    return pl.pallas_call(
        functools.partial(mlp_body, plan=plan, rows=rows, owners=count if owners else 0, rpd=rpd, groups=groups),
        grid=(steps,),
        in_specs=[SMEM, whole((rows, LANES)), whole((16, D))] + any_specs(3 + len(pieces)),
        out_specs=any_specs(5) + [whole((8, D))] * 3,
        out_shape=[sds((rows, D), bf16), sds((rows, D), f32), sds((D, D), bf16)] + grad_shapes + [sds((8, D), f32)] * 3,
        scratch_shapes=[
            pltpu.VMEM((rows, D), bf16),
            pltpu.VMEM((rows, D), bf16),
            pltpu.VMEM((padded, D), bf16),
            pltpu.VMEM((D, padded), bf16),
            pltpu.VMEM((padded, D), bf16),
            pltpu.VMEM((D, padded), bf16),
            pltpu.VMEM((rows, D), f32),
            pltpu.VMEM((rows, D), f32),
            pltpu.VMEM((steps, padded, 512), bf16),
            pltpu.VMEM((padded, 512), bf16),
            pltpu.VMEM((steps, D, 512), bf16),
            pltpu.VMEM((FF // 16, 16, D), bf16),
            pltpu.VMEM((D, D), bf16),
            pltpu.VMEM((rows, D), bf16),
            pltpu.VMEM(pk, bf16),
            dma((copies,)),
            dma((blocks,)),
            dma((blocks,)),
            dma((1,)),
            dma((1,)),
            dma((steps, 2)),
            dma((steps, max(1, 512 // (4 * rpd)))),
            dma((blocks,)),
            dma((blocks,)),
        ],
        compiler_params=params(62),
        cost_estimate=pl.CostEstimate(flops=10**7, bytes_accessed=10**5, transcendentals=0),
        name="mlp",
    )(me, vld, rowv, x, o, g, *pieces)


def attn_bwd_body(me_ref, dmid_ref, p_ref, oT_ref, q_ref, kT_ref, v_ref, pT_ref, xT_ref, w_ref, rowv_ref, *refs, owners, rpd, groups):
    dm_ref, acc_ref, vec_ref = refs[:3]
    grads = refs[3:-6]
    xs, dap, don, doT, dw, dproj = refs[-6:]
    i = pl.program_id(0)

    @pl.when(i == 0)
    def _():
        acc_ref[...] = jnp.zeros_like(acc_ref)
        dw[...] = jnp.zeros_like(dw)
        dproj[...] = jnp.zeros_like(dproj)

    xs[0:GR, :] = dmid_ref[...]
    for w in range(GW):
        dap[LANES * w : LANES * w + LANES, :] = pad_window(xs[CELLS * w : CELLS * w + 104, :])
        dm_ref[LANES * w + KP : LANES * w + LANES, :] = jnp.zeros((LANES - KP, 3 * D), bf16)
    da = dap[...]
    don[...] = nt(da, p_ref[...]).astype(bf16)
    dproj[...] += nn(oT_ref[...], da)
    for w in range(GW):
        for a in range(D // LANES):
            rows, cols = slice(LANES * w, LANES * w + LANES), slice(LANES * a, LANES * a + LANES)
            doT[cols, rows] = don[rows, cols].T
    factor = HD**-0.5

    def window(w, carry):
        start = pl.multiple_of(w * LANES, LANES)
        at = pl.ds(start, LANES)
        keys = pl.ds(start, KP)
        for g in range(4):
            c0 = LANES * g
            cols = slice(c0, c0 + LANES)
            dp = nn(by_head(v_ref[keys, cols]), doT[cols, at])
            dss = []
            for q in range(4):
                h = 4 * g + q
                head = slice(HD * h, HD * h + HD)
                delta = jnp.sum(doT[head, at].astype(f32) * oT_ref[head, at].astype(f32), axis=0, keepdims=True)
                ds = pT_ref[w, h].astype(f32) * (dp[KP * q : KP * q + KP] - delta)
                acc_ref[h] += ds
                dss.append(ds.astype(bf16))
            dq = [nn(kT_ref[c0 + HD * q : c0 + HD * q + HD, at][:, 0:KP], dss[q]) for q in range(4)]
            dm_ref[at, cols] = (jnp.concatenate(dq, axis=0) * factor).astype(bf16).T
            dk = nn(jnp.concatenate(dss, axis=1), by_head(q_ref[at, cols])) * factor
            dm_ref[keys, D + c0 : D + c0 + LANES] = dk.astype(bf16)
            dv = nn(jnp.concatenate([pT_ref[w, 4 * g + q] for q in range(4)], axis=1), by_head(don[at, cols]))
            dm_ref[keys, 2 * D + c0 : 2 * D + c0 + LANES] = dv.astype(bf16)
        return carry

    lax.fori_loop(0, GW, window, 0, unroll=4)
    dw[...] += nn(xT_ref[...], dm_ref[...])

    @pl.when(i == pl.num_programs(0) - 1)
    def _():
        s = dw[D : D + 1, :]
        vec_ref[...] = jnp.zeros_like(vec_ref)
        vec_ref[0:1, :] = s
        for a in range(D // LANES):
            rows = slice(LANES * a, LANES * a + LANES)
            col = rowv_ref[0:8, rows].T
            x = dw[rows, :]
            wt = w_ref[rows, :].astype(f32)
            by_gain = jnp.broadcast_to(jnp.sum(wt * x, axis=1, keepdims=True), (LANES, LANES)).T
            by_shift = jnp.broadcast_to(jnp.sum(wt * s, axis=1, keepdims=True), (LANES, LANES)).T
            vec_ref[1:2, rows] = by_gain[0:1]
            vec_ref[2:3, rows] = by_shift[0:1]
            dw[rows, :] = col[:, 0:1] * x + col[:, 1:2] * s
        if owners:
            me = me_ref[0]
            for k in range(owners):
                rel = k ^ me
                pos = place_of(rel, groups[1:])
                mine = slice(rpd * k, rpd * k + rpd)

                def store(to, mine=mine, pos=pos):
                    for q in range(3):
                        to[pos, rpd * q : rpd * q + rpd, :] = dw[mine, D * q : D * q + D].astype(bf16)
                    to[pos, 3 * rpd : 4 * rpd, :] = dproj[mine, :].astype(bf16)

                pl.when(rel & 1 == 0)(functools.partial(store, grads[0]))
                pl.when(rel & 1 == 1)(functools.partial(store, grads[1]))
        else:
            grads[0][...] = dw[0:D, :].astype(bf16)
            grads[1][...] = dproj[...].astype(bf16)


def attn_bwd(me, dmid, p, oT, q, kT, v, pT, xT, w, rowv, rpd, owners, count, groups):
    n = q.shape[0] // GL

    def tb(r):
        return pl.BlockSpec((r, GL), lambda i: (0, i))

    pb = pl.BlockSpec((GL, D), lambda i: (i, 0))
    if owners:
        grad_shapes = [sds((count // 2, 4 * rpd, D), bf16)] * 2
    else:
        grad_shapes = [sds((D, 3 * D), bf16), sds((D, D), bf16)]
    return pl.pallas_call(
        functools.partial(attn_bwd_body, owners=count if owners else 0, rpd=rpd, groups=groups),
        grid=(n,),
        in_specs=[SMEM, pl.BlockSpec((GR, D), lambda i: (i, 0)), whole((D, D)), tb(D), pb, tb(D), pb, pl.BlockSpec((GW, HEADS, KP, LANES), lambda i: (i, 0, 0, 0)), tb(D + 16), whole((D, 3 * D)), whole((16, D))],
        out_specs=[pl.BlockSpec((GL, 3 * D), lambda i: (i, 0)), whole((HEADS, KP, LANES)), whole((8, 3 * D))] + [whole(s.shape) for s in grad_shapes],
        out_shape=[sds((n * GL, 3 * D), bf16), sds((HEADS, KP, LANES), f32), sds((8, 3 * D), f32)] + grad_shapes,
        scratch_shapes=[
            pltpu.VMEM((GR + 8, D), f32),
            pltpu.VMEM((GL, D), bf16),
            pltpu.VMEM((GL, D), bf16),
            pltpu.VMEM((D, GL), bf16),
            pltpu.VMEM((D + 16, 3 * D), f32),
            pltpu.VMEM((D, D), f32),
        ],
        compiler_params=params(60),
        cost_estimate=pl.CostEstimate(flops=10**7, bytes_accessed=10**5, transcendentals=0),
        name="attn_bwd",
    )(me, dmid, p, oT, q, kT, v, pT, xT, w, rowv)


def grad_in_body(dm_ref, w_ref, x_ref, dmid_ref, rowv_ref, tg_ref, dsc):
    dh = nt(dm_ref[...], w_ref[...])
    for w in range(GW):
        dsc[CELLS * w : CELLS * w + 104, :] = dh[LANES * w : LANES * w + 104]
    x = x_ref[...].astype(f32)
    c = x - jnp.mean(x, axis=-1, keepdims=True)
    rs = lax.rsqrt(jnp.mean(c * c, axis=-1, keepdims=True) + 1e-5)
    xh = c * rs
    dx = dsc[0:GR, :] * rowv_ref[0:1, :]
    m1 = jnp.mean(dx, axis=-1, keepdims=True)
    m2 = jnp.mean(dx * xh, axis=-1, keepdims=True)
    tg_ref[...] = dmid_ref[...] + (dx - m1 - xh * m2) * rs


def grad_in(dm, w, x, dmid, rowv):
    n = x.shape[0] // GR
    rb = pl.BlockSpec((GR, D), lambda i: (i, 0))
    return pl.pallas_call(
        grad_in_body,
        grid=(n,),
        in_specs=[pl.BlockSpec((GL, 3 * D), lambda i: (i, 0)), whole((D, 3 * D)), rb, rb, whole((16, D))],
        out_specs=rb,
        out_shape=sds((n * GR, D), f32),
        scratch_shapes=[pltpu.VMEM((GR + 8, D), f32)],
        compiler_params=params(60),
        cost_estimate=pl.CostEstimate(flops=10**7, bytes_accessed=10**5, transcendentals=0),
        name="grad_in",
    )(dm, w, x, dmid, rowv)


SMALL = 24
SENT = 32


def to_send(small):
    lane = lax.broadcasted_iota(jnp.int32, small.shape, 1)
    lane = jnp.where(lax.broadcasted_iota(jnp.int32, small.shape, 0) >= 8, lane, -1)
    small = jnp.where(lane == RELN, small + pltpu.roll(small, D - 1, 1), small)
    hi = small.astype(bf16).astype(f32)
    small = jnp.where(lane == RELN + 1, pltpu.roll(small - hi, 1, 1), hi)
    return jnp.concatenate([small, jnp.zeros((SENT - SMALL, D), f32)], axis=0).astype(bf16)


def sent_sums(terms):
    got = [t.astype(f32)[0:SMALL] for t in terms]
    while len(got) > 1:
        got = [got[k] + got[k + 1] for k in range(0, len(got), 2)]
    return got[0]


def fold_body(*refs, first, terms, parts):
    ins, outs = refs[: 2 * terms if first else terms + 1], refs[2 * terms if first else terms + 1 :]
    nb, rows = ins[0].shape[0], ins[0].shape[1]
    n = nb // (parts + 1)
    if first:
        small = ins[2][...] + ins[3][...]
    else:
        small = sent_sums([ins[1][...]] + [r[nb * rows :, :] for r in ins[2:]])
    for p in range(parts + 1):
        at = slice(p * n, p * n + n)
        total = ins[0][at].astype(f32)
        if first:
            total = total + ins[1][at].astype(f32)
        else:
            for r in ins[2:]:
                total = total + r[p * n * rows : (p + 1) * n * rows, :].astype(f32).reshape(n, rows, D)
        if p == 0:
            outs[0][...] = total
            outs[1][...] = to_send(small)
        else:
            outs[p + 1][0 : n * rows, :] = total.reshape(n * rows, D).astype(bf16)
            outs[p + 1][n * rows :, :] = to_send(small)


def fold(arrays, parts, first=False):
    terms = 2 if first else len(arrays) - 1
    nb, rows = arrays[0].shape[:2]
    n = nb // (parts + 1)
    return pl.pallas_call(
        functools.partial(fold_body, first=first, terms=terms, parts=parts),
        out_shape=[sds((n, rows, D), f32), sds((SENT, D), bf16)] + [sds((n * rows + SENT, D), bf16)] * parts,
        compiler_params=params(16),
        cost_estimate=pl.CostEstimate(flops=10**6, bytes_accessed=10**5, transcendentals=0),
        name="fold",
    )(*arrays)


def add_body(*refs, terms, later):
    ins, outs = refs[:terms], refs[terms : -2] if later else refs[terms:]
    n = outs[0].shape[0]
    copies = []
    if later:
        buf, sem = refs[-2:]
        for p in range(len(outs)):
            at = pl.ds(p * n, n)
            copies.append(pltpu.make_async_copy(ins[0].at[at], buf.at[at], sem.at[p]))
        for c in copies:
            c.start()
        ins = (buf,) + ins[1:]
    for p, out in enumerate(outs):
        if later:
            copies[p].wait()
        at = slice(p * n, p * n + n)
        total = ins[0][at].astype(f32)
        for r in ins[1:]:
            total = total + r[at].astype(f32)
        out[...] = total.astype(out.dtype)


def add_split(terms, group, later=False):
    parts = len(masks_of(group))
    first = terms[0]
    n = first.shape[0] // (parts + 1)
    shape = (n,) + first.shape[1:]
    vmem = pl.BlockSpec(memory_space=pltpu.VMEM)
    out = pl.pallas_call(
        functools.partial(add_body, terms=len(terms), later=later),
        in_specs=[pl.BlockSpec(memory_space=pl.ANY) if later else vmem] + [vmem] * (len(terms) - 1),
        out_shape=[sds(shape, f32)] + [sds(shape, bf16)] * parts,
        scratch_shapes=[pltpu.VMEM(first.shape, first.dtype), pltpu.SemaphoreType.DMA((parts + 1,))] if later else [],
        compiler_params=params(16),
        cost_estimate=pl.CostEstimate(flops=10**6, bytes_accessed=10**5, transcendentals=0),
        name="add_split",
    )(*terms)
    return out[0], out[1:]


def spread(o_ref, block, width, at):
    each = width // LANES
    for b in range(block.shape[1] // LANES):
        o_ref[pl.ds(at // LANES + b, block.shape[0], stride=each), :] = block[:, LANES * b : LANES * b + LANES]


def attn_last_body(me_ref, own_ref, kept_ref, *refs, rpd, per):
    got_refs, (qkv_ref, proj_ref, vec_ref, table_ref, stats_ref, lines) = refs[:-6], refs[-6:]
    rows = 4 * rpd
    total = own_ref[0]
    for r in got_refs:
        total = total + r[0:rows, :].astype(f32)
    for q in range(3):
        spread(qkv_ref, total[rpd * q : rpd * q + rpd], 3 * D, D * q)
    spread(proj_ref, total[3 * rpd : rows], D, 0)
    small = sent_sums([kept_ref[...]] + [r[rows:, :] for r in got_refs])
    for k in range(8):
        for a in range(4):
            lines[4 * k + a : 4 * k + a + 1, :] = small[k : k + 1, LANES * a : LANES * a + LANES]
    lines[32:48, :] = small[8:24, RP:D]
    if per % 64:
        vec_ref[...] = lines[...]
    else:
        low = lax.broadcasted_iota(jnp.int32, (1, LANES), 1) < 64
        for p in range(0, per // 64, 2):
            halves = []
            for k in range(2):
                c = me_ref[0] * (per // 64) + min(p + k, per // 64 - 1)
                line = lines[pl.ds(c >> 1, 1), :]
                halves.append(jnp.where(c & 1 == k, line, pltpu.roll(line, 64, 1)))
            vec_ref[p // 2 : p // 2 + 1, :] = jnp.where(low, halves[0], halves[1])
    turned = small[8:24, 0:RP].T
    table_ref[...] = turned[0:RELN]
    line = turned[RELN : RELN + 1] + turned[RELN + 1 : RELN + 2]
    stats_ref[...] = jnp.sqrt(line / line[:, 5:6] + 1e-06)


def attn_last(me, arrays, rpd, per):
    lines = -(-per // LANES) if per % 64 == 0 else 48
    return pl.pallas_call(
        functools.partial(attn_last_body, rpd=rpd, per=per),
        in_specs=[SMEM] + [pl.BlockSpec(memory_space=pltpu.VMEM)] * len(arrays),
        out_shape=[sds((12 * rpd, LANES), f32), sds((4 * rpd, LANES), f32), sds((lines, LANES), f32), sds((RELN, HEADS), f32), sds((1, HEADS), f32)],
        scratch_shapes=[pltpu.VMEM((48, LANES), f32)],
        compiler_params=params(16),
        cost_estimate=pl.CostEstimate(flops=10**6, bytes_accessed=10**5, transcendentals=0),
        name="attn_last",
    )(me, *arrays)


def mlp_last_body(own_ref, *refs, rpd):
    total = own_ref[0]
    for r in refs[:-2]:
        total = total + r[0].astype(f32)
    for q in range(4):
        spread(refs[-2], total[rpd * q : rpd * q + rpd], FF, 512 * q)
    spread(refs[-1], total[4 * rpd :], D, 0)


def mlp_last(arrays, rpd):
    return pl.pallas_call(
        functools.partial(mlp_last_body, rpd=rpd),
        out_shape=[sds((16 * rpd, LANES), f32)] * 2,
        compiler_params=params(16),
        cost_estimate=pl.CostEstimate(flops=10**6, bytes_accessed=10**5, transcendentals=0),
        name="mlp_last",
    )(*arrays)


def place_hits(shape, axis, rev=0):
    c = lax.broadcasted_iota(jnp.int32, shape, 1 - axis)
    code = jnp.where(c < CELLS, (2 * WSIDE - 1) * (c // WSIDE) + c % WSIDE, -1000)
    if rev:
        code = rev - code
    return jnp.where(code == lax.broadcasted_iota(jnp.int32, shape, axis), 1.0, 0.0).astype(bf16)


def rel_bias_body(t_ref, o_ref):
    keys = place_hits((KP, 192), 1)
    queries = place_hits((256, LANES), 0)

    def head(h, carry):
        row = pltpu.roll(jnp.broadcast_to(t_ref[pl.ds(h, 1), :], (8, RP)), 0, 1, stride=1, stride_axis=0)
        t = jnp.concatenate([pltpu.roll(row, (8 * k - 180) % RP, 1)[:, 0:256] for k in range(24)], axis=0)
        hi = t.astype(bf16)
        lo = (t - hi.astype(f32)).astype(bf16)
        b = nn(jnp.concatenate([hi, lo], axis=0), queries).astype(bf16)
        b = nn(keys, jnp.concatenate([b[0:192], b[192:384]], axis=1))
        o_ref[h] = b[:, 0:LANES] + b[:, LANES : 2 * LANES]
        return carry

    lax.fori_loop(0, HEADS, head, 0, unroll=8)


def rel_bias(table):
    return pl.pallas_call(
        rel_bias_body,
        out_shape=sds((HEADS, KP, LANES), f32),
        compiler_params=params(16),
        cost_estimate=pl.CostEstimate(flops=2 * 10**10, bytes_accessed=10**6, transcendentals=0),
        name="rel_bias",
    )(table)


def rel_grad_body(a_ref, one_ref, two_ref, up_ref, squares_ref, o_ref):
    keys = place_hits((192, KP), 0, 191)
    queries = place_hits((LANES, 256), 1)
    zero = jnp.zeros((8, RP - 256), f32)
    o_ref[0:2, :] = one_ref[1:3, 0:D]
    o_ref[2:3, :] = one_ref[0:1, 0:D]
    o_ref[3:4, :] = one_ref[0:1, 2 * D : 3 * D]
    o_ref[4:8, :] = two_ref[0:4, :]

    def head(h, carry):
        a = a_ref[h]
        hi = a.astype(bf16)
        lo = (a - hi.astype(f32)).astype(bf16)
        b = nn(keys, jnp.concatenate([hi, lo], axis=1)).astype(bf16)
        b = nn(jnp.concatenate([b[:, 0:LANES], b[:, LANES : 2 * LANES]], axis=0), queries)
        b = b[0:192] + b[192:384]
        t = jnp.zeros((8, RP), f32)
        for k in range(24):
            t = t + pltpu.roll(jnp.concatenate([b[8 * k : 8 * k + 8], zero], axis=1), (8 * k - 11) % RP, 1)
        t = pltpu.roll(t, 0, 1, stride=1, stride_axis=0)
        o_ref[pl.ds(8 + h, 1), 0:RP] = jnp.sum(t, axis=0, keepdims=True)
        return carry

    lax.fori_loop(0, HEADS, head, 0, unroll=16)
    for k in range(4):
        for a in range(4):
            o_ref[8 + 4 * k + a : 9 + 4 * k + a, RP:D] = up_ref[k : k + 1, LANES * a : LANES * a + LANES]
    for k in range(6):
        o_ref[8 + k : 9 + k, RELN : RELN + 1] = jnp.sum(squares_ref[k : k + 1, :], axis=1, keepdims=True)
        o_ref[8 + k : 9 + k, RELN + 1 : RELN + 2] = jnp.zeros((1, 1), f32)


def rel_grad(acc, one, two, up, squares):
    return pl.pallas_call(
        rel_grad_body,
        out_shape=sds((SMALL, D), f32),
        compiler_params=params(16),
        cost_estimate=pl.CostEstimate(flops=10**7, bytes_accessed=10**5, transcendentals=0),
        name="rel_grad",
    )(acc, one, two, up, squares)


def shards(tokens, cotangent, regions, validity, qkv_weight, proj_weight, fc1_weight, fc2_weight, vectors, rel_table, *, count, inner):
    rows = tokens.shape[0]
    groups = bit_groups(count)
    single = groups[:2] + [(b,) for g in groups[2:] for b in g]
    rpd = D // count
    direct = rpd % 16 == 0
    me = lax.axis_index("dp") * inner + lax.axis_index("shard")
    me_s = me.astype(jnp.int32).reshape(1)

    per = vectors.shape[0]
    if direct:
        own = jnp.pad(vectors, (0, rpd * LANES - per)).reshape(rpd, LANES)
        own = jnp.concatenate([qkv_weight.reshape(rpd, 3 * D), own], axis=1)
    else:
        own = jnp.concatenate([qkv_weight, vectors]).reshape(1, -1)
    rels, attn_up = gather_upper(own, groups, count)
    packed = jnp.concatenate(
        [
            proj_weight.reshape(1, rpd, D),
            fc1_weight.reshape(rpd, 4, 512).transpose(1, 0, 2),
            fc2_weight.reshape(4, rpd, D),
        ],
        axis=0,
    )
    packed = packed.reshape(9 * rpd, D)
    attn_pieces = gather_plane(rels, attn_up, groups, count)
    table_in = after(rel_table, attn_up)
    mlp_rels, mlp_up = gather_upper(packed, single, count, attn_up)

    bias = rel_bias(jnp.pad(table_in.T * LOG2E, ((0, 0), (0, RP - RELN))))
    reg = regions.reshape(-1, GW, CELLS).astype(f32)
    key_code = jnp.where(validity.reshape(-1, GW, CELLS) == 1, reg, -2.0)
    codes = jnp.pad(jnp.concatenate([reg, key_code], axis=1), ((0, 0), (0, 0), (0, LANES - CELLS)), constant_values=-3.0)

    attn_pieces = hold(attn_pieces, bias, codes)
    mlp_up = after(mlp_up, bias, codes, [a for _, a in attn_pieces])
    attn_pieces = gather_core(attn_pieces, count)
    mlp_pieces = gather_plane(mlp_rels, mlp_up, groups, count)
    if direct:
        attn_plan = [r for r, _ in attn_pieces]
        attn_w = [a for _, a in attn_pieces]
    else:
        attn_plan = [None] * 2
        both = natural_order(attn_pieces, me, count).reshape(count, -1)
        attn_w = [both[:, : 3 * D * rpd].reshape(D, 3 * D), jnp.pad(both[:, 3 * D * rpd :].astype(f32).reshape(12, D), ((0, 4), (0, 0)))]

    x = after(tokens, mlp_up)
    oT, o, q, kT, v, pT, xT, vld, w_full, rowv = attn_fwd(me_s, x, codes, bias, attn_plan, attn_w, rpd, per, count)

    mlp_pieces = gather_core(hold(mlp_pieces, o), count)
    if direct:
        mlp_plan = [r for r, _ in mlp_pieces]
        mlp_w = [a.reshape(-1, 9, rpd, D) for _, a in mlp_pieces]
    else:
        both = natural_order(mlp_pieces, me, count).reshape(count, 9, rpd, D)
        mlp_plan = [None] * 3
        mlp_w = [both[:, 0].reshape(D, D), both[:, 1:5].transpose(1, 0, 2, 3).reshape(4, D, 512), both[:, 5:].reshape(128, 16, D)]
    result, dmid, p_full, mlp_keep, mlp_send, vec_two, dbf1, squares = mlp(
        me_s, tokens, o, cotangent, vld, rowv, mlp_plan, mlp_w, rpd, direct, count, single
    )
    order = None
    if not direct:
        blocks = jnp.arange(count)
        order, mlp_order = (
            jnp.zeros((count,), jnp.int32).at[place_of(blocks, way)].set(blocks.astype(jnp.int32)) ^ me for way in (groups, single)
        )
        dU = mlp_keep.reshape(count, rpd, 4, 512).transpose(0, 2, 1, 3).reshape(count, 4 * rpd, 512)
        pk = jnp.take(jnp.concatenate([dU, mlp_send.reshape(count, 4 * rpd, D)], axis=1), mlp_order, axis=0)
        mlp_keep, mlp_send = pk[: count // 2], pk[count // 2 :]

    other = swap(mlp_send, 1, count)
    mlp_own, parts = add_split([mlp_keep, other], groups[1], later=True)
    mlp_got = send_parts(parts, groups[1], count)
    dmid = after(dmid, parts)
    got = attn_bwd(me_s, dmid, p_full, oT, q, kT, v, pT, xT, w_full, rowv, rpd, direct, count, groups)
    dm, score_sums, vec_one = got[:3]
    if direct:
        attn_keep, attn_send = got[3:]
    else:
        dW = got[3].reshape(count, rpd, 3, D).transpose(0, 2, 1, 3).reshape(count, 3 * rpd, D)
        pk = jnp.take(jnp.concatenate([dW, got[4].reshape(count, rpd, D)], axis=1), order, axis=0)
        attn_keep, attn_send = pk[: count // 2], pk[count // 2 :]
    mlp_got, attn_send, score_sums, dm = lax.optimization_barrier((mlp_got, attn_send, score_sums, dm))

    other = swap(attn_send, 1, count)
    mlp_terms = [mlp_own] + mlp_got
    for g in single[2:3]:
        mlp_own, parts = add_split(mlp_terms, g)
        mlp_terms = [mlp_own] + send_parts(parts, g, count)
        score_sums = after(score_sums, parts)
    small = rel_grad(score_sums, vec_one, vec_two, dbf1, squares)
    other = after(other, small)
    levels = [len(masks_of(g)) for g in groups[1:]]
    out = fold([attn_keep, other, small, swap(small, 1, count)], levels[0], first=True)
    for k, g in enumerate(groups[1:]):
        own, kept, parts = out[0], out[1], out[2:]
        sent = send_parts(parts, g, count)
        if k == 0:
            mlp_terms = after(mlp_terms, parts)
            for up in single[3:]:
                mlp_own, parts = add_split(mlp_terms, up)
                mlp_terms = [mlp_own] + send_parts(parts, up, count)
            dm = after(dm, parts)
            grad_tokens = grad_in(dm, w_full, tokens, dmid, rowv)
            sent, mlp_terms = after((sent, mlp_terms), grad_tokens)
        if k + 1 < len(levels):
            out = fold([own, kept] + sent, levels[k + 1])
            mlp_terms = after(mlp_terms, out)
    grad_fc1, grad_fc2 = mlp_last(mlp_terms, rpd)
    sent = after(sent, grad_fc1)
    grad_qkv, grad_proj, grad_vectors, grad_table, stats = attn_last(me_s, [own, kept] + sent, rpd, per)
    if per % 64 == 0:
        grad_vectors = grad_vectors.reshape(-1)[:per]
    else:
        grad_vectors = lax.dynamic_slice(grad_vectors.reshape(-1), (me * per,), (per,))
    return (
        result,
        grad_tokens,
        grad_qkv.reshape(-1),
        grad_proj.reshape(-1),
        grad_fc1.reshape(-1),
        grad_fc2.reshape(-1),
        grad_vectors,
        grad_table,
        stats[0, 0:5],
    )


def solution(mesh):
    flat = P(AXES)
    tall = P(AXES, None)
    in_specs = (tall, tall, flat, flat, flat, flat, flat, flat, flat, P())
    out_specs = (tall, tall, flat, flat, flat, flat, flat, P(), P())
    inner = mesh.shape["shard"]
    body = functools.partial(shards, count=mesh.shape["dp"] * inner, inner=inner)
    return jax.shard_map(body, mesh=mesh, in_specs=in_specs, out_specs=out_specs, check_vma=False)
```

```python
import functools

import jax
import jax.numpy as jnp
from jax import lax
from jax.experimental import pallas as pl
from jax.experimental.pallas import tpu as pltpu
from jax.sharding import PartitionSpec as P

D = 512
FF = 2048
HEADS = 16
HD = 32
WSIDE = 10
RELN = 361
CELLS = WSIDE * WSIDE
GW = 4
GR = GW * CELLS
KP = 112
LANES = 128
GL = GW * LANES
RP = 384
AXES = ("dp", "shard")
LOG2E = 1.4426950408889634
NEG = -1e9
RT2 = 0.7071067811865476
PHI = 0.3989422804014327
f32 = jnp.float32
bf16 = jnp.bfloat16
sds = jax.ShapeDtypeStruct


def nn(a, b):
    return lax.dot_general(a, b, (((1,), (0,)), ((), ())), preferred_element_type=f32)


def nt(a, b):
    return lax.dot_general(a, b, (((1,), (1,)), ((), ())), preferred_element_type=f32)


def tn(a, b):
    return lax.dot_general(a, b, (((0,), (0,)), ((), ())), preferred_element_type=f32)


def whole(shape):
    return pl.BlockSpec(shape, lambda i: (0,) * len(shape))


def params(mib):
    return pltpu.CompilerParams(vmem_limit_bytes=mib * 2**20)


def bit_groups(count):
    bits = count.bit_length() - 1
    groups = [(0,)]
    at = 1
    while at < bits:
        groups.append(tuple(range(at, min(at + 2, bits))))
        at += 2
    return groups


def masks_of(group):
    return [sum(((v >> k) & 1) << b for k, b in enumerate(group)) for v in range(1, 1 << len(group))]


def swap(x, mask, count):
    return lax.ppermute(x, AXES, [(i, i ^ mask) for i in range(count)])


def place_of(rel, groups):
    pos = 0
    for g in groups:
        pos = pos * (1 << len(g)) + ((rel >> g[0]) & ((1 << len(g)) - 1))
    return pos


def after(values, *others):
    return lax.optimization_barrier((values, others))[0]


def gather_upper(x, groups, count, *others):
    cur = x[None]
    rels = [0]
    for k, g in enumerate(groups[:1:-1]):
        if k and others:
            cur = after(cur, *others)
        ms = masks_of(g)
        cur = jnp.concatenate([cur] + [swap(cur, m, count) for m in ms], axis=0)
        rels = [r ^ m for m in [0] + ms for r in rels]
    return rels, cur


def gather_plane(rels, cur, groups, count):
    return [(rels, cur)] + [([r ^ m for r in rels], swap(cur, m, count)) for m in masks_of(groups[1])]


def gather_core(pieces, count):
    return pieces + [([r ^ 1 for r in rels], swap(arr, 1, count)) for rels, arr in pieces]


def hold(pieces, *others):
    held = after([a for _, a in pieces[1:]], *others)
    return pieces[:1] + [(r, a) for (r, _), a in zip(pieces[1:], held)]


def natural_order(pieces, me, count):
    rels = [r for rs, _ in pieces for r in rs]
    where = [0] * count
    for k, r in enumerate(rels):
        where[r] = k
    both = jnp.concatenate([a for _, a in pieces], axis=0)
    return jnp.take(both, jnp.asarray(where, jnp.int32)[jnp.arange(count) ^ me], axis=0)


def send_parts(parts, group, count):
    return [swap(p, m, count) for p, m in zip(parts, masks_of(group))]


def lay_vectors(raw, per, rowv_ref):
    unit = LANES // 2
    each = per // unit
    low = lax.broadcasted_iota(jnp.int32, (1, LANES), 1) < unit

    def half(c, high):
        owner, part = divmod(c, each)
        got = raw[owner, part // 2 : part // 2 + 1, :].astype(f32)
        return got if part % 2 == high else pltpu.roll(got, unit, 1)

    for m in range((8 * D + FF) // LANES):
        row, col = divmod(m * LANES, D)
        rowv_ref[row : row + 1, col : col + LANES] = jnp.where(low, half(2 * m, 0), half(2 * m + 1, 1))


def pad_window(rows):
    at = lax.broadcasted_iota(jnp.int32, (104, 1), 0)
    rows = jnp.where(at < CELLS, rows, 0.0)
    return jnp.concatenate([rows, jnp.zeros((LANES - 104, rows.shape[1]), f32)], axis=0).astype(bf16)


def head_lanes():
    return lax.broadcasted_iota(jnp.int32, (1, LANES), 1) // HD


def by_head(block):
    lane = head_lanes()
    return jnp.concatenate([jnp.where(lane == q, block, jnp.zeros_like(block)) for q in range(4)], axis=0)


def attn_fwd_body(me_ref, x_ref, code_ref, bias_ref, *refs, plan, rpd, per):
    pieces = refs[: len(plan)]
    (oT_ref, o_ref, q_ref, kT_ref, v_ref, pT_ref, xT_ref, vld_ref, w_ref, rowv_ref) = refs[len(plan) : len(plan) + 10]
    xs, h1p, qT, kn, vT, osc, vsc, mask_ref, raw, sem = refs[len(plan) + 10 :]

    @pl.when(pl.program_id(0) == 0)
    def _():
        copies = []
        for ref, rels in zip(pieces, plan):
            if rels is None:
                copies.append(pltpu.make_async_copy(ref, (w_ref, rowv_ref)[len(copies)], sem.at[len(copies)]))
                continue
            for t, r in enumerate(rels):
                at = pl.multiple_of((r ^ me_ref[0]) * rpd, rpd)
                copies.append(
                    pltpu.make_async_copy(
                        ref.at[t, :, pl.ds(0, 3 * D)], w_ref.at[pl.ds(at, rpd), :], sem.at[len(copies)]
                    )
                )
                copies.append(
                    pltpu.make_async_copy(ref.at[t, :, pl.ds(3 * D, LANES)], raw.at[r ^ me_ref[0]], sem.at[len(copies)])
                )
        for c in copies:
            c.start()
        for c in copies:
            c.wait()
        if plan[0] is not None:
            rowv_ref[12:16, :] = jnp.zeros((4, D), f32)
            lay_vectors(raw, per, rowv_ref)

    xs[0:GR, :] = x_ref[...].astype(f32)
    gain = rowv_ref[0:1, :]
    shift = rowv_ref[1:2, :]
    for w in range(GW):
        xw = xs[CELLS * w : CELLS * w + 104, :]
        c = xw - jnp.mean(xw, axis=-1, keepdims=True)
        var = jnp.mean(c * c, axis=-1, keepdims=True)
        xh = c * lax.rsqrt(var + 1e-5)
        h1p[LANES * w : LANES * w + LANES, :] = pad_window(xh * gain + shift)
        xh = pad_window(xh)
        for a in range(D // LANES):
            xT_ref[LANES * a : LANES * a + LANES, LANES * w : LANES * w + LANES] = xh[:, LANES * a : LANES * a + LANES].T
    xT_ref[D : D + 16, :] = jnp.ones((16, GL), bf16)
    turned = code_ref[0].T
    keys = lax.broadcasted_iota(jnp.int32, (KP, LANES), 0)
    same = (keys == lax.broadcasted_iota(jnp.int32, (KP, LANES), 1)) & (keys < CELLS)
    for w in range(GW):
        of_key = turned[:, GW + w : GW + w + 1]
        equal = jnp.broadcast_to(of_key[0:KP], (KP, LANES)) == jnp.broadcast_to(code_ref[0, w : w + 1, :], (KP, LANES))
        mask_ref[w] = jnp.where(equal | same, 0.0, NEG)
        vsc[CELLS * w : CELLS * w + 104, :] = jnp.broadcast_to(jnp.where(of_key[0:104] >= 0.0, 1.0, 0.0), (104, LANES))
    vld_ref[...] = vsc[0:GR, :]
    hp = h1p[...]
    q_ref[...] = (nn(hp, w_ref[:, 0:D]) + rowv_ref[2:3, :]).astype(bf16)
    kn[...] = nn(hp, w_ref[:, D : 2 * D]).astype(bf16)
    v_ref[...] = (nn(hp, w_ref[:, 2 * D : 3 * D]) + rowv_ref[3:4, :]).astype(bf16)
    for src, dst in ((q_ref, qT), (kn, kT_ref), (v_ref, vT)):
        for w in range(GW):
            for a in range(D // LANES):
                rows, cols = slice(LANES * w, LANES * w + LANES), slice(LANES * a, LANES * a + LANES)
                dst[cols, rows] = src[rows, cols].T
    factor = HD**-0.5 * LOG2E

    def window(w, carry):
        start = pl.multiple_of(w * LANES, LANES)
        at = pl.ds(start, LANES)
        allowed = mask_ref[w]
        for g in range(4):
            cols = slice(LANES * g, LANES * g + LANES)
            s = nn(by_head(kn[pl.ds(start, KP), cols]), qT[cols, at])
            ps = []
            for q in range(4):
                h = 4 * g + q
                t = s[KP * q : KP * q + KP] * factor + bias_ref[h] + allowed
                e = jnp.exp2(t - jnp.max(t, axis=0, keepdims=True))
                p = (e * (1.0 / jnp.sum(e, axis=0, keepdims=True))).astype(bf16)
                pT_ref[w, h] = p
                ps.append(p)
            o = [nn(vT[LANES * g + HD * q : LANES * g + HD * q + HD, at][:, 0:KP], ps[q]) for q in range(4)]
            oT_ref[cols, at] = jnp.concatenate(o, axis=0).astype(bf16)
        return carry

    lax.fori_loop(0, GW, window, 0, unroll=4)
    for w in range(GW):
        for a in range(D // LANES):
            osc[CELLS * w : CELLS * w + 104, LANES * a : LANES * a + LANES] = (
                oT_ref[LANES * a : LANES * a + LANES, LANES * w : LANES * w + LANES].T[0:112].astype(f32)[0:104]
            )
    o_ref[...] = osc[0:GR, :].astype(bf16)


def any_specs(n):
    return [pl.BlockSpec(memory_space=pl.ANY)] * n


SMEM = pl.BlockSpec(memory_space=pltpu.SMEM)


def attn_fwd(me, x, codes, bias, plan, pieces, rpd, per, count):
    n = x.shape[0] // GR
    copies = sum(1 if r is None else 2 * len(r) for r in plan)
    rb = pl.BlockSpec((GR, D), lambda i: (i, 0))
    tb = pl.BlockSpec((D, GL), lambda i: (0, i))
    pb = pl.BlockSpec((GL, D), lambda i: (i, 0))
    return pl.pallas_call(
        functools.partial(attn_fwd_body, plan=plan, rpd=rpd, per=per),
        grid=(n,),
        in_specs=[SMEM, rb, pl.BlockSpec((1, 2 * GW, LANES), lambda i: (i, 0, 0)), whole((HEADS, KP, LANES))]
        + any_specs(len(pieces)),
        out_specs=[
            tb,
            rb,
            pb,
            tb,
            pb,
            pl.BlockSpec((GW, HEADS, KP, LANES), lambda i: (i, 0, 0, 0)),
            pl.BlockSpec((D + 16, GL), lambda i: (0, i)),
            pl.BlockSpec((GR, LANES), lambda i: (i, 0)),
            whole((D, 3 * D)),
            whole((16, D)),
        ],
        out_shape=[
            sds((D, n * GL), bf16),
            sds((n * GR, D), bf16),
            sds((n * GL, D), bf16),
            sds((D, n * GL), bf16),
            sds((n * GL, D), bf16),
            sds((n * GW, HEADS, KP, LANES), bf16),
            sds((D + 16, n * GL), bf16),
            sds((n * GR, LANES), f32),
            sds((D, 3 * D), bf16),
            sds((16, D), f32),
        ],
        scratch_shapes=[
            pltpu.VMEM((GR + 8, D), f32),
            pltpu.VMEM((GL, D), bf16),
            pltpu.VMEM((D, GL), bf16),
            pltpu.VMEM((GL, D), bf16),
            pltpu.VMEM((D, GL), bf16),
            pltpu.VMEM((GR + 8, D), f32),
            pltpu.VMEM((GR + 8, LANES), f32),
            pltpu.VMEM((GW, KP, LANES), f32),
            pltpu.VMEM((count, max(rpd, 16), LANES), bf16),
            pltpu.SemaphoreType.DMA((copies,)),
        ],
        compiler_params=params(60),
        cost_estimate=pl.CostEstimate(flops=10**7, bytes_accessed=10**5, transcendentals=0),
        name="attn_fwd",
    )(me, x, codes, bias, *pieces)


def mlp_body(me_ref, vld_ref, rowv_ref, x_any, o_any, g_any, *refs, plan, rows, owners, rpd, groups):
    pieces = refs[: len(plan)]
    refs = refs[len(plan) :]
    res_any, dmid_any, p_any, first_any, second_any, third_ref, vec_ref, dbf1_ref, st_ref = refs[:9]
    xb, ob, gp, gT, h2, h2T, mid, dh2, es, dus, u4, vv, pp, res, pk, sem, sem_x, sem_o, sem_p, sem_g, sem_du, sem_dv, sem_dp, sem_r, sem_m = refs[9:]
    j = pl.program_id(0)
    last = FF // 512 - 1
    padded = h2.shape[0]
    blocks = rows // GR
    me = me_ref[0]
    proj_bias = rowv_ref[4:5, :]
    gain = rowv_ref[5:6, :]
    shift = rowv_ref[6:7, :]

    def weights():
        first, later = [], []
        count = 0
        for ref, rels in zip(pieces, plan):
            if rels is None:
                dst = (pp, u4, vv)[count]
                (first if count == 0 else later).append(pltpu.make_async_copy(ref, dst, sem.at[count]))
                count += 1
                continue
            for t, r in enumerate(rels):
                at = pl.ds(pl.multiple_of((r ^ me) * rpd, rpd), rpd)
                first.append(pltpu.make_async_copy(ref.at[t, 0], pp.at[at, :], sem.at[count]))
                later.append(pltpu.make_async_copy(ref.at[t, pl.ds(1, 4)], u4.at[:, at, :], sem.at[count + 1]))
                to = vv.at[pl.ds(pl.multiple_of((r ^ me) * 4, 4), 4)]
                later.append(pltpu.make_async_copy(ref.at[t, pl.ds(5, 4)], to, sem.at[count + 2]))
                count += 3
        return first, later

    def rows_of(k):
        return pl.ds(k * GR, GR)

    def grads_out(j):
        if not owners:
            cols = pl.ds(pl.multiple_of(j * 512, 512), 512)
            return [
                pltpu.make_async_copy(pk.at[0], first_any.at[:, cols], sem_du.at[j, 0]),
                pltpu.make_async_copy(pk.at[1], second_any.at[cols, :], sem_du.at[j, 1]),
            ]
        at = pl.ds(pl.multiple_of(j * rpd, rpd), rpd)
        low = pl.ds(4 * rpd, 4 * rpd)
        out = []
        for c, to in enumerate((first_any, second_any)):
            out.append(pltpu.make_async_copy(pk.at[c, :, at, :], to.at[:, at, :], sem_du.at[j, c]))
            for m in range(256 // (4 * rpd)):
                pos = place_of((j * (256 // (4 * rpd)) + m) ^ (me >> 1), [tuple(b - 1 for b in g) for g in groups[1:]])
                n = 2 * m + c
                out.append(pltpu.make_async_copy(pk.at[c, pos, low, :], to.at[pos, low, :], sem_dv.at[j, n]))
        return out

    @pl.when(j == 0)
    def _():
        first, later = weights()
        ins = []
        for c in first:
            c.start()
        for k in range(blocks):
            ins.append(pltpu.make_async_copy(x_any.at[rows_of(k)], xb.at[rows_of(k)], sem_x.at[k]))
            ins.append(pltpu.make_async_copy(o_any.at[rows_of(k)], ob.at[rows_of(k)], sem_o.at[k]))
        load_g = pltpu.make_async_copy(g_any, gp.at[pl.ds(0, rows)], sem_g.at[0])
        for c in ins + [load_g] + later:
            c.start()
        h2[rows:padded, :] = jnp.zeros((padded - rows, D), bf16)
        gp[rows:padded, :] = jnp.zeros((padded - rows, D), bf16)
        dus[rows:padded, :] = jnp.zeros((padded - rows, 512), bf16)
        for q in range(FF // 512):
            es[q, rows:padded, :] = jnp.zeros((padded - rows, 512), bf16)
        dh2[...] = jnp.zeros_like(dh2)
        for c in first:
            c.wait()
        store_p = pltpu.make_async_copy(pp, p_any, sem_p.at[0])
        store_p.start()
        squares = jnp.zeros((1, D), f32)
        for k in range(blocks):
            at = slice(k * GR, k * GR + GR)
            ins[2 * k].wait()
            ins[2 * k + 1].wait()
            a = nn(ob[at, :], pp[...]) + proj_bias
            squares = squares + jnp.sum(a * a * vld_ref[at, 0:1], axis=0, keepdims=True)
            m = xb[at, :].astype(f32) + a
            mid[at, :] = m
            c = m - jnp.mean(m, axis=-1, keepdims=True)
            var = jnp.mean(c * c, axis=-1, keepdims=True)
            h2[at, :] = (c * lax.rsqrt(var + 1e-5) * gain + shift).astype(bf16)
        st_ref[...] = jnp.zeros_like(st_ref)
        st_ref[1:2, :] = squares
        load_g.wait()

        def turn(k, carry):
            at = pl.ds(pl.multiple_of(k * LANES, LANES), LANES)
            for a in range(D // LANES):
                cols = slice(LANES * a, LANES * a + LANES)
                h2T[cols, at] = h2[at, cols].T
                gT[cols, at] = gp[at, cols].T
            return carry

        lax.fori_loop(0, padded // LANES, turn, 0)
        for c in later:
            c.wait()
        store_p.wait()

    up = u4[j]
    down = vv[pl.ds(pl.multiple_of(32 * j, 32), 32)].reshape(512, D)
    up_bias = rowv_ref[pl.ds(8 + j, 1), :]

    def products(k):
        at = slice(k * GR, k * GR + GR)
        return nn(h2[at, :], up) + up_bias, nt(gp[at, :], down)

    up_sum = jnp.zeros((1, 512), f32)
    ahead = products(0)
    for k in range(blocks):
        u, de = ahead
        if k + 1 < blocks:
            ahead = products(k + 1)
        at = slice(k * GR, k * GR + GR)
        cdf = 0.5 * lax.erf(u * RT2) + 0.5
        es[j, at, :] = (u * cdf).astype(bf16)
        du = de * (cdf + u * (PHI * jnp.exp2(u * u * (-0.5 * LOG2E))))
        dus[at, :] = du.astype(bf16)
        up_sum = up_sum + jnp.sum(du, axis=0, keepdims=True)
        dh2[at, :] += nt(dus[at, :], up)
    dbf1_ref[pl.ds(j, 1), :] = up_sum
    dU = nn(h2T[...], dus[...]).astype(bf16)
    dV = nn(gT[...], es[j]).astype(bf16).T
    if owners:
        at = pl.ds(pl.multiple_of(j * rpd, rpd), rpd)
        for k in range(owners):
            pk[(k ^ me) & 1, place_of(k ^ me, groups[1:]), at, :] = dU[rpd * k : rpd * k + rpd]
        per = 512 // (4 * rpd)
        for k in range(per):
            rel = (j * per + k) ^ me
            pk[rel & 1, place_of(rel, groups[1:]), 4 * rpd : 8 * rpd, :] = dV[4 * rpd * k : 4 * rpd * k + 4 * rpd]
        for c in grads_out(j):
            c.start()
    else:
        pk[0] = dU
        pk[1] = dV
        for c in grads_out(j):
            c.start()
        for c in grads_out(j):
            c.wait()

    @pl.when(j == last)
    def _():
        zero = jnp.zeros((1, D), f32)
        sums = [zero] * 4
        stats = [zero] * 5
        outs = []
        proj = jnp.zeros((D, D), f32)
        for k in range(blocks):
            at = slice(k * GR, k * GR + GR)
            m = mid[at, :]
            c = m - jnp.mean(m, axis=-1, keepdims=True)
            rs = lax.rsqrt(jnp.mean(c * c, axis=-1, keepdims=True) + 1e-5)
            xh = c * rs
            d = dh2[at, :]
            dx = d * gain
            dxx = d * xh
            m1 = jnp.mean(dx, axis=-1, keepdims=True)
            m2 = jnp.mean(dxx * gain, axis=-1, keepdims=True)
            grad = gp[at, :].astype(f32)
            dm = grad + (dx - m1 - xh * m2) * rs
            dh2[at, :] = dm
            outs.append(pltpu.make_async_copy(dh2.at[rows_of(k)], dmid_any.at[rows_of(k)], sem_m.at[k]))
            outs[-1].start()
            da = dm.astype(bf16)
            proj = proj + tn(ob[at, :], da)
            terms = (da.astype(f32), dxx, d, grad)
            sums = [a + jnp.sum(t, axis=0, keepdims=True) for a, t in zip(sums, terms)]
            f = rowv_ref[7:8, :]
            for b in range(4):
                f = f + nn(es[b, at, :], vv[32 * b : 32 * b + 32].reshape(512, D))
            out = m + f
            res[at, :] = out.astype(bf16)
            outs.append(pltpu.make_async_copy(res.at[rows_of(k)], res_any.at[rows_of(k)], sem_r.at[k]))
            outs[-1].start()
            vl = vld_ref[at, 0:1]
            x = xb[at, :].astype(f32)
            terms = (x * x * vl, m * m * vl, f * f * vl, out * out * vl, jnp.broadcast_to(vl, (GR, D)))
            stats = [a + jnp.sum(t, axis=0, keepdims=True) for a, t in zip(stats, terms)]
        for q in range(4):
            vec_ref[q : q + 1, :] = sums[q]
        vec_ref[4:8, :] = jnp.zeros((4, D), f32)
        dbf1_ref[4:8, :] = jnp.zeros((4, D), f32)
        for q, t in zip((0, 2, 3, 4, 5), stats):
            st_ref[q : q + 1, :] = t
        if owners:
            proj = proj.astype(bf16)
            at = pl.ds(8 * rpd, rpd)
            for k in range(owners):
                pk[(k ^ me) & 1, place_of(k ^ me, groups[1:]), at, :] = proj[rpd * k : rpd * k + rpd]
            third_ref[...] = jnp.zeros_like(third_ref)
            for c, to in enumerate((first_any, second_any)):
                outs.append(pltpu.make_async_copy(pk.at[c, :, at, :], to.at[:, at, :], sem_dp.at[c]))
                outs[-1].start()
            for step in range(last + 1):
                outs += grads_out(step)
        else:
            third_ref[...] = proj
        for c in outs:
            c.wait()


def mlp(me, x, o, g, vld, rowv, plan, pieces, rpd, owners, count, groups):
    rows = x.shape[0]
    blocks = rows // GR
    steps = FF // 512
    padded = -(-rows // LANES) * LANES
    copies = sum(1 if r is None else 3 * len(r) for r in plan)
    if owners:
        grad_shapes = [sds((count // 2, 9 * rpd, 512), bf16)] * 2 + [sds((8, LANES), f32)]
        pk = (2, count // 2, 9 * rpd, 512)
    else:
        grad_shapes = [sds((D, FF), bf16), sds((FF, D), bf16), sds((D, D), f32)]
        pk = (2, 512, 512)
    dma = pltpu.SemaphoreType.DMA
    return pl.pallas_call(
        functools.partial(mlp_body, plan=plan, rows=rows, owners=count if owners else 0, rpd=rpd, groups=groups),
        grid=(steps,),
        in_specs=[SMEM, whole((rows, LANES)), whole((16, D))] + any_specs(3 + len(pieces)),
        out_specs=any_specs(5) + [whole(grad_shapes[2].shape)] + [whole((8, D))] * 3,
        out_shape=[sds((rows, D), bf16), sds((rows, D), f32), sds((D, D), bf16)] + grad_shapes + [sds((8, D), f32)] * 3,
        scratch_shapes=[
            pltpu.VMEM((rows, D), bf16),
            pltpu.VMEM((rows, D), bf16),
            pltpu.VMEM((padded, D), bf16),
            pltpu.VMEM((D, padded), bf16),
            pltpu.VMEM((padded, D), bf16),
            pltpu.VMEM((D, padded), bf16),
            pltpu.VMEM((rows, D), f32),
            pltpu.VMEM((rows, D), f32),
            pltpu.VMEM((steps, padded, 512), bf16),
            pltpu.VMEM((padded, 512), bf16),
            pltpu.VMEM((steps, D, 512), bf16),
            pltpu.VMEM((FF // 16, 16, D), bf16),
            pltpu.VMEM((D, D), bf16),
            pltpu.VMEM((rows, D), bf16),
            pltpu.VMEM(pk, bf16),
            dma((copies,)),
            dma((blocks,)),
            dma((blocks,)),
            dma((1,)),
            dma((1,)),
            dma((steps, 2)),
            dma((steps, max(1, 512 // (4 * rpd)))),
            dma((2,)),
            dma((blocks,)),
            dma((blocks,)),
        ],
        compiler_params=params(52),
        cost_estimate=pl.CostEstimate(flops=10**7, bytes_accessed=10**5, transcendentals=0),
        name="mlp",
    )(me, vld, rowv, x, o, g, *pieces)


def attn_bwd_body(me_ref, dmid_ref, p_ref, oT_ref, q_ref, kT_ref, v_ref, pT_ref, xT_ref, w_any, rowv_ref, *refs, owners, rpd, groups):
    dm_ref, acc_ref, vec_ref = refs[:3]
    grads = refs[3:-7]
    xs, dap, don, doT, dw, w_ref, sem_w = refs[-7:]
    i = pl.program_id(0)
    load_w = pltpu.make_async_copy(w_any, w_ref, sem_w.at[0])

    @pl.when(i == 0)
    def _():
        load_w.start()
        acc_ref[...] = jnp.zeros_like(acc_ref)
        dw[...] = jnp.zeros_like(dw)

    xs[0:GR, :] = dmid_ref[...]
    for w in range(GW):
        dap[LANES * w : LANES * w + LANES, :] = pad_window(xs[CELLS * w : CELLS * w + 104, :])
        dm_ref[LANES * w + KP : LANES * w + LANES, :] = jnp.zeros((LANES - KP, 3 * D), bf16)
    da = dap[...]
    don[...] = nt(da, p_ref[...]).astype(bf16)
    for w in range(GW):
        for a in range(D // LANES):
            rows, cols = slice(LANES * w, LANES * w + LANES), slice(LANES * a, LANES * a + LANES)
            doT[cols, rows] = don[rows, cols].T
    factor = HD**-0.5

    def window(w, carry):
        start = pl.multiple_of(w * LANES, LANES)
        at = pl.ds(start, LANES)
        keys = pl.ds(start, KP)
        for g in range(4):
            c0 = LANES * g
            cols = slice(c0, c0 + LANES)
            dp = nn(by_head(v_ref[keys, cols]), doT[cols, at])
            dss = []
            for q in range(4):
                h = 4 * g + q
                head = slice(HD * h, HD * h + HD)
                delta = jnp.sum(doT[head, at].astype(f32) * oT_ref[head, at].astype(f32), axis=0, keepdims=True)
                ds = pT_ref[w, h].astype(f32) * (dp[KP * q : KP * q + KP] - delta)
                acc_ref[h] += ds
                dss.append(ds.astype(bf16))
            dq = [nn(kT_ref[c0 + HD * q : c0 + HD * q + HD, at][:, 0:KP], dss[q]) for q in range(4)]
            dm_ref[at, cols] = (jnp.concatenate(dq, axis=0) * factor).astype(bf16).T
            dk = nn(jnp.concatenate(dss, axis=1), by_head(q_ref[at, cols])) * factor
            dm_ref[keys, D + c0 : D + c0 + LANES] = dk.astype(bf16)
            dv = nn(jnp.concatenate([pT_ref[w, 4 * g + q] for q in range(4)], axis=1), by_head(don[at, cols]))
            dm_ref[keys, 2 * D + c0 : 2 * D + c0 + LANES] = dv.astype(bf16)
        return carry

    lax.fori_loop(0, GW, window, 0, unroll=4)
    dw[...] += nn(xT_ref[...], dm_ref[...])

    @pl.when(i == pl.num_programs(0) - 1)
    def _():
        load_w.wait()
        s = dw[D : D + 1, :]
        vec_ref[...] = jnp.zeros_like(vec_ref)
        vec_ref[0:1, :] = s
        for a in range(D // LANES):
            rows = slice(LANES * a, LANES * a + LANES)
            col = rowv_ref[0:8, rows].T
            x = dw[rows, :]
            wt = w_ref[rows, :].astype(f32)
            by_gain = jnp.broadcast_to(jnp.sum(wt * x, axis=1, keepdims=True), (LANES, LANES)).T
            by_shift = jnp.broadcast_to(jnp.sum(wt * s, axis=1, keepdims=True), (LANES, LANES)).T
            vec_ref[1:2, rows] = by_gain[0:1]
            vec_ref[2:3, rows] = by_shift[0:1]
            dw[rows, :] = col[:, 0:1] * x + col[:, 1:2] * s
        if owners:
            me = me_ref[0]
            for k in range(owners):
                rel = k ^ me
                pos = place_of(rel, groups[1:])
                mine = slice(rpd * k, rpd * k + rpd)

                def store(to, mine=mine, pos=pos):
                    for q in range(3):
                        to[pos, rpd * q : rpd * q + rpd, :] = dw[mine, D * q : D * q + D].astype(bf16)

                pl.when(rel & 1 == 0)(functools.partial(store, grads[0]))
                pl.when(rel & 1 == 1)(functools.partial(store, grads[1]))
        else:
            grads[0][...] = dw[0:D, :].astype(bf16)


def attn_bwd(me, dmid, p, oT, q, kT, v, pT, xT, w, rowv, rpd, owners, count, groups):
    n = q.shape[0] // GL

    def tb(r):
        return pl.BlockSpec((r, GL), lambda i: (0, i))

    pb = pl.BlockSpec((GL, D), lambda i: (i, 0))
    if owners:
        grad_shapes = [sds((count // 2, 3 * rpd, D), bf16)] * 2
    else:
        grad_shapes = [sds((D, 3 * D), bf16)]
    return pl.pallas_call(
        functools.partial(attn_bwd_body, owners=count if owners else 0, rpd=rpd, groups=groups),
        grid=(n,),
        in_specs=[SMEM, pl.BlockSpec((GR, D), lambda i: (i, 0)), whole((D, D)), tb(D), pb, tb(D), pb, pl.BlockSpec((GW, HEADS, KP, LANES), lambda i: (i, 0, 0, 0)), tb(D + 16), pl.BlockSpec(memory_space=pl.ANY), whole((16, D))],
        out_specs=[pl.BlockSpec((GL, 3 * D), lambda i: (i, 0)), whole((HEADS, KP, LANES)), whole((8, 3 * D))] + [whole(s.shape) for s in grad_shapes],
        out_shape=[sds((n * GL, 3 * D), bf16), sds((HEADS, KP, LANES), f32), sds((8, 3 * D), f32)] + grad_shapes,
        scratch_shapes=[
            pltpu.VMEM((GR + 8, D), f32),
            pltpu.VMEM((GL, D), bf16),
            pltpu.VMEM((GL, D), bf16),
            pltpu.VMEM((D, GL), bf16),
            pltpu.VMEM((D + 16, 3 * D), f32),
            pltpu.VMEM((D, 3 * D), bf16),
            pltpu.SemaphoreType.DMA((1,)),
        ],
        compiler_params=params(60),
        cost_estimate=pl.CostEstimate(flops=10**7, bytes_accessed=10**5, transcendentals=0),
        name="attn_bwd",
    )(me, dmid, p, oT, q, kT, v, pT, xT, w, rowv)


def grad_in_body(dm_ref, w_ref, x_ref, dmid_ref, rowv_ref, tg_ref, dsc):
    dh = nt(dm_ref[...], w_ref[...])
    for w in range(GW):
        dsc[CELLS * w : CELLS * w + 104, :] = dh[LANES * w : LANES * w + 104]
    x = x_ref[...].astype(f32)
    c = x - jnp.mean(x, axis=-1, keepdims=True)
    rs = lax.rsqrt(jnp.mean(c * c, axis=-1, keepdims=True) + 1e-5)
    xh = c * rs
    dx = dsc[0:GR, :] * rowv_ref[0:1, :]
    m1 = jnp.mean(dx, axis=-1, keepdims=True)
    m2 = jnp.mean(dx * xh, axis=-1, keepdims=True)
    tg_ref[...] = dmid_ref[...] + (dx - m1 - xh * m2) * rs


def grad_in(dm, w, x, dmid, rowv):
    n = x.shape[0] // GR
    rb = pl.BlockSpec((GR, D), lambda i: (i, 0))
    return pl.pallas_call(
        grad_in_body,
        grid=(n,),
        in_specs=[pl.BlockSpec((GL, 3 * D), lambda i: (i, 0)), whole((D, 3 * D)), rb, rb, whole((16, D))],
        out_specs=rb,
        out_shape=sds((n * GR, D), f32),
        scratch_shapes=[pltpu.VMEM((GR + 8, D), f32)],
        compiler_params=params(60),
        cost_estimate=pl.CostEstimate(flops=10**7, bytes_accessed=10**5, transcendentals=0),
        name="grad_in",
    )(dm, w, x, dmid, rowv)


SMALL = 24
SENT = 32


def to_send(small):
    lane = lax.broadcasted_iota(jnp.int32, small.shape, 1)
    lane = jnp.where(lax.broadcasted_iota(jnp.int32, small.shape, 0) >= 8, lane, -1)
    small = jnp.where(lane == RELN, small + pltpu.roll(small, D - 1, 1), small)
    hi = small.astype(bf16).astype(f32)
    small = jnp.where(lane == RELN + 1, pltpu.roll(small - hi, 1, 1), hi)
    return jnp.concatenate([small, jnp.zeros((SENT - SMALL, D), f32)], axis=0).astype(bf16)


def sent_sums(terms):
    got = [t.astype(f32)[0:SMALL] for t in terms]
    while len(got) > 1:
        got = [got[k] + got[k + 1] for k in range(0, len(got), 2)]
    return got[0]


def fold_body(*refs, first, terms, parts):
    ins, outs = refs[: 2 * terms if first else terms + 1], refs[2 * terms if first else terms + 1 :]
    nb, rows = ins[0].shape[0], ins[0].shape[1]
    n = nb // (parts + 1)
    if first:
        small = ins[2][...] + ins[3][...]
    else:
        small = sent_sums([ins[1][...]] + [r[nb * rows :, :] for r in ins[2:]])
    for p in range(parts + 1):
        at = slice(p * n, p * n + n)
        total = ins[0][at].astype(f32)
        if first:
            total = total + ins[1][at].astype(f32)
        else:
            for r in ins[2:]:
                total = total + r[p * n * rows : (p + 1) * n * rows, :].astype(f32).reshape(n, rows, D)
        if p == 0:
            outs[0][...] = total
            outs[1][...] = to_send(small)
        else:
            outs[p + 1][0 : n * rows, :] = total.reshape(n * rows, D).astype(bf16)
            outs[p + 1][n * rows :, :] = to_send(small)


def fold(arrays, parts, first=False):
    terms = 2 if first else len(arrays) - 1
    nb, rows = arrays[0].shape[:2]
    n = nb // (parts + 1)
    return pl.pallas_call(
        functools.partial(fold_body, first=first, terms=terms, parts=parts),
        out_shape=[sds((n, rows, D), f32), sds((SENT, D), bf16)] + [sds((n * rows + SENT, D), bf16)] * parts,
        compiler_params=params(16),
        cost_estimate=pl.CostEstimate(flops=10**6, bytes_accessed=10**5, transcendentals=0),
        name="fold",
    )(*arrays)


def add_body(*refs, terms, later):
    ins, outs = refs[:terms], refs[terms : -2] if later else refs[terms:]
    n = outs[0].shape[0]
    copies = []
    if later:
        buf, sem = refs[-2:]
        for p in range(len(outs)):
            at = pl.ds(p * n, n)
            copies.append(pltpu.make_async_copy(ins[0].at[at], buf.at[at], sem.at[p]))
        for c in copies:
            c.start()
        ins = (buf,) + ins[1:]
    for p, out in enumerate(outs):
        if later:
            copies[p].wait()
        at = slice(p * n, p * n + n)
        total = ins[0][at].astype(f32)
        for r in ins[1:]:
            total = total + r[at].astype(f32)
        out[...] = total.astype(out.dtype)


def add_split(terms, group, later=False):
    parts = len(masks_of(group))
    first = terms[0]
    n = first.shape[0] // (parts + 1)
    shape = (n,) + first.shape[1:]
    vmem = pl.BlockSpec(memory_space=pltpu.VMEM)
    out = pl.pallas_call(
        functools.partial(add_body, terms=len(terms), later=later),
        in_specs=[pl.BlockSpec(memory_space=pltpu.HBM) if later else vmem] + [vmem] * (len(terms) - 1),
        out_shape=[sds(shape, f32)] + [sds(shape, bf16)] * parts,
        scratch_shapes=[pltpu.VMEM(first.shape, first.dtype), pltpu.SemaphoreType.DMA((parts + 1,))] if later else [],
        compiler_params=params(16),
        cost_estimate=pl.CostEstimate(flops=10**6, bytes_accessed=10**5, transcendentals=0),
        name="add_split",
    )(*terms)
    return out[0], out[1:]


def spread(o_ref, block, width, at):
    each = width // LANES
    for b in range(block.shape[1] // LANES):
        o_ref[pl.ds(at // LANES + b, block.shape[0], stride=each), :] = block[:, LANES * b : LANES * b + LANES]


def attn_last_body(me_ref, own_ref, kept_ref, *refs, rpd, per):
    got_refs, (qkv_ref, vec_ref, table_ref, stats_ref, lines) = refs[:-5], refs[-5:]
    rows = own_ref.shape[1]
    total = own_ref[0]
    for r in got_refs:
        total = total + r[0:rows, :].astype(f32)
    for q in range(3):
        spread(qkv_ref, total[rpd * q : rpd * q + rpd], 3 * D, D * q)
    small = sent_sums([kept_ref[...]] + [r[rows:, :] for r in got_refs])
    for k in range(8):
        for a in range(4):
            lines[4 * k + a : 4 * k + a + 1, :] = small[k : k + 1, LANES * a : LANES * a + LANES]
    lines[32:48, :] = small[8:24, RP:D]
    if per % 64:
        vec_ref[...] = lines[...]
    else:
        low = lax.broadcasted_iota(jnp.int32, (1, LANES), 1) < 64
        for p in range(0, per // 64, 2):
            halves = []
            for k in range(2):
                c = me_ref[0] * (per // 64) + min(p + k, per // 64 - 1)
                line = lines[pl.ds(c >> 1, 1), :]
                halves.append(jnp.where(c & 1 == k, line, pltpu.roll(line, 64, 1)))
            vec_ref[p // 2 : p // 2 + 1, :] = jnp.where(low, halves[0], halves[1])
    table_ref[...] = small[8:24, 0:RELN]
    turned = small[8:24, RP - LANES : RP].T
    at = RELN - (RP - LANES)
    line = turned[at : at + 1] + turned[at + 1 : at + 2]
    stats_ref[...] = jnp.sqrt(line / line[:, 5:6] + 1e-06)


def attn_last(me, arrays, rpd, per):
    lines = -(-per // LANES) if per % 64 == 0 else 48
    return pl.pallas_call(
        functools.partial(attn_last_body, rpd=rpd, per=per),
        in_specs=[SMEM] + [pl.BlockSpec(memory_space=pltpu.VMEM)] * len(arrays),
        out_shape=[sds((12 * rpd, LANES), f32), sds((lines, LANES), f32), sds((HEADS, RELN), f32), sds((1, HEADS), f32)],
        scratch_shapes=[pltpu.VMEM((48, LANES), f32)],
        compiler_params=params(16),
        cost_estimate=pl.CostEstimate(flops=10**6, bytes_accessed=10**5, transcendentals=0),
        name="attn_last",
    )(me, *arrays)


def mlp_last_body(own_ref, *refs, rpd):
    total = own_ref[0]
    for r in refs[:-3]:
        total = total + r[0].astype(f32)
    for q in range(4):
        spread(refs[-3], total[rpd * q : rpd * q + rpd], FF, 512 * q)
    spread(refs[-2], total[4 * rpd : 8 * rpd], D, 0)
    spread(refs[-1], total[8 * rpd :], D, 0)


def mlp_last(arrays, rpd):
    return pl.pallas_call(
        functools.partial(mlp_last_body, rpd=rpd),
        out_shape=[sds((16 * rpd, LANES), f32)] * 2 + [sds((4 * rpd, LANES), f32)],
        compiler_params=params(16),
        cost_estimate=pl.CostEstimate(flops=10**6, bytes_accessed=10**5, transcendentals=0),
        name="mlp_last",
    )(*arrays)


def place_hits(shape, axis, rev=0):
    c = lax.broadcasted_iota(jnp.int32, shape, 1 - axis)
    code = jnp.where(c < CELLS, (2 * WSIDE - 1) * (c // WSIDE) + c % WSIDE, -1000)
    if rev:
        code = rev - code
    return jnp.where(code == lax.broadcasted_iota(jnp.int32, shape, axis), 1.0, 0.0).astype(bf16)


def rel_bias_body(t_ref, o_ref):
    keys = place_hits((KP, 192), 1)
    queries = place_hits((256, LANES), 0)

    def head(h, carry):
        row = pltpu.roll(jnp.broadcast_to(t_ref[pl.ds(h, 1), :], (8, RP)), 0, 1, stride=1, stride_axis=0)
        t = jnp.concatenate([pltpu.roll(row, (8 * k - 180) % RP, 1)[:, 0:256] for k in range(24)], axis=0)
        hi = t.astype(bf16)
        lo = (t - hi.astype(f32)).astype(bf16)
        b = nn(jnp.concatenate([hi, lo], axis=0), queries).astype(bf16)
        b = nn(keys, jnp.concatenate([b[0:192], b[192:384]], axis=1))
        o_ref[h] = b[:, 0:LANES] + b[:, LANES : 2 * LANES]
        return carry

    lax.fori_loop(0, HEADS, head, 0, unroll=8)


def rel_bias(table):
    return pl.pallas_call(
        rel_bias_body,
        out_shape=sds((HEADS, KP, LANES), f32),
        compiler_params=params(16),
        cost_estimate=pl.CostEstimate(flops=2 * 10**10, bytes_accessed=10**6, transcendentals=0),
        name="rel_bias",
    )(table)


def rel_grad_body(a_ref, one_ref, two_ref, up_ref, squares_ref, o_ref):
    keys = place_hits((192, KP), 0, 191)
    queries = place_hits((LANES, 256), 1)
    zero = jnp.zeros((8, RP - 256), f32)
    o_ref[0:2, :] = one_ref[1:3, 0:D]
    o_ref[2:3, :] = one_ref[0:1, 0:D]
    o_ref[3:4, :] = one_ref[0:1, 2 * D : 3 * D]
    o_ref[4:8, :] = two_ref[0:4, :]

    def head(h, carry):
        a = a_ref[h]
        hi = a.astype(bf16)
        lo = (a - hi.astype(f32)).astype(bf16)
        b = nn(keys, jnp.concatenate([hi, lo], axis=1)).astype(bf16)
        b = nn(jnp.concatenate([b[:, 0:LANES], b[:, LANES : 2 * LANES]], axis=0), queries)
        b = b[0:192] + b[192:384]
        t = jnp.zeros((8, RP), f32)
        for k in range(24):
            t = t + pltpu.roll(jnp.concatenate([b[8 * k : 8 * k + 8], zero], axis=1), (8 * k - 11) % RP, 1)
        t = pltpu.roll(t, 0, 1, stride=1, stride_axis=0)
        o_ref[pl.ds(8 + h, 1), 0:RP] = jnp.sum(t, axis=0, keepdims=True)
        return carry

    lax.fori_loop(0, HEADS, head, 0, unroll=16)
    for k in range(4):
        for a in range(4):
            o_ref[8 + 4 * k + a : 9 + 4 * k + a, RP:D] = up_ref[k : k + 1, LANES * a : LANES * a + LANES]
    for k in range(6):
        o_ref[8 + k : 9 + k, RELN : RELN + 1] = jnp.sum(squares_ref[k : k + 1, :], axis=1, keepdims=True)
        o_ref[8 + k : 9 + k, RELN + 1 : RELN + 2] = jnp.zeros((1, 1), f32)


def rel_grad(acc, one, two, up, squares):
    return pl.pallas_call(
        rel_grad_body,
        out_shape=sds((SMALL, D), f32),
        compiler_params=params(16),
        cost_estimate=pl.CostEstimate(flops=10**7, bytes_accessed=10**5, transcendentals=0),
        name="rel_grad",
    )(acc, one, two, up, squares)


def shards(tokens, cotangent, regions, validity, qkv_weight, proj_weight, fc1_weight, fc2_weight, vectors, rel_table, *, count, inner):
    rows = tokens.shape[0]
    groups = bit_groups(count)
    single = groups[:2] + [(b,) for g in groups[2:] for b in g]
    rpd = D // count
    direct = rpd % 16 == 0
    me = lax.axis_index("dp") * inner + lax.axis_index("shard")
    me_s = me.astype(jnp.int32).reshape(1)

    per = vectors.shape[0]
    if direct:
        own = jnp.pad(vectors, (0, rpd * LANES - per)).reshape(rpd, LANES)
        own = jnp.concatenate([qkv_weight.reshape(rpd, 3 * D), own], axis=1)
    else:
        own = jnp.concatenate([qkv_weight, vectors]).reshape(1, -1)
    rels, attn_up = gather_upper(own, groups, count)
    up_rows = fc1_weight.reshape(rpd, FF)
    packed = jnp.concatenate(
        [proj_weight.reshape(rpd, D)] + [up_rows[:, 512 * q : 512 * q + 512] for q in range(4)] + [fc2_weight.reshape(4 * rpd, D)], axis=0
    )
    attn_pieces = gather_plane(rels, attn_up, groups, count)
    table_in = after(rel_table, attn_up)
    mlp_rels, mlp_up = gather_upper(packed, single, count, attn_up)

    bias = rel_bias(jnp.pad(table_in.T * LOG2E, ((0, 0), (0, RP - RELN))))
    reg = regions.reshape(-1, GW, CELLS).astype(f32)
    key_code = jnp.where(validity.reshape(-1, GW, CELLS) == 1, reg, -2.0)
    codes = jnp.pad(jnp.concatenate([reg, key_code], axis=1), ((0, 0), (0, 0), (0, LANES - CELLS)), constant_values=-3.0)

    attn_pieces = hold(attn_pieces, bias, codes)
    mlp_up = after(mlp_up, bias, codes, [a for _, a in attn_pieces])
    attn_pieces = gather_core(attn_pieces, count)
    mlp_pieces = gather_plane(mlp_rels, mlp_up, groups, count)
    if direct:
        attn_plan = [r for r, _ in attn_pieces]
        attn_w = [a for _, a in attn_pieces]
    else:
        attn_plan = [None] * 2
        both = natural_order(attn_pieces, me, count).reshape(count, -1)
        attn_w = [both[:, : 3 * D * rpd].reshape(D, 3 * D), jnp.pad(both[:, 3 * D * rpd :].astype(f32).reshape(12, D), ((0, 4), (0, 0)))]

    x = after(tokens, mlp_up)
    oT, o, q, kT, v, pT, xT, vld, w_full, rowv = attn_fwd(me_s, x, codes, bias, attn_plan, attn_w, rpd, per, count)

    mlp_pieces = gather_core(hold(mlp_pieces, o), count)
    if direct:
        mlp_plan = [r for r, _ in mlp_pieces]
        mlp_w = [a.reshape(-1, 9, rpd, D) for _, a in mlp_pieces]
    else:
        both = natural_order(mlp_pieces, me, count).reshape(count, 9, rpd, D)
        mlp_plan = [None] * 3
        mlp_w = [both[:, 0].reshape(D, D), both[:, 1:5].transpose(1, 0, 2, 3).reshape(4, D, 512), both[:, 5:].reshape(128, 16, D)]
    result, dmid, p_full, mlp_keep, mlp_send, dproj, vec_two, dbf1, squares = mlp(
        me_s, tokens, o, cotangent, vld, rowv, mlp_plan, mlp_w, rpd, direct, count, single
    )
    order = None
    if not direct:
        blocks = jnp.arange(count)
        order, mlp_order = (
            jnp.zeros((count,), jnp.int32).at[place_of(blocks, way)].set(blocks.astype(jnp.int32)) ^ me for way in (groups, single)
        )
        dU = mlp_keep.reshape(count, rpd, 4, 512).transpose(0, 2, 1, 3).reshape(count, 4 * rpd, 512)
        pk = [dU, mlp_send.reshape(count, 4 * rpd, D), dproj.astype(bf16).reshape(count, rpd, D)]
        pk = jnp.take(jnp.concatenate(pk, axis=1), mlp_order, axis=0)
        mlp_keep, mlp_send = pk[: count // 2], pk[count // 2 :]

    other = swap(mlp_send, 1, count)
    mlp_own, parts = add_split([mlp_keep, other], groups[1], later=True)
    mlp_got = send_parts(parts, groups[1], count)
    dmid = after(dmid, parts)
    got = attn_bwd(me_s, dmid, p_full, oT, q, kT, v, pT, xT, w_full, rowv, rpd, direct, count, groups)
    dm, score_sums, vec_one = got[:3]
    if direct:
        attn_keep, attn_send = got[3:]
    else:
        dW = got[3].reshape(count, rpd, 3, D).transpose(0, 2, 1, 3).reshape(count, 3 * rpd, D)
        pk = jnp.take(jnp.pad(dW, ((0, 0), (0, rpd), (0, 0))), order, axis=0)
        attn_keep, attn_send = pk[: count // 2], pk[count // 2 :]
    mlp_got, attn_send, score_sums, dm = lax.optimization_barrier((mlp_got, attn_send, score_sums, dm))

    other = swap(attn_send, 1, count)
    mlp_terms = [mlp_own] + mlp_got
    for g in single[2:3]:
        mlp_own, parts = add_split(mlp_terms, g)
        mlp_terms = [mlp_own] + send_parts(parts, g, count)
        score_sums = after(score_sums, parts)
    small = rel_grad(score_sums, vec_one, vec_two, dbf1, squares)
    other = after(other, small)
    levels = [len(masks_of(g)) for g in groups[1:]]
    out = fold([attn_keep, other, small, swap(small, 1, count)], levels[0], first=True)
    for k, g in enumerate(groups[1:]):
        own, kept, parts = out[0], out[1], out[2:]
        sent = send_parts(parts, g, count)
        if k == 0:
            mlp_terms = after(mlp_terms, parts)
            for up in single[3:]:
                mlp_own, parts = add_split(mlp_terms, up)
                mlp_terms = [mlp_own] + send_parts(parts, up, count)
            dm = after(dm, parts)
            grad_tokens = grad_in(dm, w_full, tokens, dmid, rowv)
            sent, mlp_terms = after((sent, mlp_terms), grad_tokens)
        if k + 1 < len(levels):
            out = fold([own, kept] + sent, levels[k + 1])
            mlp_terms = after(mlp_terms, out)
    grad_fc1, grad_fc2, grad_proj = mlp_last(mlp_terms, rpd)
    sent = after(sent, grad_fc1)
    grad_qkv, grad_vectors, grad_table, stats = attn_last(me_s, [own, kept] + sent, rpd, per)
    if per % 64 == 0:
        grad_vectors = grad_vectors.reshape(-1)[:per]
    else:
        grad_vectors = lax.dynamic_slice(grad_vectors.reshape(-1), (me * per,), (per,))
    return (
        result,
        grad_tokens,
        grad_qkv.reshape(-1),
        grad_proj.reshape(-1),
        grad_fc1.reshape(-1),
        grad_fc2.reshape(-1),
        grad_vectors,
        grad_table.T,
        stats[0, 0:5],
    )


def solution(mesh):
    flat = P(AXES)
    tall = P(AXES, None)
    in_specs = (tall, tall, flat, flat, flat, flat, flat, flat, flat, P())
    out_specs = (tall, tall, flat, flat, flat, flat, flat, P(), P())
    inner = mesh.shape["shard"]
    body = functools.partial(shards, count=mesh.shape["dp"] * inner, inner=inner)
    return jax.shard_map(body, mesh=mesh, in_specs=in_specs, out_specs=out_specs, check_vma=False)
```

```python
import functools

import jax
import jax.numpy as jnp
from jax import lax
from jax.experimental import pallas as pl
from jax.experimental.pallas import tpu as pltpu
from jax.sharding import PartitionSpec as P

D = 512
FF = 2048
HEADS = 16
HD = 32
WSIDE = 10
RELN = 361
CELLS = WSIDE * WSIDE
GW = 4
GR = GW * CELLS
KP = 112
LANES = 128
GL = GW * LANES
RP = 384
AXES = ("dp", "shard")
LOG2E = 1.4426950408889634
NEG = -1e9
RT2 = 0.7071067811865476
PHI = 0.3989422804014327
f32 = jnp.float32
bf16 = jnp.bfloat16
sds = jax.ShapeDtypeStruct


def nn(a, b):
    return lax.dot_general(a, b, (((1,), (0,)), ((), ())), preferred_element_type=f32)


def nt(a, b):
    return lax.dot_general(a, b, (((1,), (1,)), ((), ())), preferred_element_type=f32)


def tn(a, b):
    return lax.dot_general(a, b, (((0,), (0,)), ((), ())), preferred_element_type=f32)


def whole(shape):
    return pl.BlockSpec(shape, lambda i: (0,) * len(shape))


def params(mib):
    return pltpu.CompilerParams(vmem_limit_bytes=mib * 2**20)


def bit_groups(count):
    bits = count.bit_length() - 1
    groups = [(0,)]
    at = 1
    while at < bits:
        groups.append(tuple(range(at, min(at + 2, bits))))
        at += 2
    return groups


def masks_of(group):
    return [sum(((v >> k) & 1) << b for k, b in enumerate(group)) for v in range(1, 1 << len(group))]


def swap(x, mask, count):
    return lax.ppermute(x, AXES, [(i, i ^ mask) for i in range(count)])


def place_of(rel, groups):
    pos = 0
    for g in groups:
        pos = pos * (1 << len(g)) + ((rel >> g[0]) & ((1 << len(g)) - 1))
    return pos


def after(values, *others):
    return lax.optimization_barrier((values, others))[0]


def gather_upper(x, groups, count, *others):
    cur = x[None]
    rels = [0]
    for k, g in enumerate(groups[:1:-1]):
        if k and others:
            cur = after(cur, *others)
        ms = masks_of(g)
        cur = jnp.concatenate([cur] + [swap(cur, m, count) for m in ms], axis=0)
        rels = [r ^ m for m in [0] + ms for r in rels]
    return rels, cur


def gather_plane(rels, cur, groups, count):
    return [(rels, cur)] + [([r ^ m for r in rels], swap(cur, m, count)) for m in masks_of(groups[1])]


def gather_core(pieces, count):
    return pieces + [([r ^ 1 for r in rels], swap(arr, 1, count)) for rels, arr in pieces]


def hold(pieces, *others):
    held = after([a for _, a in pieces[1:]], *others)
    return pieces[:1] + [(r, a) for (r, _), a in zip(pieces[1:], held)]


def natural_order(pieces, me, count):
    rels = [r for rs, _ in pieces for r in rs]
    where = [0] * count
    for k, r in enumerate(rels):
        where[r] = k
    both = jnp.concatenate([a for _, a in pieces], axis=0)
    return jnp.take(both, jnp.asarray(where, jnp.int32)[jnp.arange(count) ^ me], axis=0)


def send_parts(parts, group, count):
    return [swap(p, m, count) for p, m in zip(parts, masks_of(group))]


def lay_vectors(raw, per, rowv_ref):
    unit = LANES // 2
    each = per // unit
    low = lax.broadcasted_iota(jnp.int32, (1, LANES), 1) < unit

    def half(c, high):
        owner, part = divmod(c, each)
        got = raw[owner, part // 2 : part // 2 + 1, :].astype(f32)
        return got if part % 2 == high else pltpu.roll(got, unit, 1)

    for m in range((8 * D + FF) // LANES):
        row, col = divmod(m * LANES, D)
        rowv_ref[row : row + 1, col : col + LANES] = jnp.where(low, half(2 * m, 0), half(2 * m + 1, 1))


def pad_window(rows):
    at = lax.broadcasted_iota(jnp.int32, (104, 1), 0)
    rows = jnp.where(at < CELLS, rows, 0.0)
    return jnp.concatenate([rows, jnp.zeros((LANES - 104, rows.shape[1]), f32)], axis=0).astype(bf16)


def head_lanes():
    return lax.broadcasted_iota(jnp.int32, (1, LANES), 1) // HD


def by_head(block):
    lane = head_lanes()
    return jnp.concatenate([jnp.where(lane == q, block, jnp.zeros_like(block)) for q in range(4)], axis=0)


def attn_fwd_body(me_ref, x_ref, code_ref, bias_ref, *refs, plan, rpd, per):
    pieces = refs[: len(plan)]
    (oT_ref, o_ref, q_ref, kT_ref, v_ref, pT_ref, xT_ref, vld_ref, w_ref, rowv_ref) = refs[len(plan) : len(plan) + 10]
    xs, h1p, qT, kn, vT, osc, vsc, mask_ref, raw, sem = refs[len(plan) + 10 :]

    @pl.when(pl.program_id(0) == 0)
    def _():
        copies = []
        for ref, rels in zip(pieces, plan):
            if rels is None:
                copies.append(pltpu.make_async_copy(ref, (w_ref, rowv_ref)[len(copies)], sem.at[len(copies)]))
                continue
            for t, r in enumerate(rels):
                at = pl.multiple_of((r ^ me_ref[0]) * rpd, rpd)
                copies.append(
                    pltpu.make_async_copy(
                        ref.at[t, :, pl.ds(0, 3 * D)], w_ref.at[pl.ds(at, rpd), :], sem.at[len(copies)]
                    )
                )
                copies.append(
                    pltpu.make_async_copy(ref.at[t, :, pl.ds(3 * D, LANES)], raw.at[r ^ me_ref[0]], sem.at[len(copies)])
                )
        for c in copies:
            c.start()
        for c in copies:
            c.wait()
        if plan[0] is not None:
            rowv_ref[12:16, :] = jnp.zeros((4, D), f32)
            lay_vectors(raw, per, rowv_ref)

    xs[0:GR, :] = x_ref[...].astype(f32)
    gain = rowv_ref[0:1, :]
    shift = rowv_ref[1:2, :]
    for w in range(GW):
        xw = xs[CELLS * w : CELLS * w + 104, :]
        c = xw - jnp.mean(xw, axis=-1, keepdims=True)
        var = jnp.mean(c * c, axis=-1, keepdims=True)
        xh = c * lax.rsqrt(var + 1e-5)
        h1p[LANES * w : LANES * w + LANES, :] = pad_window(xh * gain + shift)
        xh = pad_window(xh)
        for a in range(D // LANES):
            xT_ref[LANES * a : LANES * a + LANES, LANES * w : LANES * w + LANES] = xh[:, LANES * a : LANES * a + LANES].T
    xT_ref[D : D + 16, :] = jnp.ones((16, GL), bf16)
    turned = code_ref[0].T
    keys = lax.broadcasted_iota(jnp.int32, (KP, LANES), 0)
    same = (keys == lax.broadcasted_iota(jnp.int32, (KP, LANES), 1)) & (keys < CELLS)
    for w in range(GW):
        of_key = turned[:, w : w + 1]
        region = code_ref[0, w : w + 1, :]
        region = jnp.where(region < 0.0, region + 16.0, region)
        equal = jnp.broadcast_to(of_key[0:KP], (KP, LANES)) == jnp.broadcast_to(region, (KP, LANES))
        mask_ref[w] = jnp.where(equal | same, 0.0, NEG)
        vsc[CELLS * w : CELLS * w + 104, :] = jnp.broadcast_to(jnp.where(of_key[0:104] >= 0.0, 1.0, 0.0), (104, LANES))
    vld_ref[...] = vsc[0:GR, :]
    hp = h1p[...]
    q_ref[...] = (nn(hp, w_ref[:, 0:D]) + rowv_ref[2:3, :]).astype(bf16)
    kn[...] = nn(hp, w_ref[:, D : 2 * D]).astype(bf16)
    v_ref[...] = (nn(hp, w_ref[:, 2 * D : 3 * D]) + rowv_ref[3:4, :]).astype(bf16)
    for src, dst in ((q_ref, qT), (kn, kT_ref), (v_ref, vT)):
        for w in range(GW):
            for a in range(D // LANES):
                rows, cols = slice(LANES * w, LANES * w + LANES), slice(LANES * a, LANES * a + LANES)
                dst[cols, rows] = src[rows, cols].T
    factor = HD**-0.5 * LOG2E

    def window(w, carry):
        start = pl.multiple_of(w * LANES, LANES)
        at = pl.ds(start, LANES)
        allowed = mask_ref[w]
        for g in range(4):
            cols = slice(LANES * g, LANES * g + LANES)
            s = nn(by_head(kn[pl.ds(start, KP), cols]), qT[cols, at])
            ps = []
            for q in range(4):
                h = 4 * g + q
                t = s[KP * q : KP * q + KP] * factor + bias_ref[h] + allowed
                e = jnp.exp2(t - jnp.max(t, axis=0, keepdims=True))
                p = (e * (1.0 / jnp.sum(e, axis=0, keepdims=True))).astype(bf16)
                pT_ref[w, h] = p
                ps.append(p)
            o = [nn(vT[LANES * g + HD * q : LANES * g + HD * q + HD, at][:, 0:KP], ps[q]) for q in range(4)]
            oT_ref[cols, at] = jnp.concatenate(o, axis=0).astype(bf16)
        return carry

    lax.fori_loop(0, GW, window, 0, unroll=4)
    for w in range(GW):
        for a in range(D // LANES):
            osc[CELLS * w : CELLS * w + 104, LANES * a : LANES * a + LANES] = (
                oT_ref[LANES * a : LANES * a + LANES, LANES * w : LANES * w + LANES].T[0:112].astype(f32)[0:104]
            )
    o_ref[...] = osc[0:GR, :].astype(bf16)


def any_specs(n):
    return [pl.BlockSpec(memory_space=pl.ANY)] * n


SMEM = pl.BlockSpec(memory_space=pltpu.SMEM)


def attn_fwd(me, x, codes, bias, plan, pieces, rpd, per, count):
    n = x.shape[0] // GR
    copies = sum(1 if r is None else 2 * len(r) for r in plan)
    rb = pl.BlockSpec((GR, D), lambda i: (i, 0))
    tb = pl.BlockSpec((D, GL), lambda i: (0, i))
    pb = pl.BlockSpec((GL, D), lambda i: (i, 0))
    return pl.pallas_call(
        functools.partial(attn_fwd_body, plan=plan, rpd=rpd, per=per),
        grid=(n,),
        in_specs=[SMEM, rb, pl.BlockSpec((1, 2 * GW, LANES), lambda i: (i, 0, 0)), whole((HEADS, KP, LANES))]
        + any_specs(len(pieces)),
        out_specs=[
            tb,
            rb,
            pb,
            tb,
            pb,
            pl.BlockSpec((GW, HEADS, KP, LANES), lambda i: (i, 0, 0, 0)),
            pl.BlockSpec((D + 16, GL), lambda i: (0, i)),
            pl.BlockSpec((GR, LANES), lambda i: (i, 0)),
            whole((D, 3 * D)),
            whole((16, D)),
        ],
        out_shape=[
            sds((D, n * GL), bf16),
            sds((n * GR, D), bf16),
            sds((n * GL, D), bf16),
            sds((D, n * GL), bf16),
            sds((n * GL, D), bf16),
            sds((n * GW, HEADS, KP, LANES), bf16),
            sds((D + 16, n * GL), bf16),
            sds((n * GR, LANES), f32),
            sds((D, 3 * D), bf16),
            sds((16, D), f32),
        ],
        scratch_shapes=[
            pltpu.VMEM((GR + 8, D), f32),
            pltpu.VMEM((GL, D), bf16),
            pltpu.VMEM((D, GL), bf16),
            pltpu.VMEM((GL, D), bf16),
            pltpu.VMEM((D, GL), bf16),
            pltpu.VMEM((GR + 8, D), f32),
            pltpu.VMEM((GR + 8, LANES), f32),
            pltpu.VMEM((GW, KP, LANES), f32),
            pltpu.VMEM((count, max(rpd, 16), LANES), bf16),
            pltpu.SemaphoreType.DMA((copies,)),
        ],
        compiler_params=params(60),
        cost_estimate=pl.CostEstimate(flops=10**7, bytes_accessed=10**5, transcendentals=0),
        name="attn_fwd",
    )(me, x, codes, bias, *pieces)


def mlp_body(me_ref, vld_ref, rowv_ref, x_any, o_any, g_any, *refs, plan, rows, owners, rpd, groups):
    pieces = refs[: len(plan)]
    refs = refs[len(plan) :]
    res_any, dmid_any, p_any, first_any, second_any, third_ref, vec_ref, dbf1_ref, st_ref = refs[:9]
    xb, ob, gp, gT, h2, h2T, mid, dh2, es, dus, u4, vv, pp, res, pk, sem, sem_x, sem_o, sem_p, sem_g, sem_du, sem_dv, sem_dp, sem_r, sem_m = refs[9:]
    j = pl.program_id(0)
    last = FF // 512 - 1
    padded = h2.shape[0]
    blocks = rows // GR
    me = me_ref[0]
    proj_bias = rowv_ref[4:5, :]
    gain = rowv_ref[5:6, :]
    shift = rowv_ref[6:7, :]

    def weights():
        first, later = [], []
        count = 0
        for ref, rels in zip(pieces, plan):
            if rels is None:
                dst = (pp, u4, vv)[count]
                (first if count == 0 else later).append(pltpu.make_async_copy(ref, dst, sem.at[count]))
                count += 1
                continue
            for t, r in enumerate(rels):
                at = pl.ds(pl.multiple_of((r ^ me) * rpd, rpd), rpd)
                first.append(pltpu.make_async_copy(ref.at[t, 0], pp.at[at, :], sem.at[count]))
                later.append(pltpu.make_async_copy(ref.at[t, pl.ds(1, 4)], u4.at[:, at, :], sem.at[count + 1]))
                to = vv.at[pl.ds(pl.multiple_of((r ^ me) * 4, 4), 4)]
                later.append(pltpu.make_async_copy(ref.at[t, pl.ds(5, 4)], to, sem.at[count + 2]))
                count += 3
        return first, later

    def rows_of(k):
        return pl.ds(k * GR, GR)

    def grads_out(j):
        if not owners:
            cols = pl.ds(pl.multiple_of(j * 512, 512), 512)
            return [
                pltpu.make_async_copy(pk.at[0], first_any.at[:, cols], sem_du.at[j, 0]),
                pltpu.make_async_copy(pk.at[1], second_any.at[cols, :], sem_du.at[j, 1]),
            ]
        at = pl.ds(pl.multiple_of(j * rpd, rpd), rpd)
        low = pl.ds(4 * rpd, 4 * rpd)
        out = []
        for c, to in enumerate((first_any, second_any)):
            out.append(pltpu.make_async_copy(pk.at[c, :, at, :], to.at[:, at, :], sem_du.at[j, c]))
            for m in range(256 // (4 * rpd)):
                pos = place_of((j * (256 // (4 * rpd)) + m) ^ (me >> 1), [tuple(b - 1 for b in g) for g in groups[1:]])
                n = 2 * m + c
                out.append(pltpu.make_async_copy(pk.at[c, pos, low, :], to.at[pos, low, :], sem_dv.at[j, n]))
        return out

    @pl.when(j == 0)
    def _():
        first, later = weights()
        ins = []
        for c in first:
            c.start()
        for k in range(blocks):
            ins.append(pltpu.make_async_copy(x_any.at[rows_of(k)], xb.at[rows_of(k)], sem_x.at[k]))
            ins.append(pltpu.make_async_copy(o_any.at[rows_of(k)], ob.at[rows_of(k)], sem_o.at[k]))
        load_g = pltpu.make_async_copy(g_any, gp.at[pl.ds(0, rows)], sem_g.at[0])
        for c in ins + [load_g] + later:
            c.start()
        h2[rows:padded, :] = jnp.zeros((padded - rows, D), bf16)
        gp[rows:padded, :] = jnp.zeros((padded - rows, D), bf16)
        dus[rows:padded, :] = jnp.zeros((padded - rows, 512), bf16)
        for q in range(FF // 512):
            es[q, rows:padded, :] = jnp.zeros((padded - rows, 512), bf16)
        dh2[...] = jnp.zeros_like(dh2)
        for c in first:
            c.wait()
        store_p = pltpu.make_async_copy(pp, p_any, sem_p.at[0])
        store_p.start()
        squares = jnp.zeros((1, D), f32)
        for k in range(blocks):
            at = slice(k * GR, k * GR + GR)
            ins[2 * k].wait()
            ins[2 * k + 1].wait()
            a = nn(ob[at, :], pp[...]) + proj_bias
            squares = squares + jnp.sum(a * a * vld_ref[at, 0:1], axis=0, keepdims=True)
            m = xb[at, :].astype(f32) + a
            mid[at, :] = m
            c = m - jnp.mean(m, axis=-1, keepdims=True)
            var = jnp.mean(c * c, axis=-1, keepdims=True)
            h2[at, :] = (c * lax.rsqrt(var + 1e-5) * gain + shift).astype(bf16)
        st_ref[...] = jnp.zeros_like(st_ref)
        st_ref[1:2, :] = squares
        load_g.wait()

        def turn(k, carry):
            at = pl.ds(pl.multiple_of(k * LANES, LANES), LANES)
            for a in range(D // LANES):
                cols = slice(LANES * a, LANES * a + LANES)
                h2T[cols, at] = h2[at, cols].T
                gT[cols, at] = gp[at, cols].T
            return carry

        lax.fori_loop(0, padded // LANES, turn, 0)
        for c in later:
            c.wait()
        store_p.wait()

    up = u4[j]
    down = vv[pl.ds(pl.multiple_of(32 * j, 32), 32)].reshape(512, D)
    up_bias = rowv_ref[pl.ds(8 + j, 1), :]

    def products(k):
        at = slice(k * GR, k * GR + GR)
        return nn(h2[at, :], up) + up_bias, nt(gp[at, :], down)

    up_sum = jnp.zeros((1, 512), f32)
    ahead = products(0)
    for k in range(blocks):
        u, de = ahead
        if k + 1 < blocks:
            ahead = products(k + 1)
        at = slice(k * GR, k * GR + GR)
        cdf = 0.5 * lax.erf(u * RT2) + 0.5
        es[j, at, :] = (u * cdf).astype(bf16)
        du = de * (cdf + u * (PHI * jnp.exp2(u * u * (-0.5 * LOG2E))))
        dus[at, :] = du.astype(bf16)
        up_sum = up_sum + jnp.sum(du, axis=0, keepdims=True)
        dh2[at, :] += nt(dus[at, :], up)
    dbf1_ref[pl.ds(j, 1), :] = up_sum
    dU = nn(h2T[...], dus[...]).astype(bf16)
    dV = nn(gT[...], es[j]).astype(bf16).T
    if owners:
        at = pl.ds(pl.multiple_of(j * rpd, rpd), rpd)
        for k in range(owners):
            pk[(k ^ me) & 1, place_of(k ^ me, groups[1:]), at, :] = dU[rpd * k : rpd * k + rpd]
        per = 512 // (4 * rpd)
        for k in range(per):
            rel = (j * per + k) ^ me
            pk[rel & 1, place_of(rel, groups[1:]), 4 * rpd : 8 * rpd, :] = dV[4 * rpd * k : 4 * rpd * k + 4 * rpd]
        for c in grads_out(j):
            c.start()
    else:
        pk[0] = dU
        pk[1] = dV
        for c in grads_out(j):
            c.start()
        for c in grads_out(j):
            c.wait()

    @pl.when(j == last)
    def _():
        zero = jnp.zeros((1, D), f32)
        sums = [zero] * 4
        stats = [zero] * 5
        outs = []
        proj = jnp.zeros((D, D), f32)
        for k in range(blocks):
            at = slice(k * GR, k * GR + GR)
            m = mid[at, :]
            c = m - jnp.mean(m, axis=-1, keepdims=True)
            rs = lax.rsqrt(jnp.mean(c * c, axis=-1, keepdims=True) + 1e-5)
            xh = c * rs
            d = dh2[at, :]
            dx = d * gain
            dxx = d * xh
            m1 = jnp.mean(dx, axis=-1, keepdims=True)
            m2 = jnp.mean(dxx * gain, axis=-1, keepdims=True)
            grad = gp[at, :].astype(f32)
            dm = grad + (dx - m1 - xh * m2) * rs
            dh2[at, :] = dm
            outs.append(pltpu.make_async_copy(dh2.at[rows_of(k)], dmid_any.at[rows_of(k)], sem_m.at[k]))
            outs[-1].start()
            da = dm.astype(bf16)
            proj = proj + tn(ob[at, :], da)
            terms = (da.astype(f32), dxx, d, grad)
            sums = [a + jnp.sum(t, axis=0, keepdims=True) for a, t in zip(sums, terms)]
            f = rowv_ref[7:8, :]
            for b in range(4):
                f = f + nn(es[b, at, :], vv[32 * b : 32 * b + 32].reshape(512, D))
            out = m + f
            res[at, :] = out.astype(bf16)
            outs.append(pltpu.make_async_copy(res.at[rows_of(k)], res_any.at[rows_of(k)], sem_r.at[k]))
            outs[-1].start()
            vl = vld_ref[at, 0:1]
            x = xb[at, :].astype(f32)
            terms = (x * x * vl, m * m * vl, f * f * vl, out * out * vl, jnp.broadcast_to(vl, (GR, D)))
            stats = [a + jnp.sum(t, axis=0, keepdims=True) for a, t in zip(stats, terms)]
        for q in range(4):
            vec_ref[q : q + 1, :] = sums[q]
        vec_ref[4:8, :] = jnp.zeros((4, D), f32)
        dbf1_ref[4:8, :] = jnp.zeros((4, D), f32)
        for q, t in zip((0, 2, 3, 4, 5), stats):
            st_ref[q : q + 1, :] = t
        if owners:
            proj = proj.astype(bf16)
            at = pl.ds(8 * rpd, rpd)
            for k in range(owners):
                pk[(k ^ me) & 1, place_of(k ^ me, groups[1:]), at, :] = proj[rpd * k : rpd * k + rpd]
            third_ref[...] = jnp.zeros_like(third_ref)
            for c, to in enumerate((first_any, second_any)):
                outs.append(pltpu.make_async_copy(pk.at[c, :, at, :], to.at[:, at, :], sem_dp.at[c]))
                outs[-1].start()
            for step in range(last + 1):
                outs += grads_out(step)
        else:
            third_ref[...] = proj
        for c in outs:
            c.wait()


def mlp(me, x, o, g, vld, rowv, plan, pieces, rpd, owners, count, groups):
    rows = x.shape[0]
    blocks = rows // GR
    steps = FF // 512
    padded = -(-rows // LANES) * LANES
    copies = sum(1 if r is None else 3 * len(r) for r in plan)
    if owners:
        grad_shapes = [sds((count // 2, 9 * rpd, 512), bf16)] * 2 + [sds((8, LANES), f32)]
        pk = (2, count // 2, 9 * rpd, 512)
    else:
        grad_shapes = [sds((D, FF), bf16), sds((FF, D), bf16), sds((D, D), f32)]
        pk = (2, 512, 512)
    dma = pltpu.SemaphoreType.DMA
    return pl.pallas_call(
        functools.partial(mlp_body, plan=plan, rows=rows, owners=count if owners else 0, rpd=rpd, groups=groups),
        grid=(steps,),
        in_specs=[SMEM, whole((rows, LANES)), whole((16, D))] + any_specs(3 + len(pieces)),
        out_specs=any_specs(5) + [whole(grad_shapes[2].shape)] + [whole((8, D))] * 3,
        out_shape=[sds((rows, D), bf16), sds((rows, D), f32), sds((D, D), bf16)] + grad_shapes + [sds((8, D), f32)] * 3,
        scratch_shapes=[
            pltpu.VMEM((rows, D), bf16),
            pltpu.VMEM((rows, D), bf16),
            pltpu.VMEM((padded, D), bf16),
            pltpu.VMEM((D, padded), bf16),
            pltpu.VMEM((padded, D), bf16),
            pltpu.VMEM((D, padded), bf16),
            pltpu.VMEM((rows, D), f32),
            pltpu.VMEM((rows, D), f32),
            pltpu.VMEM((steps, padded, 512), bf16),
            pltpu.VMEM((padded, 512), bf16),
            pltpu.VMEM((steps, D, 512), bf16),
            pltpu.VMEM((FF // 16, 16, D), bf16),
            pltpu.VMEM((D, D), bf16),
            pltpu.VMEM((rows, D), bf16),
            pltpu.VMEM(pk, bf16),
            dma((copies,)),
            dma((blocks,)),
            dma((blocks,)),
            dma((1,)),
            dma((1,)),
            dma((steps, 2)),
            dma((steps, max(1, 512 // (4 * rpd)))),
            dma((2,)),
            dma((blocks,)),
            dma((blocks,)),
        ],
        compiler_params=params(52),
        cost_estimate=pl.CostEstimate(flops=10**7, bytes_accessed=10**5, transcendentals=0),
        name="mlp",
    )(me, vld, rowv, x, o, g, *pieces)


def attn_bwd_body(me_ref, dmid_ref, p_ref, oT_ref, q_ref, kT_ref, v_ref, pT_ref, xT_ref, w_any, rowv_ref, *refs, owners, rpd, groups):
    dm_ref, acc_ref, vec_ref = refs[:3]
    grads = refs[3:-7]
    xs, dap, don, doT, dw, w_ref, sem_w = refs[-7:]
    i = pl.program_id(0)
    load_w = pltpu.make_async_copy(w_any, w_ref, sem_w.at[0])

    @pl.when(i == 0)
    def _():
        load_w.start()
        acc_ref[...] = jnp.zeros_like(acc_ref)
        dw[...] = jnp.zeros_like(dw)

    xs[0:GR, :] = dmid_ref[...]
    for w in range(GW):
        dap[LANES * w : LANES * w + LANES, :] = pad_window(xs[CELLS * w : CELLS * w + 104, :])
        dm_ref[LANES * w + KP : LANES * w + LANES, :] = jnp.zeros((LANES - KP, 3 * D), bf16)
    da = dap[...]
    don[...] = nt(da, p_ref[...]).astype(bf16)
    for w in range(GW):
        for a in range(D // LANES):
            rows, cols = slice(LANES * w, LANES * w + LANES), slice(LANES * a, LANES * a + LANES)
            doT[cols, rows] = don[rows, cols].T
    factor = HD**-0.5

    def window(w, carry):
        start = pl.multiple_of(w * LANES, LANES)
        at = pl.ds(start, LANES)
        keys = pl.ds(start, KP)
        for g in range(4):
            c0 = LANES * g
            cols = slice(c0, c0 + LANES)
            dp = nn(by_head(v_ref[keys, cols]), doT[cols, at])
            dss = []
            for q in range(4):
                h = 4 * g + q
                head = slice(HD * h, HD * h + HD)
                delta = jnp.sum(doT[head, at].astype(f32) * oT_ref[head, at].astype(f32), axis=0, keepdims=True)
                ds = pT_ref[w, h].astype(f32) * (dp[KP * q : KP * q + KP] - delta)
                acc_ref[h] += ds
                dss.append(ds.astype(bf16))
            dq = [nn(kT_ref[c0 + HD * q : c0 + HD * q + HD, at][:, 0:KP], dss[q]) for q in range(4)]
            dm_ref[at, cols] = (jnp.concatenate(dq, axis=0) * factor).astype(bf16).T
            dk = nn(jnp.concatenate(dss, axis=1), by_head(q_ref[at, cols])) * factor
            dm_ref[keys, D + c0 : D + c0 + LANES] = dk.astype(bf16)
            dv = nn(jnp.concatenate([pT_ref[w, 4 * g + q] for q in range(4)], axis=1), by_head(don[at, cols]))
            dm_ref[keys, 2 * D + c0 : 2 * D + c0 + LANES] = dv.astype(bf16)
        return carry

    lax.fori_loop(0, GW, window, 0, unroll=4)
    dw[...] += nn(xT_ref[...], dm_ref[...])

    @pl.when(i == pl.num_programs(0) - 1)
    def _():
        load_w.wait()
        s = dw[D : D + 1, :]
        vec_ref[...] = jnp.zeros_like(vec_ref)
        vec_ref[0:1, :] = s
        for a in range(D // LANES):
            rows = slice(LANES * a, LANES * a + LANES)
            col = rowv_ref[0:8, rows].T
            x = dw[rows, :]
            wt = w_ref[rows, :].astype(f32)
            by_gain = jnp.broadcast_to(jnp.sum(wt * x, axis=1, keepdims=True), (LANES, LANES)).T
            by_shift = jnp.broadcast_to(jnp.sum(wt * s, axis=1, keepdims=True), (LANES, LANES)).T
            vec_ref[1:2, rows] = by_gain[0:1]
            vec_ref[2:3, rows] = by_shift[0:1]
            dw[rows, :] = col[:, 0:1] * x + col[:, 1:2] * s
        if owners:
            me = me_ref[0]
            for k in range(owners):
                rel = k ^ me
                pos = place_of(rel, groups[1:])
                mine = slice(rpd * k, rpd * k + rpd)

                def store(to, mine=mine, pos=pos):
                    for q in range(3):
                        to[pos, rpd * q : rpd * q + rpd, :] = dw[mine, D * q : D * q + D].astype(bf16)

                pl.when(rel & 1 == 0)(functools.partial(store, grads[0]))
                pl.when(rel & 1 == 1)(functools.partial(store, grads[1]))
        else:
            grads[0][...] = dw[0:D, :].astype(bf16)


def attn_bwd(me, dmid, p, oT, q, kT, v, pT, xT, w, rowv, rpd, owners, count, groups):
    n = q.shape[0] // GL

    def tb(r):
        return pl.BlockSpec((r, GL), lambda i: (0, i))

    pb = pl.BlockSpec((GL, D), lambda i: (i, 0))
    if owners:
        grad_shapes = [sds((count // 2, 3 * rpd, D), bf16)] * 2
    else:
        grad_shapes = [sds((D, 3 * D), bf16)]
    return pl.pallas_call(
        functools.partial(attn_bwd_body, owners=count if owners else 0, rpd=rpd, groups=groups),
        grid=(n,),
        in_specs=[SMEM, pl.BlockSpec((GR, D), lambda i: (i, 0)), whole((D, D)), tb(D), pb, tb(D), pb, pl.BlockSpec((GW, HEADS, KP, LANES), lambda i: (i, 0, 0, 0)), tb(D + 16), pl.BlockSpec(memory_space=pl.ANY), whole((16, D))],
        out_specs=[pl.BlockSpec((GL, 3 * D), lambda i: (i, 0)), whole((HEADS, KP, LANES)), whole((8, 3 * D))] + [whole(s.shape) for s in grad_shapes],
        out_shape=[sds((n * GL, 3 * D), bf16), sds((HEADS, KP, LANES), f32), sds((8, 3 * D), f32)] + grad_shapes,
        scratch_shapes=[
            pltpu.VMEM((GR + 8, D), f32),
            pltpu.VMEM((GL, D), bf16),
            pltpu.VMEM((GL, D), bf16),
            pltpu.VMEM((D, GL), bf16),
            pltpu.VMEM((D + 16, 3 * D), f32),
            pltpu.VMEM((D, 3 * D), bf16),
            pltpu.SemaphoreType.DMA((1,)),
        ],
        compiler_params=params(60),
        cost_estimate=pl.CostEstimate(flops=10**7, bytes_accessed=10**5, transcendentals=0),
        name="attn_bwd",
    )(me, dmid, p, oT, q, kT, v, pT, xT, w, rowv)


def grad_in_body(dm_ref, w_ref, x_ref, dmid_ref, rowv_ref, tg_ref, dsc):
    dh = nt(dm_ref[...], w_ref[...])
    for w in range(GW):
        dsc[CELLS * w : CELLS * w + 104, :] = dh[LANES * w : LANES * w + 104]
    x = x_ref[...].astype(f32)
    c = x - jnp.mean(x, axis=-1, keepdims=True)
    rs = lax.rsqrt(jnp.mean(c * c, axis=-1, keepdims=True) + 1e-5)
    xh = c * rs
    dx = dsc[0:GR, :] * rowv_ref[0:1, :]
    m1 = jnp.mean(dx, axis=-1, keepdims=True)
    m2 = jnp.mean(dx * xh, axis=-1, keepdims=True)
    tg_ref[...] = dmid_ref[...] + (dx - m1 - xh * m2) * rs


def grad_in(dm, w, x, dmid, rowv):
    n = x.shape[0] // GR
    rb = pl.BlockSpec((GR, D), lambda i: (i, 0))
    return pl.pallas_call(
        grad_in_body,
        grid=(n,),
        in_specs=[pl.BlockSpec((GL, 3 * D), lambda i: (i, 0)), whole((D, 3 * D)), rb, rb, whole((16, D))],
        out_specs=rb,
        out_shape=sds((n * GR, D), f32),
        scratch_shapes=[pltpu.VMEM((GR + 8, D), f32)],
        compiler_params=params(60),
        cost_estimate=pl.CostEstimate(flops=10**7, bytes_accessed=10**5, transcendentals=0),
        name="grad_in",
    )(dm, w, x, dmid, rowv)


SMALL = 24
SENT = 32


def to_send(small):
    lane = lax.broadcasted_iota(jnp.int32, small.shape, 1)
    lane = jnp.where(lax.broadcasted_iota(jnp.int32, small.shape, 0) >= 8, lane, -1)
    small = jnp.where(lane == RELN, small + pltpu.roll(small, D - 1, 1), small)
    hi = small.astype(bf16).astype(f32)
    small = jnp.where(lane == RELN + 1, pltpu.roll(small - hi, 1, 1), hi)
    return jnp.concatenate([small, jnp.zeros((SENT - SMALL, D), f32)], axis=0).astype(bf16)


def sent_sums(terms):
    got = [t.astype(f32)[0:SMALL] for t in terms]
    while len(got) > 1:
        got = [got[k] + got[k + 1] for k in range(0, len(got), 2)]
    return got[0]


def fold_body(*refs, first, terms, parts):
    ins, outs = refs[: 2 * terms if first else terms + 1], refs[2 * terms if first else terms + 1 :]
    nb, rows = ins[0].shape[0], ins[0].shape[1]
    n = nb // (parts + 1)
    if first:
        small = ins[2][...] + ins[3][...]
    else:
        small = sent_sums([ins[1][...]] + [r[nb * rows :, :] for r in ins[2:]])
    for p in range(parts + 1):
        at = slice(p * n, p * n + n)
        total = ins[0][at].astype(f32)
        if first:
            total = total + ins[1][at].astype(f32)
        else:
            for r in ins[2:]:
                total = total + r[p * n * rows : (p + 1) * n * rows, :].astype(f32).reshape(n, rows, D)
        if p == 0:
            outs[0][...] = total
            outs[1][...] = to_send(small)
        else:
            outs[p + 1][0 : n * rows, :] = total.reshape(n * rows, D).astype(bf16)
            outs[p + 1][n * rows :, :] = to_send(small)


def fold(arrays, parts, first=False):
    terms = 2 if first else len(arrays) - 1
    nb, rows = arrays[0].shape[:2]
    n = nb // (parts + 1)
    return pl.pallas_call(
        functools.partial(fold_body, first=first, terms=terms, parts=parts),
        out_shape=[sds((n, rows, D), f32), sds((SENT, D), bf16)] + [sds((n * rows + SENT, D), bf16)] * parts,
        compiler_params=params(16),
        cost_estimate=pl.CostEstimate(flops=10**6, bytes_accessed=10**5, transcendentals=0),
        name="fold",
    )(*arrays)


def add_body(*refs, terms):
    ins, outs = refs[:terms], refs[terms:]
    n = outs[0].shape[0]
    for p, out in enumerate(outs):
        at = slice(p * n, p * n + n)
        total = ins[0][at].astype(f32)
        for r in ins[1:]:
            total = total + r[at].astype(f32)
        out[...] = total.astype(out.dtype)


def add_split(terms, group):
    parts = len(masks_of(group))
    shape = (terms[0].shape[0] // (parts + 1),) + terms[0].shape[1:]
    out = pl.pallas_call(
        functools.partial(add_body, terms=len(terms)),
        out_shape=[sds(shape, f32)] + [sds(shape, bf16)] * parts,
        compiler_params=params(24),
        cost_estimate=pl.CostEstimate(flops=10**6, bytes_accessed=10**5, transcendentals=0),
        name="add_split",
    )(*terms)
    return out[0], out[1:]


def spread(o_ref, block, width, at):
    each = width // LANES
    for b in range(block.shape[1] // LANES):
        o_ref[pl.ds(at // LANES + b, block.shape[0], stride=each), :] = block[:, LANES * b : LANES * b + LANES]


def attn_last_body(me_ref, own_ref, kept_ref, *refs, rpd, per):
    got_refs, (qkv_ref, vec_ref, table_ref, stats_ref, lines) = refs[:-5], refs[-5:]
    rows = own_ref.shape[1]
    total = own_ref[0]
    for r in got_refs:
        total = total + r[0:rows, :].astype(f32)
    for q in range(3):
        spread(qkv_ref, total[rpd * q : rpd * q + rpd], 3 * D, D * q)
    small = sent_sums([kept_ref[...]] + [r[rows:, :] for r in got_refs])
    for k in range(8):
        for a in range(4):
            lines[4 * k + a : 4 * k + a + 1, :] = small[k : k + 1, LANES * a : LANES * a + LANES]
    lines[32:48, :] = small[8:24, RP:D]
    if per % 64:
        vec_ref[...] = lines[...]
    else:
        low = lax.broadcasted_iota(jnp.int32, (1, LANES), 1) < 64
        for p in range(0, per // 64, 2):
            halves = []
            for k in range(2):
                c = me_ref[0] * (per // 64) + min(p + k, per // 64 - 1)
                line = lines[pl.ds(c >> 1, 1), :]
                halves.append(jnp.where(c & 1 == k, line, pltpu.roll(line, 64, 1)))
            vec_ref[p // 2 : p // 2 + 1, :] = jnp.where(low, halves[0], halves[1])
    table_ref[...] = small[8:24, 0:RELN]
    turned = small[8:24, RP - LANES : RP].T
    at = RELN - (RP - LANES)
    line = turned[at : at + 1] + turned[at + 1 : at + 2]
    stats_ref[...] = jnp.sqrt(line / line[:, 5:6] + 1e-06)


def attn_last(me, arrays, rpd, per):
    lines = -(-per // LANES) if per % 64 == 0 else 48
    return pl.pallas_call(
        functools.partial(attn_last_body, rpd=rpd, per=per),
        in_specs=[SMEM] + [pl.BlockSpec(memory_space=pltpu.VMEM)] * len(arrays),
        out_shape=[sds((12 * rpd, LANES), f32), sds((lines, LANES), f32), sds((HEADS, RELN), f32), sds((1, HEADS), f32)],
        scratch_shapes=[pltpu.VMEM((48, LANES), f32)],
        compiler_params=params(16),
        cost_estimate=pl.CostEstimate(flops=10**6, bytes_accessed=10**5, transcendentals=0),
        name="attn_last",
    )(me, *arrays)


def mlp_last_body(own_ref, *refs, rpd):
    total = own_ref[0]
    for r in refs[:-3]:
        total = total + r[0].astype(f32)
    for q in range(4):
        spread(refs[-3], total[rpd * q : rpd * q + rpd], FF, 512 * q)
    spread(refs[-2], total[4 * rpd : 8 * rpd], D, 0)
    spread(refs[-1], total[8 * rpd :], D, 0)


def mlp_last(arrays, rpd):
    return pl.pallas_call(
        functools.partial(mlp_last_body, rpd=rpd),
        out_shape=[sds((16 * rpd, LANES), f32)] * 2 + [sds((4 * rpd, LANES), f32)],
        compiler_params=params(16),
        cost_estimate=pl.CostEstimate(flops=10**6, bytes_accessed=10**5, transcendentals=0),
        name="mlp_last",
    )(*arrays)


def place_hits(shape, axis, rev=0):
    c = lax.broadcasted_iota(jnp.int32, shape, 1 - axis)
    code = jnp.where(c < CELLS, (2 * WSIDE - 1) * (c // WSIDE) + c % WSIDE, -1000)
    if rev:
        code = rev - code
    return jnp.where(code == lax.broadcasted_iota(jnp.int32, shape, axis), 1.0, 0.0).astype(bf16)


def rel_bias_body(t_ref, o_ref):
    keys = place_hits((KP, 192), 1)
    queries = place_hits((256, LANES), 0)

    def head(h, carry):
        row = pltpu.roll(jnp.broadcast_to(t_ref[pl.ds(h, 1), :], (8, RP)), 0, 1, stride=1, stride_axis=0)
        t = jnp.concatenate([pltpu.roll(row, (8 * k - 180) % RP, 1)[:, 0:256] for k in range(24)], axis=0)
        hi = t.astype(bf16)
        lo = (t - hi.astype(f32)).astype(bf16)
        b = nn(jnp.concatenate([hi, lo], axis=0), queries).astype(bf16)
        b = nn(keys, jnp.concatenate([b[0:192], b[192:384]], axis=1))
        o_ref[h] = b[:, 0:LANES] + b[:, LANES : 2 * LANES]
        return carry

    lax.fori_loop(0, HEADS, head, 0, unroll=8)


def rel_bias(table):
    return pl.pallas_call(
        rel_bias_body,
        out_shape=sds((HEADS, KP, LANES), f32),
        compiler_params=params(16),
        cost_estimate=pl.CostEstimate(flops=2 * 10**10, bytes_accessed=10**6, transcendentals=0),
        name="rel_bias",
    )(table)


def rel_grad_body(a_ref, one_ref, two_ref, up_ref, squares_ref, o_ref):
    keys = place_hits((192, KP), 0, 191)
    queries = place_hits((LANES, 256), 1)
    zero = jnp.zeros((8, RP - 256), f32)
    o_ref[0:2, :] = one_ref[1:3, 0:D]
    o_ref[2:3, :] = one_ref[0:1, 0:D]
    o_ref[3:4, :] = one_ref[0:1, 2 * D : 3 * D]
    o_ref[4:8, :] = two_ref[0:4, :]

    def head(h, carry):
        a = a_ref[h]
        hi = a.astype(bf16)
        lo = (a - hi.astype(f32)).astype(bf16)
        b = nn(keys, jnp.concatenate([hi, lo], axis=1)).astype(bf16)
        b = nn(jnp.concatenate([b[:, 0:LANES], b[:, LANES : 2 * LANES]], axis=0), queries)
        b = b[0:192] + b[192:384]
        t = jnp.zeros((8, RP), f32)
        for k in range(24):
            t = t + pltpu.roll(jnp.concatenate([b[8 * k : 8 * k + 8], zero], axis=1), (8 * k - 11) % RP, 1)
        t = pltpu.roll(t, 0, 1, stride=1, stride_axis=0)
        o_ref[pl.ds(8 + h, 1), 0:RP] = jnp.sum(t, axis=0, keepdims=True)
        return carry

    lax.fori_loop(0, HEADS, head, 0, unroll=16)
    for k in range(4):
        for a in range(4):
            o_ref[8 + 4 * k + a : 9 + 4 * k + a, RP:D] = up_ref[k : k + 1, LANES * a : LANES * a + LANES]
    for k in range(6):
        o_ref[8 + k : 9 + k, RELN : RELN + 1] = jnp.sum(squares_ref[k : k + 1, :], axis=1, keepdims=True)
        o_ref[8 + k : 9 + k, RELN + 1 : RELN + 2] = jnp.zeros((1, 1), f32)


def rel_grad(acc, one, two, up, squares):
    return pl.pallas_call(
        rel_grad_body,
        out_shape=sds((SMALL, D), f32),
        compiler_params=params(16),
        cost_estimate=pl.CostEstimate(flops=10**7, bytes_accessed=10**5, transcendentals=0),
        name="rel_grad",
    )(acc, one, two, up, squares)


def shards(tokens, cotangent, regions, validity, qkv_weight, proj_weight, fc1_weight, fc2_weight, vectors, rel_table, *, count, inner):
    rows = tokens.shape[0]
    groups = bit_groups(count)
    single = groups[:2] + [(b,) for g in groups[2:] for b in g]
    rpd = D // count
    direct = rpd % 16 == 0
    me = lax.axis_index("dp") * inner + lax.axis_index("shard")
    me_s = me.astype(jnp.int32).reshape(1)

    per = vectors.shape[0]
    if direct:
        own = jnp.pad(vectors, (0, rpd * LANES - per)).reshape(rpd, LANES)
        own = jnp.concatenate([qkv_weight.reshape(rpd, 3 * D), own], axis=1)
    else:
        own = jnp.concatenate([qkv_weight, vectors]).reshape(1, -1)
    rels, attn_up = gather_upper(own, groups, count)
    up_rows = fc1_weight.reshape(rpd, FF)
    packed = jnp.concatenate(
        [proj_weight.reshape(rpd, D)] + [up_rows[:, 512 * q : 512 * q + 512] for q in range(4)] + [fc2_weight.reshape(4 * rpd, D)], axis=0
    )
    attn_pieces = gather_plane(rels, attn_up, groups, count)
    table_in = after(rel_table, attn_up)
    mlp_rels, mlp_up = gather_upper(packed, single, count, attn_up)

    bias = rel_bias(jnp.pad(table_in.T * LOG2E, ((0, 0), (0, RP - RELN))))
    codes = jnp.where(validity == 1, regions, regions - 16).astype(f32).reshape(-1, GW, CELLS)
    codes = jnp.pad(codes, ((0, 0), (0, 8 - GW), (0, LANES - CELLS)), constant_values=-100.0)

    attn_pieces = hold(attn_pieces, bias, codes)
    mlp_up = after(mlp_up, bias, codes, [a for _, a in attn_pieces])
    attn_pieces = gather_core(attn_pieces, count)
    mlp_pieces = gather_plane(mlp_rels, mlp_up, groups, count)
    if direct:
        attn_plan = [r for r, _ in attn_pieces]
        attn_w = [a for _, a in attn_pieces]
    else:
        attn_plan = [None] * 2
        both = natural_order(attn_pieces, me, count).reshape(count, -1)
        attn_w = [both[:, : 3 * D * rpd].reshape(D, 3 * D), jnp.pad(both[:, 3 * D * rpd :].astype(f32).reshape(12, D), ((0, 4), (0, 0)))]

    x = after(tokens, mlp_up)
    oT, o, q, kT, v, pT, xT, vld, w_full, rowv = attn_fwd(me_s, x, codes, bias, attn_plan, attn_w, rpd, per, count)

    mlp_pieces = gather_core(hold(mlp_pieces, o), count)
    if direct:
        mlp_plan = [r for r, _ in mlp_pieces]
        mlp_w = [a.reshape(-1, 9, rpd, D) for _, a in mlp_pieces]
    else:
        both = natural_order(mlp_pieces, me, count).reshape(count, 9, rpd, D)
        mlp_plan = [None] * 3
        mlp_w = [both[:, 0].reshape(D, D), both[:, 1:5].transpose(1, 0, 2, 3).reshape(4, D, 512), both[:, 5:].reshape(128, 16, D)]
    result, dmid, p_full, mlp_keep, mlp_send, dproj, vec_two, dbf1, squares = mlp(
        me_s, tokens, o, cotangent, vld, rowv, mlp_plan, mlp_w, rpd, direct, count, single
    )
    order = None
    if not direct:
        blocks = jnp.arange(count)
        order, mlp_order = (
            jnp.zeros((count,), jnp.int32).at[place_of(blocks, way)].set(blocks.astype(jnp.int32)) ^ me for way in (groups, single)
        )
        dU = mlp_keep.reshape(count, rpd, 4, 512).transpose(0, 2, 1, 3).reshape(count, 4 * rpd, 512)
        pk = [dU, mlp_send.reshape(count, 4 * rpd, D), dproj.astype(bf16).reshape(count, rpd, D)]
        pk = jnp.take(jnp.concatenate(pk, axis=1), mlp_order, axis=0)
        mlp_keep, mlp_send = pk[: count // 2], pk[count // 2 :]

    other = swap(mlp_send, 1, count)
    mlp_own, parts = add_split([mlp_keep, other], groups[1])
    mlp_got = send_parts(parts, groups[1], count)
    dmid = after(dmid, parts)
    got = attn_bwd(me_s, dmid, p_full, oT, q, kT, v, pT, xT, w_full, rowv, rpd, direct, count, groups)
    dm, score_sums, vec_one = got[:3]
    if direct:
        attn_keep, attn_send = got[3:]
    else:
        dW = got[3].reshape(count, rpd, 3, D).transpose(0, 2, 1, 3).reshape(count, 3 * rpd, D)
        pk = jnp.take(jnp.pad(dW, ((0, 0), (0, rpd), (0, 0))), order, axis=0)
        attn_keep, attn_send = pk[: count // 2], pk[count // 2 :]
    mlp_got, attn_send, score_sums, dm = lax.optimization_barrier((mlp_got, attn_send, score_sums, dm))

    other = swap(attn_send, 1, count)
    mlp_terms = [mlp_own] + mlp_got
    for g in single[2:3]:
        mlp_own, parts = add_split(mlp_terms, g)
        mlp_terms = [mlp_own] + send_parts(parts, g, count)
        score_sums = after(score_sums, parts)
    small = rel_grad(score_sums, vec_one, vec_two, dbf1, squares)
    other = after(other, small)
    levels = [len(masks_of(g)) for g in groups[1:]]
    out = fold([attn_keep, other, small, swap(small, 1, count)], levels[0], first=True)
    for k, g in enumerate(groups[1:]):
        own, kept, parts = out[0], out[1], out[2:]
        sent = send_parts(parts, g, count)
        if k == 0:
            mlp_terms = after(mlp_terms, parts)
            for up in single[3:]:
                mlp_own, parts = add_split(mlp_terms, up)
                mlp_terms = [mlp_own] + send_parts(parts, up, count)
            dm = after(dm, parts)
            grad_tokens = grad_in(dm, w_full, tokens, dmid, rowv)
            sent, mlp_terms = after((sent, mlp_terms), grad_tokens)
        if k + 1 < len(levels):
            out = fold([own, kept] + sent, levels[k + 1])
            mlp_terms = after(mlp_terms, out)
    grad_fc1, grad_fc2, grad_proj = mlp_last(mlp_terms, rpd)
    sent = after(sent, grad_fc1)
    grad_qkv, grad_vectors, grad_table, stats = attn_last(me_s, [own, kept] + sent, rpd, per)
    if per % 64 == 0:
        grad_vectors = grad_vectors.reshape(-1)[:per]
    else:
        grad_vectors = lax.dynamic_slice(grad_vectors.reshape(-1), (me * per,), (per,))
    return (
        result,
        grad_tokens,
        grad_qkv.reshape(-1),
        grad_proj.reshape(-1),
        grad_fc1.reshape(-1),
        grad_fc2.reshape(-1),
        grad_vectors,
        grad_table.T,
        stats[0, 0:5],
    )


def solution(mesh):
    flat = P(AXES)
    tall = P(AXES, None)
    in_specs = (tall, tall, flat, flat, flat, flat, flat, flat, flat, P())
    out_specs = (tall, tall, flat, flat, flat, flat, flat, P(), P())
    inner = mesh.shape["shard"]
    body = functools.partial(shards, count=mesh.shape["dp"] * inner, inner=inner)
    return jax.shard_map(body, mesh=mesh, in_specs=in_specs, out_specs=out_specs, check_vma=False)
```

```python
import functools

import jax
import jax.numpy as jnp
from jax import lax
from jax.experimental import pallas as pl
from jax.experimental.pallas import tpu as pltpu
from jax.sharding import PartitionSpec as P

D = 512
FF = 2048
HEADS = 16
HD = 32
WSIDE = 10
RELN = 361
CELLS = WSIDE * WSIDE
GW = 4
GR = GW * CELLS
KP = 112
LANES = 128
GL = GW * LANES
RP = 384
AXES = ("dp", "shard")
LOG2E = 1.4426950408889634
NEG = -1e9
RT2 = 0.7071067811865476
PHI = 0.3989422804014327
f32 = jnp.float32
bf16 = jnp.bfloat16
sds = jax.ShapeDtypeStruct


def nn(a, b):
    return lax.dot_general(a, b, (((1,), (0,)), ((), ())), preferred_element_type=f32)


def nt(a, b):
    return lax.dot_general(a, b, (((1,), (1,)), ((), ())), preferred_element_type=f32)


def tn(a, b):
    return lax.dot_general(a, b, (((0,), (0,)), ((), ())), preferred_element_type=f32)


def whole(shape):
    return pl.BlockSpec(shape, lambda i: (0,) * len(shape))


def params(mib):
    return pltpu.CompilerParams(vmem_limit_bytes=mib * 2**20)


def bit_groups(count):
    bits = count.bit_length() - 1
    groups = [(0,)]
    at = 1
    while at < bits:
        groups.append(tuple(range(at, min(at + 2, bits))))
        at += 2
    return groups


def masks_of(group):
    return [sum(((v >> k) & 1) << b for k, b in enumerate(group)) for v in range(1, 1 << len(group))]


def swap(x, mask, count):
    return lax.ppermute(x, AXES, [(i, i ^ mask) for i in range(count)])


def place_of(rel, groups):
    pos = 0
    for g in groups:
        pos = pos * (1 << len(g)) + ((rel >> g[0]) & ((1 << len(g)) - 1))
    return pos


def after(values, *others):
    return lax.optimization_barrier((values, others))[0]


def gather_upper(x, groups, count, *others):
    cur = x[None]
    rels = [0]
    for k, g in enumerate(groups[:1:-1]):
        if k and others:
            cur = after(cur, *others)
        ms = masks_of(g)
        cur = jnp.concatenate([cur] + [swap(cur, m, count) for m in ms], axis=0)
        rels = [r ^ m for m in [0] + ms for r in rels]
    return rels, cur


def gather_plane(rels, cur, groups, count):
    return [(rels, cur)] + [([r ^ m for r in rels], swap(cur, m, count)) for m in masks_of(groups[1])]


def gather_core(pieces, count):
    return pieces + [([r ^ 1 for r in rels], swap(arr, 1, count)) for rels, arr in pieces]


def hold(pieces, *others):
    held = after([a for _, a in pieces[1:]], *others)
    return pieces[:1] + [(r, a) for (r, _), a in zip(pieces[1:], held)]


def natural_order(pieces, me, count):
    rels = [r for rs, _ in pieces for r in rs]
    where = [0] * count
    for k, r in enumerate(rels):
        where[r] = k
    both = jnp.concatenate([a for _, a in pieces], axis=0)
    return jnp.take(both, jnp.asarray(where, jnp.int32)[jnp.arange(count) ^ me], axis=0)


def send_parts(parts, group, count):
    return [swap(p, m, count) for p, m in zip(parts, masks_of(group))]


def lay_vectors(raw, per, rowv_ref):
    unit = LANES // 2
    each = per // unit
    low = lax.broadcasted_iota(jnp.int32, (1, LANES), 1) < unit

    def half(c, high):
        owner, part = divmod(c, each)
        got = raw[owner, part // 2 : part // 2 + 1, :].astype(f32)
        return got if part % 2 == high else pltpu.roll(got, unit, 1)

    for m in range((8 * D + FF) // LANES):
        row, col = divmod(m * LANES, D)
        rowv_ref[row : row + 1, col : col + LANES] = jnp.where(low, half(2 * m, 0), half(2 * m + 1, 1))


def pad_window(rows):
    at = lax.broadcasted_iota(jnp.int32, (104, 1), 0)
    rows = jnp.where(at < CELLS, rows, 0.0)
    return jnp.concatenate([rows, jnp.zeros((LANES - 104, rows.shape[1]), f32)], axis=0).astype(bf16)


def head_lanes():
    return lax.broadcasted_iota(jnp.int32, (1, LANES), 1) // HD


def by_head(block):
    lane = head_lanes()
    return jnp.concatenate([jnp.where(lane == q, block, jnp.zeros_like(block)) for q in range(4)], axis=0)


def attn_fwd_body(me_ref, x_ref, code_ref, bias_ref, *refs, plan, rpd, per):
    pieces = refs[: len(plan)]
    (oT_ref, o_ref, q_ref, kT_ref, v_ref, pT_ref, xT_ref, vld_ref, w_ref, rowv_ref) = refs[len(plan) : len(plan) + 10]
    xs, h1p, qT, kn, vT, osc, vsc, mask_ref, raw, sem = refs[len(plan) + 10 :]

    @pl.when(pl.program_id(0) == 0)
    def _():
        copies = []
        for ref, rels in zip(pieces, plan):
            if rels is None:
                copies.append(pltpu.make_async_copy(ref, (w_ref, rowv_ref)[len(copies)], sem.at[len(copies)]))
                continue
            for t, r in enumerate(rels):
                at = pl.multiple_of((r ^ me_ref[0]) * rpd, rpd)
                copies.append(
                    pltpu.make_async_copy(
                        ref.at[t, :, pl.ds(0, 3 * D)], w_ref.at[pl.ds(at, rpd), :], sem.at[len(copies)]
                    )
                )
                copies.append(
                    pltpu.make_async_copy(ref.at[t, :, pl.ds(3 * D, LANES)], raw.at[r ^ me_ref[0]], sem.at[len(copies)])
                )
        for c in copies:
            c.start()
        for c in copies:
            c.wait()
        if plan[0] is not None:
            rowv_ref[12:16, :] = jnp.zeros((4, D), f32)
            lay_vectors(raw, per, rowv_ref)

    xs[0:GR, :] = x_ref[...].astype(f32)
    gain = rowv_ref[0:1, :]
    shift = rowv_ref[1:2, :]
    for w in range(GW):
        xw = xs[CELLS * w : CELLS * w + 104, :]
        c = xw - jnp.mean(xw, axis=-1, keepdims=True)
        var = jnp.mean(c * c, axis=-1, keepdims=True)
        xh = c * lax.rsqrt(var + 1e-5)
        h1p[LANES * w : LANES * w + LANES, :] = pad_window(xh * gain + shift)
        xh = pad_window(xh)
        for a in range(D // LANES):
            xT_ref[LANES * a : LANES * a + LANES, LANES * w : LANES * w + LANES] = xh[:, LANES * a : LANES * a + LANES].T
    xT_ref[D : D + 16, :] = jnp.ones((16, GL), bf16)
    turned = code_ref[0].T
    keys = lax.broadcasted_iota(jnp.int32, (KP, LANES), 0)
    same = (keys == lax.broadcasted_iota(jnp.int32, (KP, LANES), 1)) & (keys < CELLS)
    for w in range(GW):
        of_key = turned[:, w : w + 1]
        region = code_ref[0, w : w + 1, :]
        region = jnp.where(region < 0.0, region + 16.0, region)
        equal = jnp.broadcast_to(of_key[0:KP], (KP, LANES)) == jnp.broadcast_to(region, (KP, LANES))
        mask_ref[w] = jnp.where(equal | same, 0.0, NEG)
        vsc[CELLS * w : CELLS * w + 104, :] = jnp.broadcast_to(jnp.where(of_key[0:104] >= 0.0, 1.0, 0.0), (104, LANES))
    vld_ref[...] = vsc[0:GR, :]
    hp = h1p[...]
    q_ref[...] = (nn(hp, w_ref[:, 0:D]) + rowv_ref[2:3, :]).astype(bf16)
    kn[...] = nn(hp, w_ref[:, D : 2 * D]).astype(bf16)
    v_ref[...] = (nn(hp, w_ref[:, 2 * D : 3 * D]) + rowv_ref[3:4, :]).astype(bf16)
    for src, dst in ((q_ref, qT), (kn, kT_ref), (v_ref, vT)):
        for w in range(GW):
            for a in range(D // LANES):
                rows, cols = slice(LANES * w, LANES * w + LANES), slice(LANES * a, LANES * a + LANES)
                dst[cols, rows] = src[rows, cols].T
    factor = HD**-0.5 * LOG2E

    def window(w, carry):
        start = pl.multiple_of(w * LANES, LANES)
        at = pl.ds(start, LANES)
        allowed = mask_ref[w]
        for g in range(4):
            cols = slice(LANES * g, LANES * g + LANES)
            s = nn(by_head(kn[pl.ds(start, KP), cols]), qT[cols, at])
            ps = []
            for q in range(4):
                h = 4 * g + q
                t = s[KP * q : KP * q + KP] * factor + bias_ref[h] + allowed
                e = jnp.exp2(t - jnp.max(t, axis=0, keepdims=True))
                p = (e * (1.0 / jnp.sum(e, axis=0, keepdims=True))).astype(bf16)
                pT_ref[w, h] = p
                ps.append(p)
            o = [nn(vT[LANES * g + HD * q : LANES * g + HD * q + HD, at][:, 0:KP], ps[q]) for q in range(4)]
            oT_ref[cols, at] = jnp.concatenate(o, axis=0).astype(bf16)
        return carry

    lax.fori_loop(0, GW, window, 0, unroll=4)
    for w in range(GW):
        for a in range(D // LANES):
            osc[CELLS * w : CELLS * w + 104, LANES * a : LANES * a + LANES] = (
                oT_ref[LANES * a : LANES * a + LANES, LANES * w : LANES * w + LANES].T[0:112].astype(f32)[0:104]
            )
    o_ref[...] = osc[0:GR, :].astype(bf16)


def any_specs(n):
    return [pl.BlockSpec(memory_space=pl.ANY)] * n


SMEM = pl.BlockSpec(memory_space=pltpu.SMEM)


def attn_fwd(me, x, codes, bias, plan, pieces, rpd, per, count):
    n = x.shape[0] // GR
    copies = sum(1 if r is None else 2 * len(r) for r in plan)
    rb = pl.BlockSpec((GR, D), lambda i: (i, 0))
    tb = pl.BlockSpec((D, GL), lambda i: (0, i))
    pb = pl.BlockSpec((GL, D), lambda i: (i, 0))
    return pl.pallas_call(
        functools.partial(attn_fwd_body, plan=plan, rpd=rpd, per=per),
        grid=(n,),
        in_specs=[SMEM, rb, pl.BlockSpec((1, 2 * GW, LANES), lambda i: (i, 0, 0)), whole((HEADS, KP, LANES))]
        + any_specs(len(pieces)),
        out_specs=[
            tb,
            rb,
            pb,
            tb,
            pb,
            pl.BlockSpec((GW, HEADS, KP, LANES), lambda i: (i, 0, 0, 0)),
            pl.BlockSpec((D + 16, GL), lambda i: (0, i)),
            pl.BlockSpec((GR, LANES), lambda i: (i, 0)),
            whole((D, 3 * D)),
            whole((16, D)),
        ],
        out_shape=[
            sds((D, n * GL), bf16),
            sds((n * GR, D), bf16),
            sds((n * GL, D), bf16),
            sds((D, n * GL), bf16),
            sds((n * GL, D), bf16),
            sds((n * GW, HEADS, KP, LANES), bf16),
            sds((D + 16, n * GL), bf16),
            sds((n * GR, LANES), f32),
            sds((D, 3 * D), bf16),
            sds((16, D), f32),
        ],
        scratch_shapes=[
            pltpu.VMEM((GR + 8, D), f32),
            pltpu.VMEM((GL, D), bf16),
            pltpu.VMEM((D, GL), bf16),
            pltpu.VMEM((GL, D), bf16),
            pltpu.VMEM((D, GL), bf16),
            pltpu.VMEM((GR + 8, D), f32),
            pltpu.VMEM((GR + 8, LANES), f32),
            pltpu.VMEM((GW, KP, LANES), f32),
            pltpu.VMEM((count, max(rpd, 16), LANES), bf16),
            pltpu.SemaphoreType.DMA((copies,)),
        ],
        compiler_params=params(60),
        cost_estimate=pl.CostEstimate(flops=10**7, bytes_accessed=10**5, transcendentals=0),
        name="attn_fwd",
    )(me, x, codes, bias, *pieces)


def mlp_body(me_ref, vld_ref, rowv_ref, x_any, o_any, g_any, *refs, plan, rows, owners, rpd, groups):
    pieces = refs[: len(plan)]
    refs = refs[len(plan) :]
    res_any, dmid_any, p_any, first_any, second_any, third_ref, vec_ref, dbf1_ref, st_ref = refs[:9]
    xb, ob, gp, gT, h2, h2T, mid, dh2, es, dus, u4, vv, pp, res, pk, sem, sem_x, sem_o, sem_p, sem_g, sem_du, sem_dv, sem_dp, sem_r, sem_m = refs[9:]
    j = pl.program_id(0)
    last = FF // 512 - 1
    padded = h2.shape[0]
    blocks = rows // GR
    me = me_ref[0]
    proj_bias = rowv_ref[4:5, :]
    gain = rowv_ref[5:6, :]
    shift = rowv_ref[6:7, :]

    def weights():
        first, later = [], []
        count = 0
        for ref, rels in zip(pieces, plan):
            if rels is None:
                dst = (pp, u4, vv)[count]
                (first if count == 0 else later).append(pltpu.make_async_copy(ref, dst, sem.at[count]))
                count += 1
                continue
            for t, r in enumerate(rels):
                at = pl.ds(pl.multiple_of((r ^ me) * rpd, rpd), rpd)
                first.append(pltpu.make_async_copy(ref.at[t, 0], pp.at[at, :], sem.at[count]))
                later.append(pltpu.make_async_copy(ref.at[t, pl.ds(1, 4)], u4.at[:, at, :], sem.at[count + 1]))
                to = vv.at[pl.ds(pl.multiple_of((r ^ me) * 4, 4), 4)]
                later.append(pltpu.make_async_copy(ref.at[t, pl.ds(5, 4)], to, sem.at[count + 2]))
                count += 3
        return first, later

    def rows_of(k):
        return pl.ds(k * GR, GR)

    def grads_out(j):
        if not owners:
            cols = pl.ds(pl.multiple_of(j * 512, 512), 512)
            return [
                pltpu.make_async_copy(pk.at[0], first_any.at[:, cols], sem_du.at[j, 0]),
                pltpu.make_async_copy(pk.at[1], second_any.at[cols, :], sem_du.at[j, 1]),
            ]
        at = pl.ds(pl.multiple_of(j * rpd, rpd), rpd)
        low = pl.ds(4 * rpd, 4 * rpd)
        out = []
        for c, to in enumerate((first_any, second_any)):
            out.append(pltpu.make_async_copy(pk.at[c, :, at, :], to.at[:, at, :], sem_du.at[j, c]))
            for m in range(256 // (4 * rpd)):
                pos = place_of((j * (256 // (4 * rpd)) + m) ^ (me >> 1), [tuple(b - 1 for b in g) for g in groups[1:]])
                n = 2 * m + c
                out.append(pltpu.make_async_copy(pk.at[c, pos, low, :], to.at[pos, low, :], sem_dv.at[j, n]))
        return out

    @pl.when(j == 0)
    def _():
        first, later = weights()
        ins = []
        for c in first:
            c.start()
        for k in range(blocks):
            ins.append(pltpu.make_async_copy(x_any.at[rows_of(k)], xb.at[rows_of(k)], sem_x.at[k]))
            ins.append(pltpu.make_async_copy(o_any.at[rows_of(k)], ob.at[rows_of(k)], sem_o.at[k]))
        load_g = pltpu.make_async_copy(g_any, gp.at[pl.ds(0, rows)], sem_g.at[0])
        for c in ins + [load_g] + later:
            c.start()
        h2[rows:padded, :] = jnp.zeros((padded - rows, D), bf16)
        gp[rows:padded, :] = jnp.zeros((padded - rows, D), bf16)
        dus[rows:padded, :] = jnp.zeros((padded - rows, 512), bf16)
        for q in range(FF // 512):
            es[q, rows:padded, :] = jnp.zeros((padded - rows, 512), bf16)
        dh2[...] = jnp.zeros_like(dh2)
        for c in first:
            c.wait()
        store_p = pltpu.make_async_copy(pp, p_any, sem_p.at[0])
        store_p.start()
        squares = jnp.zeros((1, D), f32)
        for k in range(blocks):
            at = slice(k * GR, k * GR + GR)
            ins[2 * k].wait()
            ins[2 * k + 1].wait()
            a = nn(ob[at, :], pp[...]) + proj_bias
            squares = squares + jnp.sum(a * a * vld_ref[at, 0:1], axis=0, keepdims=True)
            m = xb[at, :].astype(f32) + a
            mid[at, :] = m
            c = m - jnp.mean(m, axis=-1, keepdims=True)
            var = jnp.mean(c * c, axis=-1, keepdims=True)
            h2[at, :] = (c * lax.rsqrt(var + 1e-5) * gain + shift).astype(bf16)
        st_ref[...] = jnp.zeros_like(st_ref)
        st_ref[1:2, :] = squares
        load_g.wait()

        def turn(k, carry):
            at = pl.ds(pl.multiple_of(k * LANES, LANES), LANES)
            for a in range(D // LANES):
                cols = slice(LANES * a, LANES * a + LANES)
                h2T[cols, at] = h2[at, cols].T
                gT[cols, at] = gp[at, cols].T
            return carry

        lax.fori_loop(0, padded // LANES, turn, 0, unroll=True)
        for c in later:
            c.wait()
        store_p.wait()

    up = u4[j]
    down = vv[pl.ds(pl.multiple_of(32 * j, 32), 32)].reshape(512, D)
    up_bias = rowv_ref[pl.ds(8 + j, 1), :]

    def products(k):
        at = slice(k * GR, k * GR + GR)
        return nn(h2[at, :], up) + up_bias, nt(gp[at, :], down)

    up_sum = jnp.zeros((1, 512), f32)
    ahead = products(0)
    for k in range(blocks):
        u, de = ahead
        if k + 1 < blocks:
            ahead = products(k + 1)
        at = slice(k * GR, k * GR + GR)
        cdf = 0.5 * lax.erf(u * RT2) + 0.5
        es[j, at, :] = (u * cdf).astype(bf16)
        du = de * (cdf + u * (PHI * jnp.exp2(u * u * (-0.5 * LOG2E))))
        dus[at, :] = du.astype(bf16)
        up_sum = up_sum + jnp.sum(du, axis=0, keepdims=True)
        dh2[at, :] += nt(dus[at, :], up)
    dbf1_ref[pl.ds(j, 1), :] = up_sum
    dU = nn(h2T[...], dus[...]).astype(bf16)
    dV = nn(gT[...], es[j]).astype(bf16).T
    if owners:
        at = pl.ds(pl.multiple_of(j * rpd, rpd), rpd)
        for k in range(owners):
            pk[(k ^ me) & 1, place_of(k ^ me, groups[1:]), at, :] = dU[rpd * k : rpd * k + rpd]
        per = 512 // (4 * rpd)
        for k in range(per):
            rel = (j * per + k) ^ me
            pk[rel & 1, place_of(rel, groups[1:]), 4 * rpd : 8 * rpd, :] = dV[4 * rpd * k : 4 * rpd * k + 4 * rpd]
        for c in grads_out(j):
            c.start()
    else:
        pk[0] = dU
        pk[1] = dV
        for c in grads_out(j):
            c.start()
        for c in grads_out(j):
            c.wait()

    @pl.when(j == last)
    def _():
        zero = jnp.zeros((1, D), f32)
        sums = [zero] * 4
        stats = [zero] * 5
        outs = []
        proj = jnp.zeros((D, D), f32)
        for k in range(blocks):
            at = slice(k * GR, k * GR + GR)
            m = mid[at, :]
            c = m - jnp.mean(m, axis=-1, keepdims=True)
            rs = lax.rsqrt(jnp.mean(c * c, axis=-1, keepdims=True) + 1e-5)
            xh = c * rs
            d = dh2[at, :]
            dx = d * gain
            dxx = d * xh
            m1 = jnp.mean(dx, axis=-1, keepdims=True)
            m2 = jnp.mean(dxx * gain, axis=-1, keepdims=True)
            grad = gp[at, :].astype(f32)
            dm = grad + (dx - m1 - xh * m2) * rs
            dh2[at, :] = dm
            outs.append(pltpu.make_async_copy(dh2.at[rows_of(k)], dmid_any.at[rows_of(k)], sem_m.at[k]))
            outs[-1].start()
            da = dm.astype(bf16)
            proj = proj + tn(ob[at, :], da)
            terms = (da.astype(f32), dxx, d, grad)
            sums = [a + jnp.sum(t, axis=0, keepdims=True) for a, t in zip(sums, terms)]
            f = rowv_ref[7:8, :]
            for b in range(4):
                f = f + nn(es[b, at, :], vv[32 * b : 32 * b + 32].reshape(512, D))
            out = m + f
            res[at, :] = out.astype(bf16)
            outs.append(pltpu.make_async_copy(res.at[rows_of(k)], res_any.at[rows_of(k)], sem_r.at[k]))
            outs[-1].start()
            vl = vld_ref[at, 0:1]
            x = xb[at, :].astype(f32)
            terms = (x * x * vl, m * m * vl, f * f * vl, out * out * vl, jnp.broadcast_to(vl, (GR, D)))
            stats = [a + jnp.sum(t, axis=0, keepdims=True) for a, t in zip(stats, terms)]
        for q in range(4):
            vec_ref[q : q + 1, :] = sums[q]
        vec_ref[4:8, :] = jnp.zeros((4, D), f32)
        dbf1_ref[4:8, :] = jnp.zeros((4, D), f32)
        for q, t in zip((0, 2, 3, 4, 5), stats):
            st_ref[q : q + 1, :] = t
        if owners:
            proj = proj.astype(bf16)
            at = pl.ds(8 * rpd, rpd)
            for k in range(owners):
                pk[(k ^ me) & 1, place_of(k ^ me, groups[1:]), at, :] = proj[rpd * k : rpd * k + rpd]
            third_ref[...] = jnp.zeros_like(third_ref)
            for c, to in enumerate((first_any, second_any)):
                outs.append(pltpu.make_async_copy(pk.at[c, :, at, :], to.at[:, at, :], sem_dp.at[c]))
                outs[-1].start()
            for step in range(last + 1):
                outs += grads_out(step)
        else:
            third_ref[...] = proj
        for c in outs:
            c.wait()


def mlp(me, x, o, g, vld, rowv, plan, pieces, rpd, owners, count, groups):
    rows = x.shape[0]
    blocks = rows // GR
    steps = FF // 512
    padded = -(-rows // LANES) * LANES
    copies = sum(1 if r is None else 3 * len(r) for r in plan)
    if owners:
        grad_shapes = [sds((count // 2, 9 * rpd, 512), bf16)] * 2 + [sds((8, LANES), f32)]
        pk = (2, count // 2, 9 * rpd, 512)
    else:
        grad_shapes = [sds((D, FF), bf16), sds((FF, D), bf16), sds((D, D), f32)]
        pk = (2, 512, 512)
    dma = pltpu.SemaphoreType.DMA
    return pl.pallas_call(
        functools.partial(mlp_body, plan=plan, rows=rows, owners=count if owners else 0, rpd=rpd, groups=groups),
        grid=(steps,),
        in_specs=[SMEM, whole((rows, LANES)), whole((16, D))] + any_specs(3 + len(pieces)),
        out_specs=any_specs(5) + [whole(grad_shapes[2].shape)] + [whole((8, D))] * 3,
        out_shape=[sds((rows, D), bf16), sds((rows, D), f32), sds((D, D), bf16)] + grad_shapes + [sds((8, D), f32)] * 3,
        scratch_shapes=[
            pltpu.VMEM((rows, D), bf16),
            pltpu.VMEM((rows, D), bf16),
            pltpu.VMEM((padded, D), bf16),
            pltpu.VMEM((D, padded), bf16),
            pltpu.VMEM((padded, D), bf16),
            pltpu.VMEM((D, padded), bf16),
            pltpu.VMEM((rows, D), f32),
            pltpu.VMEM((rows, D), f32),
            pltpu.VMEM((steps, padded, 512), bf16),
            pltpu.VMEM((padded, 512), bf16),
            pltpu.VMEM((steps, D, 512), bf16),
            pltpu.VMEM((FF // 16, 16, D), bf16),
            pltpu.VMEM((D, D), bf16),
            pltpu.VMEM((rows, D), bf16),
            pltpu.VMEM(pk, bf16),
            dma((copies,)),
            dma((blocks,)),
            dma((blocks,)),
            dma((1,)),
            dma((1,)),
            dma((steps, 2)),
            dma((steps, max(1, 512 // (4 * rpd)))),
            dma((2,)),
            dma((blocks,)),
            dma((blocks,)),
        ],
        compiler_params=params(52),
        cost_estimate=pl.CostEstimate(flops=10**7, bytes_accessed=10**5, transcendentals=0),
        name="mlp",
    )(me, vld, rowv, x, o, g, *pieces)


def attn_bwd_body(me_ref, dmid_ref, p_ref, oT_ref, q_ref, kT_ref, v_ref, pT_ref, xT_ref, w_any, rowv_ref, *refs, owners, rpd, groups):
    dm_ref, acc_ref, vec_ref = refs[:3]
    grads = refs[3:-7]
    xs, dap, don, doT, dw, w_ref, sem_w = refs[-7:]
    i = pl.program_id(0)
    load_w = pltpu.make_async_copy(w_any, w_ref, sem_w.at[0])

    @pl.when(i == 0)
    def _():
        load_w.start()
        acc_ref[...] = jnp.zeros_like(acc_ref)
        dw[...] = jnp.zeros_like(dw)

    xs[0:GR, :] = dmid_ref[...]
    for w in range(GW):
        dap[LANES * w : LANES * w + LANES, :] = pad_window(xs[CELLS * w : CELLS * w + 104, :])
        dm_ref[LANES * w + KP : LANES * w + LANES, :] = jnp.zeros((LANES - KP, 3 * D), bf16)
    da = dap[...]
    don[...] = nt(da, p_ref[...]).astype(bf16)
    for w in range(GW):
        for a in range(D // LANES):
            rows, cols = slice(LANES * w, LANES * w + LANES), slice(LANES * a, LANES * a + LANES)
            doT[cols, rows] = don[rows, cols].T
    factor = HD**-0.5

    def window(w, carry):
        start = pl.multiple_of(w * LANES, LANES)
        at = pl.ds(start, LANES)
        keys = pl.ds(start, KP)
        for g in range(4):
            c0 = LANES * g
            cols = slice(c0, c0 + LANES)
            dp = nn(by_head(v_ref[keys, cols]), doT[cols, at])
            dss = []
            for q in range(4):
                h = 4 * g + q
                head = slice(HD * h, HD * h + HD)
                delta = jnp.sum(doT[head, at].astype(f32) * oT_ref[head, at].astype(f32), axis=0, keepdims=True)
                ds = pT_ref[w, h].astype(f32) * (dp[KP * q : KP * q + KP] - delta)
                acc_ref[h] += ds
                dss.append(ds.astype(bf16))
            dq = [nn(kT_ref[c0 + HD * q : c0 + HD * q + HD, at][:, 0:KP], dss[q]) for q in range(4)]
            dm_ref[at, cols] = (jnp.concatenate(dq, axis=0) * factor).astype(bf16).T
            dk = nn(jnp.concatenate(dss, axis=1), by_head(q_ref[at, cols])) * factor
            dm_ref[keys, D + c0 : D + c0 + LANES] = dk.astype(bf16)
            dv = nn(jnp.concatenate([pT_ref[w, 4 * g + q] for q in range(4)], axis=1), by_head(don[at, cols]))
            dm_ref[keys, 2 * D + c0 : 2 * D + c0 + LANES] = dv.astype(bf16)
        return carry

    lax.fori_loop(0, GW, window, 0, unroll=4)
    dw[...] += nn(xT_ref[...], dm_ref[...])

    @pl.when(i == pl.num_programs(0) - 1)
    def _():
        load_w.wait()
        s = dw[D : D + 1, :]
        vec_ref[...] = jnp.zeros_like(vec_ref)
        vec_ref[0:1, :] = s
        for a in range(D // LANES):
            rows = slice(LANES * a, LANES * a + LANES)
            col = rowv_ref[0:8, rows].T
            x = dw[rows, :]
            wt = w_ref[rows, :].astype(f32)
            by_gain = jnp.broadcast_to(jnp.sum(wt * x, axis=1, keepdims=True), (LANES, LANES)).T
            by_shift = jnp.broadcast_to(jnp.sum(wt * s, axis=1, keepdims=True), (LANES, LANES)).T
            vec_ref[1:2, rows] = by_gain[0:1]
            vec_ref[2:3, rows] = by_shift[0:1]
            dw[rows, :] = col[:, 0:1] * x + col[:, 1:2] * s
        if owners:
            me = me_ref[0]
            for k in range(owners):
                rel = k ^ me
                pos = place_of(rel, groups[1:])
                mine = slice(rpd * k, rpd * k + rpd)

                def store(to, mine=mine, pos=pos):
                    for q in range(3):
                        to[pos, rpd * q : rpd * q + rpd, :] = dw[mine, D * q : D * q + D].astype(bf16)

                pl.when(rel & 1 == 0)(functools.partial(store, grads[0]))
                pl.when(rel & 1 == 1)(functools.partial(store, grads[1]))
        else:
            grads[0][...] = dw[0:D, :].astype(bf16)


def attn_bwd(me, dmid, p, oT, q, kT, v, pT, xT, w, rowv, rpd, owners, count, groups):
    n = q.shape[0] // GL

    def tb(r):
        return pl.BlockSpec((r, GL), lambda i: (0, i))

    pb = pl.BlockSpec((GL, D), lambda i: (i, 0))
    if owners:
        grad_shapes = [sds((count // 2, 3 * rpd, D), bf16)] * 2
    else:
        grad_shapes = [sds((D, 3 * D), bf16)]
    return pl.pallas_call(
        functools.partial(attn_bwd_body, owners=count if owners else 0, rpd=rpd, groups=groups),
        grid=(n,),
        in_specs=[SMEM, pl.BlockSpec((GR, D), lambda i: (i, 0)), whole((D, D)), tb(D), pb, tb(D), pb, pl.BlockSpec((GW, HEADS, KP, LANES), lambda i: (i, 0, 0, 0)), tb(D + 16), pl.BlockSpec(memory_space=pl.ANY), whole((16, D))],
        out_specs=[pl.BlockSpec((GL, 3 * D), lambda i: (i, 0)), whole((HEADS, KP, LANES)), whole((8, 3 * D))] + [whole(s.shape) for s in grad_shapes],
        out_shape=[sds((n * GL, 3 * D), bf16), sds((HEADS, KP, LANES), f32), sds((8, 3 * D), f32)] + grad_shapes,
        scratch_shapes=[
            pltpu.VMEM((GR + 8, D), f32),
            pltpu.VMEM((GL, D), bf16),
            pltpu.VMEM((GL, D), bf16),
            pltpu.VMEM((D, GL), bf16),
            pltpu.VMEM((D + 16, 3 * D), f32),
            pltpu.VMEM((D, 3 * D), bf16),
            pltpu.SemaphoreType.DMA((1,)),
        ],
        compiler_params=params(60),
        cost_estimate=pl.CostEstimate(flops=10**7, bytes_accessed=10**5, transcendentals=0),
        name="attn_bwd",
    )(me, dmid, p, oT, q, kT, v, pT, xT, w, rowv)


def grad_in_body(dm_ref, w_ref, x_ref, dmid_ref, rowv_ref, tg_ref, dsc):
    dh = nt(dm_ref[...], w_ref[...])
    for w in range(GW):
        dsc[CELLS * w : CELLS * w + 104, :] = dh[LANES * w : LANES * w + 104]
    x = x_ref[...].astype(f32)
    c = x - jnp.mean(x, axis=-1, keepdims=True)
    rs = lax.rsqrt(jnp.mean(c * c, axis=-1, keepdims=True) + 1e-5)
    xh = c * rs
    dx = dsc[0:GR, :] * rowv_ref[0:1, :]
    m1 = jnp.mean(dx, axis=-1, keepdims=True)
    m2 = jnp.mean(dx * xh, axis=-1, keepdims=True)
    tg_ref[...] = dmid_ref[...] + (dx - m1 - xh * m2) * rs


def grad_in(dm, w, x, dmid, rowv):
    n = x.shape[0] // GR
    rb = pl.BlockSpec((GR, D), lambda i: (i, 0))
    return pl.pallas_call(
        grad_in_body,
        grid=(n,),
        in_specs=[pl.BlockSpec((GL, 3 * D), lambda i: (i, 0)), whole((D, 3 * D)), rb, rb, whole((16, D))],
        out_specs=rb,
        out_shape=sds((n * GR, D), f32),
        scratch_shapes=[pltpu.VMEM((GR + 8, D), f32)],
        compiler_params=params(60),
        cost_estimate=pl.CostEstimate(flops=10**7, bytes_accessed=10**5, transcendentals=0),
        name="grad_in",
    )(dm, w, x, dmid, rowv)


SMALL = 24
SENT = 32


def to_send(small):
    lane = lax.broadcasted_iota(jnp.int32, small.shape, 1)
    lane = jnp.where(lax.broadcasted_iota(jnp.int32, small.shape, 0) >= 8, lane, -1)
    small = jnp.where(lane == RELN, small + pltpu.roll(small, D - 1, 1), small)
    hi = small.astype(bf16).astype(f32)
    small = jnp.where(lane == RELN + 1, pltpu.roll(small - hi, 1, 1), hi)
    return jnp.concatenate([small, jnp.zeros((SENT - SMALL, D), f32)], axis=0).astype(bf16)


def sent_sums(terms):
    got = [t.astype(f32)[0:SMALL] for t in terms]
    while len(got) > 1:
        got = [got[k] + got[k + 1] for k in range(0, len(got), 2)]
    return got[0]


def fold_body(*refs, first, terms, parts):
    ins, outs = refs[: 2 * terms if first else terms + 1], refs[2 * terms if first else terms + 1 :]
    nb, rows = ins[0].shape[0], ins[0].shape[1]
    n = nb // (parts + 1)
    if first:
        small = ins[2][...] + ins[3][...]
    else:
        small = sent_sums([ins[1][...]] + [r[nb * rows :, :] for r in ins[2:]])
    for p in range(parts + 1):
        at = slice(p * n, p * n + n)
        total = ins[0][at].astype(f32)
        if first:
            total = total + ins[1][at].astype(f32)
        else:
            for r in ins[2:]:
                total = total + r[p * n * rows : (p + 1) * n * rows, :].astype(f32).reshape(n, rows, D)
        if p == 0:
            outs[0][...] = total
            outs[1][...] = to_send(small)
        else:
            outs[p + 1][0 : n * rows, :] = total.reshape(n * rows, D).astype(bf16)
            outs[p + 1][n * rows :, :] = to_send(small)


def fold(arrays, parts, first=False):
    terms = 2 if first else len(arrays) - 1
    nb, rows = arrays[0].shape[:2]
    n = nb // (parts + 1)
    return pl.pallas_call(
        functools.partial(fold_body, first=first, terms=terms, parts=parts),
        out_shape=[sds((n, rows, D), f32), sds((SENT, D), bf16)] + [sds((n * rows + SENT, D), bf16)] * parts,
        compiler_params=params(16),
        cost_estimate=pl.CostEstimate(flops=10**6, bytes_accessed=10**5, transcendentals=0),
        name="fold",
    )(*arrays)


def add_body(*refs, terms):
    ins, outs = refs[:terms], refs[terms:]
    n = outs[0].shape[0]
    for p, out in enumerate(outs):
        at = slice(p * n, p * n + n)
        total = ins[0][at].astype(f32)
        for r in ins[1:]:
            total = total + r[at].astype(f32)
        out[...] = total.astype(out.dtype)


def add_split(terms, group):
    parts = len(masks_of(group))
    shape = (terms[0].shape[0] // (parts + 1),) + terms[0].shape[1:]
    out = pl.pallas_call(
        functools.partial(add_body, terms=len(terms)),
        out_shape=[sds(shape, f32)] + [sds(shape, bf16)] * parts,
        compiler_params=params(24),
        cost_estimate=pl.CostEstimate(flops=10**6, bytes_accessed=10**5, transcendentals=0),
        name="add_split",
    )(*terms)
    return out[0], out[1:]


def spread(o_ref, block, width, at):
    each = width // LANES
    for b in range(block.shape[1] // LANES):
        o_ref[pl.ds(at // LANES + b, block.shape[0], stride=each), :] = block[:, LANES * b : LANES * b + LANES]


def attn_last_body(me_ref, own_ref, kept_ref, *refs, rpd, per):
    got_refs, (qkv_ref, vec_ref, table_ref, stats_ref, lines) = refs[:-5], refs[-5:]
    rows = own_ref.shape[1]
    total = own_ref[0]
    for r in got_refs:
        total = total + r[0:rows, :].astype(f32)
    for q in range(3):
        spread(qkv_ref, total[rpd * q : rpd * q + rpd], 3 * D, D * q)
    small = sent_sums([kept_ref[...]] + [r[rows:, :] for r in got_refs])
    for k in range(8):
        for a in range(4):
            lines[4 * k + a : 4 * k + a + 1, :] = small[k : k + 1, LANES * a : LANES * a + LANES]
    lines[32:48, :] = small[8:24, RP:D]
    if per % 64:
        vec_ref[...] = lines[...]
    else:
        low = lax.broadcasted_iota(jnp.int32, (1, LANES), 1) < 64
        for p in range(0, per // 64, 2):
            halves = []
            for k in range(2):
                c = me_ref[0] * (per // 64) + min(p + k, per // 64 - 1)
                line = lines[pl.ds(c >> 1, 1), :]
                halves.append(jnp.where(c & 1 == k, line, pltpu.roll(line, 64, 1)))
            vec_ref[p // 2 : p // 2 + 1, :] = jnp.where(low, halves[0], halves[1])
    table_ref[...] = small[8:24, 0:RELN]
    turned = small[8:24, RP - LANES : RP].T
    at = RELN - (RP - LANES)
    line = turned[at : at + 1] + turned[at + 1 : at + 2]
    stats_ref[...] = jnp.sqrt(line / line[:, 5:6] + 1e-06)


def attn_last(me, arrays, rpd, per):
    lines = -(-per // LANES) if per % 64 == 0 else 48
    return pl.pallas_call(
        functools.partial(attn_last_body, rpd=rpd, per=per),
        in_specs=[SMEM] + [pl.BlockSpec(memory_space=pltpu.VMEM)] * len(arrays),
        out_shape=[sds((12 * rpd, LANES), f32), sds((lines, LANES), f32), sds((HEADS, RELN), f32), sds((1, HEADS), f32)],
        scratch_shapes=[pltpu.VMEM((48, LANES), f32)],
        compiler_params=params(16),
        cost_estimate=pl.CostEstimate(flops=10**6, bytes_accessed=10**5, transcendentals=0),
        name="attn_last",
    )(me, *arrays)


def mlp_last_body(own_ref, *refs, rpd):
    total = own_ref[0]
    for r in refs[:-3]:
        total = total + r[0].astype(f32)
    for q in range(4):
        spread(refs[-3], total[rpd * q : rpd * q + rpd], FF, 512 * q)
    spread(refs[-2], total[4 * rpd : 8 * rpd], D, 0)
    spread(refs[-1], total[8 * rpd :], D, 0)


def mlp_last(arrays, rpd):
    return pl.pallas_call(
        functools.partial(mlp_last_body, rpd=rpd),
        out_shape=[sds((16 * rpd, LANES), f32)] * 2 + [sds((4 * rpd, LANES), f32)],
        compiler_params=params(16),
        cost_estimate=pl.CostEstimate(flops=10**6, bytes_accessed=10**5, transcendentals=0),
        name="mlp_last",
    )(*arrays)


def place_hits(shape, axis, rev=0):
    c = lax.broadcasted_iota(jnp.int32, shape, 1 - axis)
    code = jnp.where(c < CELLS, (2 * WSIDE - 1) * (c // WSIDE) + c % WSIDE, -1000)
    if rev:
        code = rev - code
    return jnp.where(code == lax.broadcasted_iota(jnp.int32, shape, axis), 1.0, 0.0).astype(bf16)


def rel_bias_body(t_ref, o_ref):
    keys = place_hits((KP, 192), 1)
    queries = place_hits((256, LANES), 0)

    def head(h, carry):
        row = pltpu.roll(jnp.broadcast_to(t_ref[pl.ds(h, 1), :], (8, RP)), 0, 1, stride=1, stride_axis=0)
        t = jnp.concatenate([pltpu.roll(row, (8 * k - 180) % RP, 1)[:, 0:256] for k in range(24)], axis=0)
        hi = t.astype(bf16)
        lo = (t - hi.astype(f32)).astype(bf16)
        b = nn(jnp.concatenate([hi, lo], axis=0), queries).astype(bf16)
        b = nn(keys, jnp.concatenate([b[0:192], b[192:384]], axis=1))
        o_ref[h] = b[:, 0:LANES] + b[:, LANES : 2 * LANES]
        return carry

    lax.fori_loop(0, HEADS, head, 0, unroll=8)


def rel_bias(table):
    return pl.pallas_call(
        rel_bias_body,
        out_shape=sds((HEADS, KP, LANES), f32),
        compiler_params=params(16),
        cost_estimate=pl.CostEstimate(flops=2 * 10**10, bytes_accessed=10**6, transcendentals=0),
        name="rel_bias",
    )(table)


def rel_grad_body(a_ref, one_ref, two_ref, up_ref, squares_ref, o_ref):
    keys = place_hits((192, KP), 0, 191)
    queries = place_hits((LANES, 256), 1)
    zero = jnp.zeros((8, RP - 256), f32)
    o_ref[0:2, :] = one_ref[1:3, 0:D]
    o_ref[2:3, :] = one_ref[0:1, 0:D]
    o_ref[3:4, :] = one_ref[0:1, 2 * D : 3 * D]
    o_ref[4:8, :] = two_ref[0:4, :]

    def head(h, carry):
        a = a_ref[h]
        hi = a.astype(bf16)
        lo = (a - hi.astype(f32)).astype(bf16)
        b = nn(keys, jnp.concatenate([hi, lo], axis=1)).astype(bf16)
        b = nn(jnp.concatenate([b[:, 0:LANES], b[:, LANES : 2 * LANES]], axis=0), queries)
        b = b[0:192] + b[192:384]
        t = jnp.zeros((8, RP), f32)
        for k in range(24):
            t = t + pltpu.roll(jnp.concatenate([b[8 * k : 8 * k + 8], zero], axis=1), (8 * k - 11) % RP, 1)
        t = pltpu.roll(t, 0, 1, stride=1, stride_axis=0)
        o_ref[pl.ds(8 + h, 1), 0:RP] = jnp.sum(t, axis=0, keepdims=True)
        return carry

    lax.fori_loop(0, HEADS, head, 0, unroll=16)
    for k in range(4):
        for a in range(4):
            o_ref[8 + 4 * k + a : 9 + 4 * k + a, RP:D] = up_ref[k : k + 1, LANES * a : LANES * a + LANES]
    for k in range(6):
        o_ref[8 + k : 9 + k, RELN : RELN + 1] = jnp.sum(squares_ref[k : k + 1, :], axis=1, keepdims=True)
        o_ref[8 + k : 9 + k, RELN + 1 : RELN + 2] = jnp.zeros((1, 1), f32)


def rel_grad(acc, one, two, up, squares):
    return pl.pallas_call(
        rel_grad_body,
        out_shape=sds((SMALL, D), f32),
        compiler_params=params(16),
        cost_estimate=pl.CostEstimate(flops=10**7, bytes_accessed=10**5, transcendentals=0),
        name="rel_grad",
    )(acc, one, two, up, squares)


def shards(tokens, cotangent, regions, validity, qkv_weight, proj_weight, fc1_weight, fc2_weight, vectors, rel_table, *, count, inner):
    rows = tokens.shape[0]
    groups = bit_groups(count)
    single = groups[:2] + [(b,) for g in groups[2:] for b in g]
    rpd = D // count
    direct = rpd % 16 == 0
    me = lax.axis_index("dp") * inner + lax.axis_index("shard")
    me_s = me.astype(jnp.int32).reshape(1)

    per = vectors.shape[0]
    if direct:
        own = jnp.pad(vectors, (0, rpd * LANES - per)).reshape(rpd, LANES)
        own = jnp.concatenate([qkv_weight.reshape(rpd, 3 * D), own], axis=1)
    else:
        own = jnp.concatenate([qkv_weight, vectors]).reshape(1, -1)
    rels, attn_up = gather_upper(own, groups, count)
    up_rows = fc1_weight.reshape(rpd, FF)
    packed = jnp.concatenate(
        [proj_weight.reshape(rpd, D)] + [up_rows[:, 512 * q : 512 * q + 512] for q in range(4)] + [fc2_weight.reshape(4 * rpd, D)], axis=0
    )
    attn_pieces = gather_plane(rels, attn_up, groups, count)
    table_in = after(rel_table, attn_up)
    mlp_rels, mlp_up = gather_upper(packed, single, count, attn_up)

    bias = rel_bias(jnp.pad(table_in.T * LOG2E, ((0, 0), (0, RP - RELN))))
    codes = jnp.where(validity == 1, regions, regions - 16).astype(f32).reshape(-1, GW, CELLS)
    codes = jnp.pad(codes, ((0, 0), (0, 8 - GW), (0, LANES - CELLS)), constant_values=-100.0)

    attn_pieces = hold(attn_pieces, bias, codes)
    mlp_up = after(mlp_up, bias, codes, [a for _, a in attn_pieces])
    attn_pieces = gather_core(attn_pieces, count)
    mlp_pieces = gather_plane(mlp_rels, mlp_up, groups, count)
    if direct:
        attn_plan = [r for r, _ in attn_pieces]
        attn_w = [a for _, a in attn_pieces]
    else:
        attn_plan = [None] * 2
        both = natural_order(attn_pieces, me, count).reshape(count, -1)
        attn_w = [both[:, : 3 * D * rpd].reshape(D, 3 * D), jnp.pad(both[:, 3 * D * rpd :].astype(f32).reshape(12, D), ((0, 4), (0, 0)))]

    x = after(tokens, mlp_up)
    oT, o, q, kT, v, pT, xT, vld, w_full, rowv = attn_fwd(me_s, x, codes, bias, attn_plan, attn_w, rpd, per, count)

    mlp_pieces = gather_core(hold(mlp_pieces, o), count)
    if direct:
        mlp_plan = [r for r, _ in mlp_pieces]
        mlp_w = [a.reshape(-1, 9, rpd, D) for _, a in mlp_pieces]
    else:
        both = natural_order(mlp_pieces, me, count).reshape(count, 9, rpd, D)
        mlp_plan = [None] * 3
        mlp_w = [both[:, 0].reshape(D, D), both[:, 1:5].transpose(1, 0, 2, 3).reshape(4, D, 512), both[:, 5:].reshape(128, 16, D)]
    result, dmid, p_full, mlp_keep, mlp_send, dproj, vec_two, dbf1, squares = mlp(
        me_s, tokens, o, cotangent, vld, rowv, mlp_plan, mlp_w, rpd, direct, count, single
    )
    order = None
    if not direct:
        blocks = jnp.arange(count)
        order, mlp_order = (
            jnp.zeros((count,), jnp.int32).at[place_of(blocks, way)].set(blocks.astype(jnp.int32)) ^ me for way in (groups, single)
        )
        dU = mlp_keep.reshape(count, rpd, 4, 512).transpose(0, 2, 1, 3).reshape(count, 4 * rpd, 512)
        pk = [dU, mlp_send.reshape(count, 4 * rpd, D), dproj.astype(bf16).reshape(count, rpd, D)]
        pk = jnp.take(jnp.concatenate(pk, axis=1), mlp_order, axis=0)
        mlp_keep, mlp_send = pk[: count // 2], pk[count // 2 :]

    other = swap(mlp_send, 1, count)
    mlp_own, parts = add_split([mlp_keep, other], groups[1])
    mlp_got = send_parts(parts, groups[1], count)
    dmid = after(dmid, parts)
    got = attn_bwd(me_s, dmid, p_full, oT, q, kT, v, pT, xT, w_full, rowv, rpd, direct, count, groups)
    dm, score_sums, vec_one = got[:3]
    if direct:
        attn_keep, attn_send = got[3:]
    else:
        dW = got[3].reshape(count, rpd, 3, D).transpose(0, 2, 1, 3).reshape(count, 3 * rpd, D)
        pk = jnp.take(jnp.pad(dW, ((0, 0), (0, rpd), (0, 0))), order, axis=0)
        attn_keep, attn_send = pk[: count // 2], pk[count // 2 :]
    mlp_got, attn_send, score_sums, dm = lax.optimization_barrier((mlp_got, attn_send, score_sums, dm))

    other = swap(attn_send, 1, count)
    mlp_terms = [mlp_own] + mlp_got
    for g in single[2:3]:
        mlp_own, parts = add_split(mlp_terms, g)
        mlp_terms = [mlp_own] + send_parts(parts, g, count)
        score_sums = after(score_sums, parts)
    small = rel_grad(score_sums, vec_one, vec_two, dbf1, squares)
    other = after(other, small)
    levels = [len(masks_of(g)) for g in groups[1:]]
    out = fold([attn_keep, other, small, swap(small, 1, count)], levels[0], first=True)
    for k, g in enumerate(groups[1:]):
        own, kept, parts = out[0], out[1], out[2:]
        sent = send_parts(parts, g, count)
        if k == 0:
            mlp_terms = after(mlp_terms, parts)
            for up in single[3:]:
                mlp_own, parts = add_split(mlp_terms, up)
                mlp_terms = [mlp_own] + send_parts(parts, up, count)
            dm = after(dm, parts)
            grad_tokens = grad_in(dm, w_full, tokens, dmid, rowv)
            sent, mlp_terms = after((sent, mlp_terms), grad_tokens)
        if k + 1 < len(levels):
            out = fold([own, kept] + sent, levels[k + 1])
            mlp_terms = after(mlp_terms, out)
    grad_fc1, grad_fc2, grad_proj = mlp_last(mlp_terms, rpd)
    sent = after(sent, grad_fc1)
    grad_qkv, grad_vectors, grad_table, stats = attn_last(me_s, [own, kept] + sent, rpd, per)
    if per % 64 == 0:
        grad_vectors = grad_vectors.reshape(-1)[:per]
    else:
        grad_vectors = lax.dynamic_slice(grad_vectors.reshape(-1), (me * per,), (per,))
    return (
        result,
        grad_tokens,
        grad_qkv.reshape(-1),
        grad_proj.reshape(-1),
        grad_fc1.reshape(-1),
        grad_fc2.reshape(-1),
        grad_vectors,
        grad_table.T,
        stats[0, 0:5],
    )


def solution(mesh):
    flat = P(AXES)
    tall = P(AXES, None)
    in_specs = (tall, tall, flat, flat, flat, flat, flat, flat, flat, P())
    out_specs = (tall, tall, flat, flat, flat, flat, flat, P(), P())
    inner = mesh.shape["shard"]
    body = functools.partial(shards, count=mesh.shape["dp"] * inner, inner=inner)
    return jax.shard_map(body, mesh=mesh, in_specs=in_specs, out_specs=out_specs, check_vma=False)
```
